32 devices in a mesh: freq: 4 (over y, x), mx: 2 (over core), my: 4 (over z).
Axes of the slice: x: 2, y: 2, z: 4, core: 2. Of those that a mesh axis runs over, the one named last changes fastest.
Arguments:
- adjoint_rhs: float32 [4, 2, 3, 128, 1024], P('freq', None, None, 'mx', 'my'), may hold values from -4 to 6
- state: bfloat16 [4, 2, 3, 128, 1024], P('freq', None, None, 'mx', 'my'), may hold values from -1.5 to 1.5
- density: float32 [128, 1024], P('mx', 'my'), may hold values from 0.85 to 1
- stiffness: float32 [128, 1024], P('mx', 'my'), may hold values from 1.5 to 4
- mass: float32 [128, 1024], P('mx', 'my'), may hold values from 0.2 to 1
- omega: float32 [4], P('freq'), may hold values from 0.15 to 0.45
- send_rows: int32 [8, 256], P(('mx', 'my')), may hold values from 0 to 16383, as said below
- recv_rows: int32 [8, 256], P(('mx', 'my')), may hold values from 0 to 16383, as said below
- mortar_weight: float32 [8, 256], P(('mx', 'my')), may hold values from 0 to 1.5, as said below
Outputs:
- adjoint: float32 [4, 2, 3, 128, 1024], P('freq', None, None, 'mx', 'my')
- filtered_sensitivity: float32 [128, 1024], P('mx', 'my')
The draws below stay inside these ranges and needn't reach their ends.
Inputs may be any that keep to these rules, and one draw needn't show every extreme that they name: `send_rows`: a local cell of the sending device; slots past the live count of a device pair hold 0. `recv_rows`: a local cell of the receiving device; empty slots hold 0. Live slots of a pair come first, up to 32 of them. `mortar_weight`: zero exactly in empty slots, at least 0.5 in live ones; every receiving device has a source device with all 32 slots live.
All inputs are finite; a program needn't handle non-finite values.
Results may differ from the reference program's by a relative error of at most 0.0003.
Values may be sent and summed in bfloat16 or wider, within the bound.
No kernel may reach another device: no remote copies, remote signals or barrier semaphores. Data moves between devices by JAX's collectives and lax.ppermute only.
A program may use at most 64 MiB of HBM per device.

```python
import math
import jax
import jax.numpy as jnp

CX = 64
CY = 256
CAP = 32
ITERS = 20
FREQS = 4
PEERS = 8
CELLS_DEV = 16384
NX = 128
NY = 1024
N_MX = 2
N_MY = 4


def live_slots(key):
    counts = jax.random.randint(jax.random.fold_in(key, 11), (PEERS, PEERS), CAP // 2, CAP + 1)
    forced = (jnp.arange(PEERS) * 7 + 3) % PEERS
    counts = jnp.where(jnp.arange(PEERS)[None, :] == forced[:, None], CAP, counts)
    return jnp.arange(CAP)[None, None, :] < counts[:, :, None]


def draw_recv_rows(key, part):
    live = live_slots(key)
    rows = jax.random.randint(jax.random.fold_in(key, 12), (PEERS, PEERS, CAP), 0, CELLS_DEV)
    return jnp.where(live, rows, 0).astype(jnp.int32).reshape(PEERS, PEERS * CAP)


def draw_send_rows(key, part):
    live = jnp.transpose(live_slots(key), (1, 0, 2))
    rows = jax.random.randint(jax.random.fold_in(key, 13), (PEERS, PEERS, CAP), 0, CELLS_DEV)
    return jnp.where(live, rows, 0).astype(jnp.int32).reshape(PEERS, PEERS * CAP)


def draw_mortar_weight(key, part):
    live = live_slots(key)
    values = jax.random.uniform(jax.random.fold_in(key, 14), (PEERS, PEERS, CAP), jnp.float32, 0.5, 1.5)
    return jnp.where(live, values, 0.0).astype(jnp.float32).reshape(PEERS, PEERS * CAP)


def draw_adjoint_rhs(key, part):
    shape = (FREQS, 2, 3, NX, NY)
    xs = (jnp.arange(NX, dtype=jnp.float32) + 0.5) / NX
    ys = (jnp.arange(NY, dtype=jnp.float32) + 0.5) / NY
    phase_x = jax.random.uniform(jax.random.fold_in(key, 21), (FREQS, 2, 3, 1, 1), jnp.float32, 0.0, 2.0 * math.pi)
    phase_y = jax.random.uniform(jax.random.fold_in(key, 22), (FREQS, 2, 3, 1, 1), jnp.float32, 0.0, 2.0 * math.pi)
    amp = jax.random.uniform(jax.random.fold_in(key, 23), (FREQS, 2, 3, 1, 1), jnp.float32, 0.8, 1.4)
    rough = jnp.clip(jax.random.normal(jax.random.fold_in(key, 24), shape, jnp.float32), -4.0, 4.0)
    wave = jnp.sin(2.0 * math.pi * xs[:, None] + phase_x) * jnp.sin(2.0 * math.pi * ys[None, :] + phase_y)
    smooth = amp * (1.0 + 0.4 * wave)
    return (smooth + rough).astype(jnp.float32)


def block_levels(rng, shape, shards, low, top_value):
    level = 1.0
    for dim, parts in shards:
        heights = jax.random.uniform(jax.random.fold_in(jax.random.fold_in(rng, 6), dim), (parts,), jnp.float32, low / len(shards), top_value / len(shards))
        level = level * jnp.repeat(jnp.exp(heights), shape[dim] // parts).reshape((-1,) + (1,) * (len(shape) - 1 - dim))
    return level


def centred(key, dims, width, reach, pieces=(), held_as=jnp.bfloat16):
    values = width * jax.random.normal(key, dims, jnp.float32)
    if pieces:
        values = values * block_levels(key, dims, pieces, -0.22, 0.18)
    return jnp.clip(values, -reach, reach).astype(held_as)


def setup_inputs(seed: int = 0) -> dict:
    keys = jax.random.split(jax.random.key(seed), 10)
    adjoint_rhs = draw_adjoint_rhs(jax.random.fold_in(keys[9], 71), 0)
    state = centred(keys[1], (FREQS, 2, 3, NX, NY), 0.1, 1.5, ((0, 4), (3, 2), (4, 4)))
    density = jnp.clip(jnp.exp(math.log(1.0) - 0.1625189 * jax.random.uniform(keys[2], (NX, NY), jnp.float32) ** block_levels(keys[2], (NX, NY), ((0, 2), (1, 4)), -0.2, 0.2)), 0.85, 1.0)
    stiffness = jnp.clip(jnp.exp(math.log(4.0) - 0.98082925 * jax.random.uniform(keys[3], (NX, NY), jnp.float32) ** block_levels(keys[3], (NX, NY), ((0, 2), (1, 4)), -0.2, 0.2)), 1.5, 4.0)
    mass = jnp.clip(0.2 + 0.8 * jax.random.uniform(keys[4], (NX, NY), jnp.float32) ** block_levels(keys[4], (NX, NY), ((0, 2), (1, 4)), -0.2, 0.2), 0.2, 1.0)
    omega = jnp.clip(jnp.exp(math.log(0.45) - 1.0986122 * jax.random.uniform(keys[5], (FREQS,), jnp.float32) ** block_levels(keys[5], (FREQS,), ((0, 4),), -0.2, 0.2)), 0.15, 0.45)
    send_rows = draw_send_rows(jax.random.fold_in(keys[9], 71), 0)
    recv_rows = draw_recv_rows(jax.random.fold_in(keys[9], 71), 0)
    mortar_weight = draw_mortar_weight(jax.random.fold_in(keys[9], 71), 0)
    return dict(adjoint_rhs=adjoint_rhs, state=state, density=density, stiffness=stiffness, mass=mass, omega=omega, send_rows=send_rows, recv_rows=recv_rows, mortar_weight=mortar_weight)


def edge_sum(field):
    padded = jnp.pad(field, ((0, 0), (1, 1), (1, 1)))
    return padded[:, 2:, 1:-1] + padded[:, :-2, 1:-1] + padded[:, 1:-1, 2:] + padded[:, 1:-1, :-2]


def global_cells(device, local):
    row_dev = device // N_MY
    col_dev = device % N_MY
    return (row_dev * CX + local // CY) * NY + col_dev * CY + local % CY


def reference(adjoint_rhs, state, density, stiffness, mass, omega, send_rows, recv_rows, mortar_weight):
    peers = N_MX * N_MY
    senders = send_rows.reshape(peers, peers, CAP).transpose(1, 0, 2)
    dest_ids = jnp.arange(peers, dtype=jnp.int32)[:, None, None]
    src_ids = jnp.arange(peers, dtype=jnp.int32)[None, :, None]
    sources = global_cells(src_ids, senders).reshape(-1)
    targets = global_cells(dest_ids, recv_rows.reshape(peers, peers, CAP)).reshape(-1)
    weights = mortar_weight.reshape(-1)
    stiff = density ** 3 * stiffness
    dstiff = 3.0 * density ** 2 * stiffness
    rmass = density * mass
    mdiag = jnp.zeros((NX * NY,), jnp.float32).at[targets].add(weights).reshape(NX, NY)
    adjoints = []
    total = jnp.zeros((NX, NY), jnp.float32)
    for freq_index in range(FREQS):
        w = omega[freq_index]
        real_d = 4.4 * stiff + 0.3 + mdiag - w * w * rmass
        imag_d = 0.2 * w * (stiff + rmass)
        den = real_d * real_d + imag_d * imag_d
        rhs = adjoint_rhs[freq_index].reshape(6, NX, NY)

        def sweep(step, field):
            flat = field.reshape(6, NX * NY)
            mortar = jnp.zeros((6, NX * NY), jnp.float32).at[:, targets].add(flat[:, sources] * weights)
            h = rhs + stiff * edge_sum(field) + mortar.reshape(6, NX, NY)
            new_re = (h[:3] * real_d + h[3:] * imag_d) / den
            new_im = (h[3:] * real_d - h[:3] * imag_d) / den
            return jnp.concatenate([new_re, new_im], axis=0)

        field = jax.lax.fori_loop(0, ITERS, sweep, jnp.zeros((6, NX, NY), jnp.float32))
        adjoints.append(field.reshape(2, 3, NX, NY))
        u = state[freq_index].reshape(6, NX, NY).astype(jnp.float32)
        nb = edge_sum(u)
        da = 4.4 * dstiff - w * w * mass
        db = 0.2 * w * (dstiff + mass)
        t_re = da * u[:3] - db * u[3:] - dstiff * nb[:3]
        t_im = da * u[3:] + db * u[:3] - dstiff * nb[3:]
        total = total - jnp.sum(field[:3] * t_re - field[3:] * t_im, axis=0)
    weighted = jnp.pad(density * total, 1)
    filt = weighted[1:-1, 1:-1]
    filt = filt + 0.5 * (weighted[2:, 1:-1] + weighted[:-2, 1:-1] + weighted[1:-1, 2:] + weighted[1:-1, :-2])
    filt = filt + 0.25 * (weighted[2:, 2:] + weighted[:-2, :-2] + weighted[2:, :-2] + weighted[:-2, 2:])
    return jnp.stack(adjoints, axis=0), filt / (4.0 * density)
```

```python
import functools

import jax
import jax.numpy as jnp
from jax import lax
from jax.experimental import pallas as pl
from jax.experimental.pallas import tpu as pltpu
from jax.sharding import PartitionSpec as P

ITERS = 20
PARTS = 3
LANES = 128
F32 = jnp.float32
BF16 = jnp.bfloat16


def extended(x, sides, width):
    for axis, dim in sides:
        size, length = (lax.axis_size(axis), x.shape[dim])
        up = [(i, (i + 1) % size) for i in range(size - 1)]
        down = [(j, i) for i, j in up]
        last = lax.slice_in_dim(x, length - width, length, axis=dim)
        first = lax.slice_in_dim(x, 0, width, axis=dim)
        before = lax.ppermute(last, axis, up)
        after = lax.ppermute(first, axis, down)
        x = jnp.concatenate([before, x, after], axis=dim)
    return x


def pack_kernel(comps, rhs, density, stiffness, mass, send, recv, weight, *outs):
    *outs, pages = outs
    rows = density.shape[0]
    tiles = rows // 8
    cy = density.shape[1]
    info = []
    for ref in (send, recv):
        cell = ref[...]
        x, y = cell // cy, cell % cy
        row = (x % tiles) * 8 + x // tiles + (y // LANES) * rows
        info += [row.astype(F32), (y % LANES).astype(F32)]
    info += [weight[...]]
    slot = 0

    def interleaved(value):
        nonlocal slot
        halves = []
        for u in range(cy // LANES):
            page = pages.at[slot % pages.shape[0]]
            slot += 1
            page[...] = value[:, u * LANES : (u + 1) * LANES]
            halves.append(jnp.concatenate([page[pl.ds(t, 8, stride=tiles), :] for t in range(tiles)], axis=0))
        return jnp.concatenate(halves, axis=1)

    rho = density[...]
    stiff = interleaved(rho * rho * rho * stiffness[...])
    rmass = interleaved(rho * mass[...])
    for s, out in enumerate(outs):
        c = comps[s]
        out[:rows, :] = interleaved(rhs[c])
        out[rows : 2 * rows, :] = interleaved(rhs[PARTS + c])
        out[2 * rows : 3 * rows, :] = stiff
        out[3 * rows : 4 * rows, :] = rmass
    for out in outs:
        for k, line in enumerate(info):
            out[pl.ds(4 * rows + k, 1), :] = line
        out[pl.ds(4 * rows + 5, 3), :] = jnp.zeros((3, cy), F32)


def split(v):
    high = v.astype(BF16)
    return high, (v - high.astype(F32)).astype(BF16)


def sweep_kernel(n_i, n_j, cap, pos, omega, *refs):
    blocks = n_i * n_j
    msgs, refs = refs[: blocks], refs[blocks:]
    outs, refs = refs[:n_j], refs[n_j:]
    field, rhs, stiff, gain, lag, info, take, lane_of, put, weights, picked, pages = refs
    rows = rhs.shape[2] // 2
    slots = blocks * cap
    me_i, me_j = pos[0], pos[1]
    w = omega[0]

    def both(x):
        return x[:, :LANES], x[:, LANES:]

    order = [(a, s) for a in range(n_i) for s in range(n_j)]
    index = [lax.rem(me_i + a, n_i) * n_j + lax.rem(me_j + n_j - s, n_j) for a, s in order]
    for msg, b in zip(msgs, index):
        info[b] = msg[4 * rows :, :]
    lines = jnp.concatenate([info[b] for b in range(blocks)], axis=0)
    columns = jnp.transpose(lines)
    lane = lax.broadcasted_iota(jnp.int32, (slots, LANES), 1)
    depth = lax.broadcasted_iota(jnp.int32, (2 * rows, slots), 0)

    def column(b, kind):
        return jnp.broadcast_to(columns[:, b * 8 + kind : b * 8 + kind + 1], (slots, LANES))

    for b in range(blocks):
        pick = (column(b, 0).astype(jnp.int32) == lane).astype(F32).astype(BF16)
        take[b] = jnp.concatenate([pick, pick], axis=1)
        lane_of[b] = column(b, 1).astype(jnp.int32)
        target = info[b, 2:3, :].astype(jnp.int32)
        spread = (jnp.broadcast_to(target, depth.shape) == depth).astype(F32).astype(BF16)
        put[b] = jnp.concatenate([spread, spread], axis=1)
        weighted = jnp.where(column(b, 3).astype(jnp.int32) == lane, column(b, 4), 0.0)
        for p in range(blocks):
            weights[p, b * cap : (b + 1) * cap, :] = weighted[p * cap : (p + 1) * cap, :]
        high, low = split(weighted)
        gain[b] = jnp.dot(put[b], jnp.concatenate([high, low], axis=0), preferred_element_type=F32)

    for msg, b in zip(msgs, index):
        for u in range(2):
            at = slice(u * rows, (u + 1) * rows)
            lanes = slice(u * LANES, (u + 1) * LANES)
            rhs_re, rhs_im, k, m = [msg[n * rows : (n + 1) * rows, lanes] for n in range(4)]
            real_d = 4.4 * k + 0.3 + gain[b, at] - w * w * m
            imag_d = 0.2 * w * (k + m)
            den = real_d * real_d + imag_d * imag_d
            g, l = real_d / den, imag_d / den
            stiff[b, at], gain[b, at], lag[b, at] = k, g, l
            rhs[b, 0, at], rhs[b, 1, at] = rhs_re, rhs_im
            field[0, b, 0, at] = rhs_re * g + rhs_im * l
            field[0, b, 1, at] = rhs_im * g - rhs_re * l

    row8 = lax.broadcasted_iota(jnp.int32, (8, LANES), 0)
    lane_r = lax.broadcasted_iota(jnp.int32, (rows, LANES), 1)

    def sweep(step, carry):
        now = lax.rem(step, 2)
        then = 1 - now
        for b in range(blocks):
            re_h, re_l = split(field[now, b, 0])
            im_h, im_l = split(field[now, b, 1])
            source = jnp.concatenate(
                [jnp.concatenate([re_h, im_h], axis=1), jnp.concatenate([re_l, im_l], axis=1)], axis=0
            )
            got = jnp.dot(take[b], source, preferred_element_type=F32)
            at_lane, wt = lane_of[b], weights[b]
            for part, g in enumerate(both(got)):
                value = jnp.take_along_axis(g, at_lane, axis=1, mode="promise_in_bounds") * wt
                high, low = split(value)
                lanes = slice(part * LANES, (part + 1) * LANES)
                for q in range(blocks):
                    chunk = slice(q * cap, (q + 1) * cap)
                    picked[q, b * cap : (b + 1) * cap, lanes] = high[chunk]
                    picked[q, slots + b * cap : slots + (b + 1) * cap, lanes] = low[chunk]
        for i in range(n_i):
            for j in range(n_j):
                b = i * n_j + j
                mortar = jnp.dot(put[b], picked[b], preferred_element_type=F32)
                h = [[None, None], [None, None]]
                for part in range(2):
                    whole = field[now, b, part]
                    v = [whole[:rows], whole[rows:]]
                    zero = jnp.zeros((rows, LANES), F32)
                    west = field[now, b - 1, part, rows:] if j > 0 else zero
                    east = field[now, b + 1, part, :rows] if j < n_j - 1 else zero
                    for u in range(2):
                        own = v[u]
                        left = west if u == 0 else v[0]
                        right = v[1] if u == 0 else east
                        around = pltpu.roll(jnp.where(lane_r == LANES - 1, left, own), 1, 1)
                        around += pltpu.roll(jnp.where(lane_r == 0, right, own), LANES - 1, 1)
                        top = pltpu.roll(own[rows - 8 :], 1, 0)
                        bottom = pltpu.roll(own[:8], 7, 0)
                        above = jnp.zeros((8, LANES), F32)
                        below = above
                        if i > 0:
                            above = pltpu.roll(
                                field[now, b - n_j, part, (u + 1) * rows - 8 : (u + 1) * rows], 1, 0
                            )
                        if i < n_i - 1:
                            below = pltpu.roll(field[now, b + n_j, part, u * rows : u * rows + 8], 7, 0)
                        top = jnp.where(row8 == 0, above, top)
                        bottom = jnp.where(row8 == 7, below, bottom)
                        around += jnp.concatenate([top, own[:-8]], axis=0)
                        around += jnp.concatenate([own[8:], bottom], axis=0)
                        at = slice(u * rows, (u + 1) * rows)
                        m = mortar[at, part * LANES : (part + 1) * LANES]
                        h[part][u] = m + rhs[b, part, at] + stiff[b, at] * around
                for u in range(2):
                    at = slice(u * rows, (u + 1) * rows)
                    g, l = gain[b, at], lag[b, at]
                    field[then, b, 0, at] = h[0][u] * g + h[1][u] * l
                    field[then, b, 1, at] = h[1][u] * g - h[0][u] * l
        return carry

    lax.fori_loop(0, ITERS - 1, sweep, 0)
    last = (ITERS - 1) % 2
    tiles = rows // 8
    for s, out in enumerate(outs):
        b = me_i * n_j + lax.rem(me_j + s, n_j)
        for part in range(2):
            for u in range(2):
                page = pages.at[(s * 4 + part * 2 + u) % 8]
                for t in range(tiles):
                    row = u * rows + t * 8
                    page[pl.ds(t, 8, stride=tiles), :] = field[last, b, part, row : row + 8, :]
                out[part, :, u * LANES : (u + 1) * LANES] = page[...]


def vmem():
    return pl.BlockSpec(memory_space=pltpu.VMEM)


def smem():
    return pl.BlockSpec(memory_space=pltpu.SMEM)


def shifts(n_j, source_limit, target_limit):
    return [
        [(a, (a + s) % n_j) for a in range(n_j) if a < source_limit and (a + s) % n_j < target_limit]
        for s in range(1, n_j)
    ]


def solve(rhs, density, stiffness, mass, omega, send_rows, recv_rows, mortar_weight):
    rows, cy = density.shape
    n_i, n_j = lax.axis_size("mx"), lax.axis_size("my")
    blocks = n_i * n_j
    slots = send_rows.shape[1]
    cap = slots // blocks
    me_i, me_j = lax.axis_index("mx"), lax.axis_index("my")
    ahead = (me_j + jnp.arange(n_j, dtype=jnp.int32)) % n_j
    comps = jnp.minimum(ahead, PARTS - 1)
    height = 4 * rows + 8
    message = jax.ShapeDtypeStruct((height, cy), F32)
    own = pl.pallas_call(
        pack_kernel,
        out_shape=[message] * n_j,
        in_specs=[smem()] + [vmem()] * 7,
        out_specs=[vmem()] * n_j,
        scratch_shapes=[pltpu.VMEM((8, rows, LANES), F32)],
        name="pack",
    )(comps, rhs, density, stiffness, mass, send_rows, recv_rows, mortar_weight)
    msgs = [own[0]]
    for s, pairs in enumerate(shifts(n_j, n_j, PARTS), 1):
        msgs.append(lax.ppermute(own[s], "my", pairs))
    swap = [(a, (a + 1) % n_i) for a in range(n_i)]
    for other in range(1, n_i):
        msgs += [lax.ppermute(m, "mx", swap) for m in msgs[-n_j:]]
    pos = jnp.stack([me_i, me_j]).astype(jnp.int32)
    block = (blocks, 2 * rows, LANES)
    outs = pl.pallas_call(
        functools.partial(sweep_kernel, n_i, n_j, cap),
        out_shape=[jax.ShapeDtypeStruct((2, rows, cy), F32)] * n_j,
        in_specs=[smem(), smem()] + [vmem()] * blocks,
        out_specs=[vmem()] * n_j,
        scratch_shapes=[
            pltpu.VMEM((2, blocks, 2, 2 * rows, LANES), F32),
            pltpu.VMEM((blocks, 2, 2 * rows, LANES), F32),
            pltpu.VMEM(block, F32),
            pltpu.VMEM(block, F32),
            pltpu.VMEM(block, F32),
            pltpu.VMEM((blocks, 8, cy), F32),
            pltpu.VMEM((blocks, slots, 4 * rows), BF16),
            pltpu.VMEM((blocks, slots, LANES), jnp.int32),
            pltpu.VMEM((blocks, 2 * rows, 2 * slots), BF16),
            pltpu.VMEM((blocks, slots, LANES), F32),
            pltpu.VMEM((blocks, 2 * slots, 2 * LANES), BF16),
            pltpu.VMEM((8, rows, LANES), F32),
        ],
        compiler_params=pltpu.CompilerParams(vmem_limit_bytes=40 * 1024 * 1024),
        name="sweeps",
    )(pos, omega, *msgs)
    parts = [outs[0]]
    for s, pairs in enumerate(shifts(n_j, PARTS, n_j), 1):
        parts.append(lax.ppermute(outs[s], "my", pairs))
    stacked = jnp.stack(parts)
    comps_of = [lax.dynamic_index_in_dim(stacked, (me_j + n_j - c) % n_j, 0, False) for c in range(PARTS)]
    return jnp.stack(comps_of, axis=1).reshape(2 * PARTS, rows, cy)


def solve_split(rhs, density, stiffness, mass, omega, send_rows, recv_rows, mortar_weight):
    rows_x, rows_y = density.shape
    cells = rows_x * rows_y
    w = omega[0]
    stiff = density**3 * stiffness
    rmass = density * mass
    sources = send_rows[0]
    targets = recv_rows[0]
    weights = mortar_weight[0]
    mdiag = jnp.zeros((cells,), jnp.float32).at[targets].add(weights).reshape(rows_x, rows_y)
    real_d = 4.4 * stiff + 0.3 + mdiag - w * w * rmass
    imag_d = 0.2 * w * (stiff + rmass)
    den = real_d * real_d + imag_d * imag_d

    def mortar(field):
        sent = field.reshape(6, cells)[:, sources]
        got = lax.all_to_all(sent, ("mx", "my"), split_axis=1, concat_axis=1, tiled=True)
        added = jnp.zeros((6, cells), jnp.float32).at[:, targets].add(got * weights)
        return added.reshape(6, rows_x, rows_y)

    def sweep(step, field):
        padded = extended(field, (("mx", 1), ("my", 2)), 1)
        beside = (
            padded[:, 2:, 1:-1] + padded[:, :-2, 1:-1] + padded[:, 1:-1, 2:] + padded[:, 1:-1, :-2]
        )
        h = rhs + stiff * beside + mortar(field)
        new_re = (h[:3] * real_d + h[3:] * imag_d) / den
        new_im = (h[3:] * real_d - h[:3] * imag_d) / den
        return jnp.concatenate([new_re, new_im], axis=0)

    return lax.fori_loop(0, ITERS, sweep, jnp.zeros((6, rows_x, rows_y), jnp.float32))


def on_device(
    adjoint_rhs, state, density, stiffness, mass, omega, send_rows, recv_rows, mortar_weight
):
    rows_x, rows_y = density.shape
    w = omega[0]
    dstiff = 3.0 * density**2 * stiffness
    rhs = adjoint_rhs.reshape(6, rows_x, rows_y)
    n_i, n_j = lax.axis_size("mx"), lax.axis_size("my")
    fits = n_i == 2 and PARTS <= n_j <= 4 and rows_x % 64 == 0 and rows_y == 2 * LANES
    fits = fits and send_rows.shape[1] == rows_y
    system = (rhs, density, stiffness, mass, omega, send_rows, recv_rows, mortar_weight)
    field = (solve if fits else solve_split)(*system)
    state_six = state.reshape(6, rows_x, rows_y)
    state_pad = extended(state_six, (("mx", 1), ("my", 2)), 1).astype(jnp.float32)
    u = state_six.astype(jnp.float32)
    nb = (
        state_pad[:, 2:, 1:-1]
        + state_pad[:, :-2, 1:-1]
        + state_pad[:, 1:-1, 2:]
        + state_pad[:, 1:-1, :-2]
    )
    da = 4.4 * dstiff - w * w * mass
    db = 0.2 * w * (dstiff + mass)
    t_re = da * u[:3] - db * u[3:] - dstiff * nb[:3]
    t_im = da * u[3:] + db * u[:3] - dstiff * nb[3:]
    sens = -jnp.sum(field[:3] * t_re - field[3:] * t_im, axis=0)
    size = lax.axis_size("freq")
    total = sens
    for s in range(1, size):
        total = total + lax.ppermute(sens, "freq", [(a, (a + s) % size) for a in range(size)])
    weighted = extended(density * total, (("mx", 0), ("my", 1)), 1)
    filt = weighted[1:-1, 1:-1]
    filt = filt + 0.5 * (
        weighted[2:, 1:-1] + weighted[:-2, 1:-1] + weighted[1:-1, 2:] + weighted[1:-1, :-2]
    )
    filt = filt + 0.25 * (
        weighted[2:, 2:] + weighted[:-2, :-2] + weighted[2:, :-2] + weighted[:-2, 2:]
    )
    return (field.reshape(1, 2, 3, rows_x, rows_y), filt / (4.0 * density))


def solution(mesh):
    return jax.shard_map(
        on_device,
        mesh=mesh,
        in_specs=(
            P("freq", None, None, "mx", "my"),
            P("freq", None, None, "mx", "my"),
            P("mx", "my"),
            P("mx", "my"),
            P("mx", "my"),
            P("freq"),
            P(("mx", "my"), None),
            P(("mx", "my"), None),
            P(("mx", "my"), None),
        ),
        out_specs=(P("freq", None, None, "mx", "my"), P("mx", "my")),
        check_vma=False,
    )
```

```python
import functools

import jax
import jax.numpy as jnp
from jax import lax
from jax.experimental import pallas as pl
from jax.experimental.pallas import tpu as pltpu
from jax.sharding import PartitionSpec as P

ITERS = 20
PARTS = 3
LANES = 128
F32 = jnp.float32
BF16 = jnp.bfloat16


def extended(x, sides, width):
    for axis, dim in sides:
        size, length = (lax.axis_size(axis), x.shape[dim])
        up = [(i, (i + 1) % size) for i in range(size - 1)]
        down = [(j, i) for i, j in up]
        last = lax.slice_in_dim(x, length - width, length, axis=dim)
        first = lax.slice_in_dim(x, 0, width, axis=dim)
        before = lax.ppermute(last, axis, up)
        after = lax.ppermute(first, axis, down)
        x = jnp.concatenate([before, x, after], axis=dim)
    return x


def pack_kernel(comps, rhs, density, stiffness, mass, send, recv, weight, *outs):
    *outs, pages = outs
    rows = density.shape[0]
    tiles = rows // 8
    cy = density.shape[1]
    info = []
    for ref in (send, recv):
        cell = ref[...]
        x, y = cell // cy, cell % cy
        row = (x % tiles) * 8 + x // tiles + (y // LANES) * rows
        info += [row.astype(F32), (y % LANES).astype(F32)]
    info += [weight[...]]
    slot = 0

    def interleaved(value):
        nonlocal slot
        halves = []
        for u in range(cy // LANES):
            page = pages.at[slot % pages.shape[0]]
            slot += 1
            page[...] = value[:, u * LANES : (u + 1) * LANES]
            halves.append(jnp.concatenate([page[pl.ds(t, 8, stride=tiles), :] for t in range(tiles)], axis=0))
        return jnp.concatenate(halves, axis=1)

    rho = density[...]
    stiff = interleaved(rho * rho * rho * stiffness[...])
    rmass = interleaved(rho * mass[...])
    for s, out in enumerate(outs):
        c = comps[s]
        out[:rows, :] = interleaved(rhs[c])
        out[rows : 2 * rows, :] = interleaved(rhs[PARTS + c])
        out[2 * rows : 3 * rows, :] = stiff
        out[3 * rows : 4 * rows, :] = rmass
    for out in outs:
        for k, line in enumerate(info):
            out[pl.ds(4 * rows + k, 1), :] = line
        out[pl.ds(4 * rows + 5, 3), :] = jnp.zeros((3, cy), F32)


def split(v):
    high = v.astype(BF16)
    return high, (v - high.astype(F32)).astype(BF16)


def sweep_kernel(n_i, n_j, cap, pos, omega, *refs):
    blocks = n_i * n_j
    msgs, refs = refs[: blocks], refs[blocks:]
    outs, refs = refs[:n_j], refs[n_j:]
    field, rhs, stiff, gain, lag, info, weights, pick, rowmask, spread, place, group, values, pages = refs
    rows = rhs.shape[2] // 2
    slots = blocks * cap
    me_i, me_j = pos[0], pos[1]
    w = omega[0]

    order = [(a, s) for a in range(n_i) for s in range(n_j)]
    index = [lax.rem(me_i + a, n_i) * n_j + lax.rem(me_j + n_j - s, n_j) for a, s in order]
    for msg, b in zip(msgs, index):
        info[b] = msg[4 * rows :, :]
    depth = lax.broadcasted_iota(jnp.int32, (LANES, slots), 0)
    chunk = lax.broadcasted_iota(jnp.int32, (blocks, slots), 1) // cap
    source = lax.broadcasted_iota(jnp.int32, (blocks, slots), 0)

    def one_hot(line):
        return (jnp.broadcast_to(line.astype(jnp.int32), depth.shape) == depth).astype(F32)

    for b in range(blocks):
        line = info[b]
        line = pltpu.roll(line, b * cap, 1) if b else line
        lane_in = one_hot(line[1:2]).astype(BF16)
        pick[b] = jnp.concatenate([lane_in, lane_in], axis=0)
        rowmask[b] = one_hot(line[0:1])
        row_out = one_hot(line[2:3])
        spread[b] = row_out.astype(BF16)
        lane_out = jnp.transpose(one_hot(line[3:4])).astype(BF16)
        place[b] = jnp.concatenate([lane_out, lane_out], axis=0)
        group[b] = (chunk == (source + b) % blocks).astype(F32)
        weights[pl.ds(b, 1), :] = line[4:5]
        high, low = split(row_out * line[4:5])
        gain[b] = jnp.dot(jnp.concatenate([high, low], axis=1), place[b], preferred_element_type=F32)

    for msg, b in zip(msgs, index):
        for u in range(2):
            at = slice(u * rows, (u + 1) * rows)
            lanes = slice(u * LANES, (u + 1) * LANES)
            rhs_re, rhs_im, k, m = [msg[n * rows : (n + 1) * rows, lanes] for n in range(4)]
            real_d = 4.4 * k + 0.3 + gain[b, at] - w * w * m
            imag_d = 0.2 * w * (k + m)
            den = real_d * real_d + imag_d * imag_d
            g, l = real_d / den, imag_d / den
            stiff[b, at], gain[b, at], lag[b, at] = k, g, l
            rhs[b, 0, at], rhs[b, 1, at] = rhs_re, rhs_im
            field[0, b, 0, at] = rhs_re * g + rhs_im * l
            field[0, b, 1, at] = rhs_im * g - rhs_re * l

    row8 = lax.broadcasted_iota(jnp.int32, (8, LANES), 0)
    lane_r = lax.broadcasted_iota(jnp.int32, (rows, LANES), 1)

    def sweep(step, carry):
        now = lax.rem(step, 2)
        then = 1 - now
        for b in range(blocks):
            whole = jnp.concatenate([field[now, b, 0], field[now, b, 1]], axis=0)
            got = jnp.dot(jnp.concatenate(split(whole), axis=1), pick[b], preferred_element_type=F32)
            for part in range(2):
                mine = got[part * LANES : (part + 1) * LANES] * rowmask[b]
                values[part, pl.ds(b, 1), :] = jnp.sum(mine, axis=0, keepdims=True)
        for i in range(n_i):
            for j in range(n_j):
                b = i * n_j + j
                left = []
                for part in range(2):
                    arrived = jnp.sum(values[part] * group[b], axis=0, keepdims=True)
                    high, low = split(arrived * weights[b : b + 1, :])
                    left.append(jnp.concatenate([spread[b] * high, spread[b] * low], axis=1))
                mortar = jnp.dot(jnp.concatenate(left, axis=0), place[b], preferred_element_type=F32)
                h = [[None, None], [None, None]]
                for part in range(2):
                    whole = field[now, b, part]
                    v = [whole[:rows], whole[rows:]]
                    zero = jnp.zeros((rows, LANES), F32)
                    west = field[now, b - 1, part, rows:] if j > 0 else zero
                    east = field[now, b + 1, part, :rows] if j < n_j - 1 else zero
                    for u in range(2):
                        own = v[u]
                        left = west if u == 0 else v[0]
                        right = v[1] if u == 0 else east
                        around = pltpu.roll(jnp.where(lane_r == LANES - 1, left, own), 1, 1)
                        around += pltpu.roll(jnp.where(lane_r == 0, right, own), LANES - 1, 1)
                        top = pltpu.roll(own[rows - 8 :], 1, 0)
                        bottom = pltpu.roll(own[:8], 7, 0)
                        above = jnp.zeros((8, LANES), F32)
                        below = above
                        if i > 0:
                            above = pltpu.roll(
                                field[now, b - n_j, part, (u + 1) * rows - 8 : (u + 1) * rows], 1, 0
                            )
                        if i < n_i - 1:
                            below = pltpu.roll(field[now, b + n_j, part, u * rows : u * rows + 8], 7, 0)
                        top = jnp.where(row8 == 0, above, top)
                        bottom = jnp.where(row8 == 7, below, bottom)
                        around += jnp.concatenate([top, own[:-8]], axis=0)
                        around += jnp.concatenate([own[8:], bottom], axis=0)
                        at = slice(u * rows, (u + 1) * rows)
                        m = mortar[part * 2 * rows + u * rows : part * 2 * rows + (u + 1) * rows]
                        h[part][u] = m + rhs[b, part, at] + stiff[b, at] * around
                for u in range(2):
                    at = slice(u * rows, (u + 1) * rows)
                    g, l = gain[b, at], lag[b, at]
                    field[then, b, 0, at] = h[0][u] * g + h[1][u] * l
                    field[then, b, 1, at] = h[1][u] * g - h[0][u] * l
        return carry

    lax.fori_loop(0, ITERS - 1, sweep, 0)
    last = (ITERS - 1) % 2
    tiles = rows // 8
    for s, out in enumerate(outs):
        b = me_i * n_j + lax.rem(me_j + s, n_j)
        for part in range(2):
            for u in range(2):
                page = pages.at[(s * 4 + part * 2 + u) % 8]
                for t in range(tiles):
                    row = u * rows + t * 8
                    page[pl.ds(t, 8, stride=tiles), :] = field[last, b, part, row : row + 8, :]
                out[part, :, u * LANES : (u + 1) * LANES] = page[...]


def vmem():
    return pl.BlockSpec(memory_space=pltpu.VMEM)


def smem():
    return pl.BlockSpec(memory_space=pltpu.SMEM)


def shifts(n_j, source_limit, target_limit):
    return [
        [(a, (a + s) % n_j) for a in range(n_j) if a < source_limit and (a + s) % n_j < target_limit]
        for s in range(1, n_j)
    ]


def solve(rhs, density, stiffness, mass, omega, send_rows, recv_rows, mortar_weight):
    rows, cy = density.shape
    n_i, n_j = lax.axis_size("mx"), lax.axis_size("my")
    blocks = n_i * n_j
    slots = send_rows.shape[1]
    cap = slots // blocks
    me_i, me_j = lax.axis_index("mx"), lax.axis_index("my")
    ahead = (me_j + jnp.arange(n_j, dtype=jnp.int32)) % n_j
    comps = jnp.minimum(ahead, PARTS - 1)
    height = 4 * rows + 8
    message = jax.ShapeDtypeStruct((height, cy), F32)
    own = pl.pallas_call(
        pack_kernel,
        out_shape=[message] * n_j,
        in_specs=[smem()] + [vmem()] * 7,
        out_specs=[vmem()] * n_j,
        scratch_shapes=[pltpu.VMEM((8, rows, LANES), F32)],
        name="pack",
    )(comps, rhs, density, stiffness, mass, send_rows, recv_rows, mortar_weight)
    msgs = [own[0]]
    for s, pairs in enumerate(shifts(n_j, n_j, PARTS), 1):
        msgs.append(lax.ppermute(own[s], "my", pairs))
    swap = [(a, (a + 1) % n_i) for a in range(n_i)]
    for other in range(1, n_i):
        msgs += [lax.ppermute(m, "mx", swap) for m in msgs[-n_j:]]
    pos = jnp.stack([me_i, me_j]).astype(jnp.int32)
    block = (blocks, 2 * rows, LANES)
    outs = pl.pallas_call(
        functools.partial(sweep_kernel, n_i, n_j, cap),
        out_shape=[jax.ShapeDtypeStruct((2, rows, cy), F32)] * n_j,
        in_specs=[smem(), smem()] + [vmem()] * blocks,
        out_specs=[vmem()] * n_j,
        scratch_shapes=[
            pltpu.VMEM((2, blocks, 2, 2 * rows, LANES), F32),
            pltpu.VMEM((blocks, 2, 2 * rows, LANES), F32),
            pltpu.VMEM(block, F32),
            pltpu.VMEM(block, F32),
            pltpu.VMEM(block, F32),
            pltpu.VMEM((blocks, 8, cy), F32),
            pltpu.VMEM((blocks, slots), F32),
            pltpu.VMEM((blocks, 2 * LANES, slots), BF16),
            pltpu.VMEM((blocks, 2 * rows, slots), F32),
            pltpu.VMEM((blocks, 2 * rows, slots), BF16),
            pltpu.VMEM((blocks, 2 * slots, LANES), BF16),
            pltpu.VMEM((blocks, blocks, slots), F32),
            pltpu.VMEM((2, blocks, slots), F32),
            pltpu.VMEM((8, rows, LANES), F32),
        ],
        compiler_params=pltpu.CompilerParams(vmem_limit_bytes=40 * 1024 * 1024),
        name="sweeps",
    )(pos, omega, *msgs)
    parts = [outs[0]]
    for s, pairs in enumerate(shifts(n_j, PARTS, n_j), 1):
        parts.append(lax.ppermute(outs[s], "my", pairs))
    stacked = jnp.stack(parts)
    comps_of = [lax.dynamic_index_in_dim(stacked, (me_j + n_j - c) % n_j, 0, False) for c in range(PARTS)]
    return jnp.stack(comps_of, axis=1).reshape(2 * PARTS, rows, cy)


def solve_split(rhs, density, stiffness, mass, omega, send_rows, recv_rows, mortar_weight):
    rows_x, rows_y = density.shape
    cells = rows_x * rows_y
    w = omega[0]
    stiff = density**3 * stiffness
    rmass = density * mass
    sources = send_rows[0]
    targets = recv_rows[0]
    weights = mortar_weight[0]
    mdiag = jnp.zeros((cells,), jnp.float32).at[targets].add(weights).reshape(rows_x, rows_y)
    real_d = 4.4 * stiff + 0.3 + mdiag - w * w * rmass
    imag_d = 0.2 * w * (stiff + rmass)
    den = real_d * real_d + imag_d * imag_d

    def mortar(field):
        sent = field.reshape(6, cells)[:, sources]
        got = lax.all_to_all(sent, ("mx", "my"), split_axis=1, concat_axis=1, tiled=True)
        added = jnp.zeros((6, cells), jnp.float32).at[:, targets].add(got * weights)
        return added.reshape(6, rows_x, rows_y)

    def sweep(step, field):
        padded = extended(field, (("mx", 1), ("my", 2)), 1)
        beside = (
            padded[:, 2:, 1:-1] + padded[:, :-2, 1:-1] + padded[:, 1:-1, 2:] + padded[:, 1:-1, :-2]
        )
        h = rhs + stiff * beside + mortar(field)
        new_re = (h[:3] * real_d + h[3:] * imag_d) / den
        new_im = (h[3:] * real_d - h[:3] * imag_d) / den
        return jnp.concatenate([new_re, new_im], axis=0)

    return lax.fori_loop(0, ITERS, sweep, jnp.zeros((6, rows_x, rows_y), jnp.float32))


def on_device(
    adjoint_rhs, state, density, stiffness, mass, omega, send_rows, recv_rows, mortar_weight
):
    rows_x, rows_y = density.shape
    w = omega[0]
    dstiff = 3.0 * density**2 * stiffness
    rhs = adjoint_rhs.reshape(6, rows_x, rows_y)
    n_i, n_j = lax.axis_size("mx"), lax.axis_size("my")
    fits = n_i == 2 and PARTS <= n_j <= 4 and 2 * rows_x == LANES and rows_y == 2 * LANES
    fits = fits and send_rows.shape[1] == rows_y
    system = (rhs, density, stiffness, mass, omega, send_rows, recv_rows, mortar_weight)
    field = (solve if fits else solve_split)(*system)
    state_six = state.reshape(6, rows_x, rows_y)
    state_pad = extended(state_six, (("mx", 1), ("my", 2)), 1).astype(jnp.float32)
    u = state_six.astype(jnp.float32)
    nb = (
        state_pad[:, 2:, 1:-1]
        + state_pad[:, :-2, 1:-1]
        + state_pad[:, 1:-1, 2:]
        + state_pad[:, 1:-1, :-2]
    )
    da = 4.4 * dstiff - w * w * mass
    db = 0.2 * w * (dstiff + mass)
    t_re = da * u[:3] - db * u[3:] - dstiff * nb[:3]
    t_im = da * u[3:] + db * u[:3] - dstiff * nb[3:]
    sens = -jnp.sum(field[:3] * t_re - field[3:] * t_im, axis=0)
    size = lax.axis_size("freq")
    total = sens
    for s in range(1, size):
        total = total + lax.ppermute(sens, "freq", [(a, (a + s) % size) for a in range(size)])
    weighted = extended(density * total, (("mx", 0), ("my", 1)), 1)
    filt = weighted[1:-1, 1:-1]
    filt = filt + 0.5 * (
        weighted[2:, 1:-1] + weighted[:-2, 1:-1] + weighted[1:-1, 2:] + weighted[1:-1, :-2]
    )
    filt = filt + 0.25 * (
        weighted[2:, 2:] + weighted[:-2, :-2] + weighted[2:, :-2] + weighted[:-2, 2:]
    )
    return (field.reshape(1, 2, 3, rows_x, rows_y), filt / (4.0 * density))


def solution(mesh):
    return jax.shard_map(
        on_device,
        mesh=mesh,
        in_specs=(
            P("freq", None, None, "mx", "my"),
            P("freq", None, None, "mx", "my"),
            P("mx", "my"),
            P("mx", "my"),
            P("mx", "my"),
            P("freq"),
            P(("mx", "my"), None),
            P(("mx", "my"), None),
            P(("mx", "my"), None),
        ),
        out_specs=(P("freq", None, None, "mx", "my"), P("mx", "my")),
        check_vma=False,
    )
```

```python
import functools

import jax
import jax.numpy as jnp
from jax import lax
from jax.experimental import pallas as pl
from jax.experimental.pallas import tpu as pltpu
from jax.sharding import PartitionSpec as P

ITERS = 20
PARTS = 3
LANES = 128
F32 = jnp.float32
BF16 = jnp.bfloat16


def extended(x, sides, width):
    for axis, dim in sides:
        size, length = (lax.axis_size(axis), x.shape[dim])
        up = [(i, (i + 1) % size) for i in range(size - 1)]
        down = [(j, i) for i, j in up]
        last = lax.slice_in_dim(x, length - width, length, axis=dim)
        first = lax.slice_in_dim(x, 0, width, axis=dim)
        before = lax.ppermute(last, axis, up)
        after = lax.ppermute(first, axis, down)
        x = jnp.concatenate([before, x, after], axis=dim)
    return x


def placed(cell, rows, cy):
    x, y = cell // cy, cell % cy
    tiles = rows // 8
    return (x % tiles) * 8 + x // tiles, (y % 2) * LANES + y // 2


def lane_order(cy, inverse):
    a = lax.broadcasted_iota(jnp.int32, (cy, cy), 0)
    b = lax.broadcasted_iota(jnp.int32, (cy, cy), 1)
    natural, kept = (b, a) if inverse else (a, b)
    return ((natural % 2) * LANES + natural // 2 == kept).astype(F32)


STIFF_SCALE, STIFF_POWER = 1.92, 96.0
MASS_SCALE, MASS_POWER = 1.0, 16.0
POWER, FLOOR, SHIFT = 30.0, 1.0 / 256.0, 4.0


def coded(v, most):
    size = jnp.exp2(POWER * (jnp.log2(jnp.abs(v) / most + FLOOR) + SHIFT))
    return jnp.where(v < 0.0, -size, size).astype(BF16)


def decoded(v, most):
    v = v.astype(F32)
    size = (jnp.exp2(jnp.log2(jnp.abs(v)) * (1.0 / POWER) - SHIFT) - FLOOR) * most
    return jnp.where(v < 0.0, -size, size)


def largest(*arrays):
    tops = [jnp.max(jnp.abs(v), axis=(0, 1), keepdims=True) for v in arrays]
    return jnp.maximum(functools.reduce(jnp.maximum, tops), 1e-30)


def raised(v, scale, power):
    return jnp.exp2(power * jnp.log2(v * (1.0 / scale))).astype(BF16)


def lowered(v, scale, power):
    return scale * jnp.exp2(jnp.log2(v.astype(F32)) * (1.0 / power))


def pieces(v):
    out = []
    for _ in range(3):
        out.append(v.astype(BF16).astype(F32))
        v = v - out[-1]
    return out


def permuted(v, order):
    return jnp.dot(v, order, precision=lax.Precision.HIGHEST, preferred_element_type=F32)


def pack_kernel(n_j, rhs, density, stiffness, mass, send, recv, weight, *outs):
    *outs, pages = outs
    rows, cy = density.shape
    tiles = rows // 8
    info = []
    for ref in (send, recv):
        row, column = placed(ref[...], rows, cy)
        info += [row.astype(F32), column.astype(F32)]
    info += pieces(weight[...])
    order = lane_order(cy, False)
    slot = 0

    def packed(value):
        nonlocal slot
        value = permuted(value, order)
        halves = []
        for u in range(cy // LANES):
            page = pages.at[slot % pages.shape[0]]
            slot += 1
            page[...] = value[:, u * LANES : (u + 1) * LANES]
            halves.append(jnp.concatenate([page[pl.ds(t, 8, stride=tiles), :] for t in range(tiles)], axis=0))
        return jnp.concatenate(halves, axis=1)

    rho = density[...]
    stiff = raised(packed(rho * rho * rho * stiffness[...]), STIFF_SCALE, STIFF_POWER)
    rmass = raised(packed(rho * mass[...]), MASS_SCALE, MASS_POWER)
    for s, out in enumerate(outs):
        c = jnp.minimum(lax.rem(lax.axis_index("my") + s, n_j), PARTS - 1)
        re, im = rhs[c], rhs[PARTS + c]
        most = largest(re, im)
        out[:rows, :] = coded(packed(re), most)
        out[rows : 2 * rows, :] = coded(packed(im), most)
        out[2 * rows : 3 * rows, :] = stiff
        out[3 * rows : 4 * rows, :] = rmass
        scale = [jnp.broadcast_to(x, (1, cy)) for x in pieces(most)]
        out[4 * rows :, :] = jnp.concatenate(info + scale + [jnp.zeros((6, cy), F32)], axis=0).astype(BF16)


def split(v):
    high = v.astype(BF16)
    return high, (v - high.astype(F32)).astype(BF16)


def sweep_kernel(n_i, n_j, cap, omega, *refs):
    blocks = n_i * n_j
    msgs, refs = refs[: blocks], refs[blocks:]
    outs, refs = refs[:n_j], refs[n_j:]
    field_a, field_b, start, inverse, gain, lag, info, weights, pick, rowmask, spread, place, group, values, pages, plain, ends, rim, frame = refs
    rows, cy = start.shape[2:]
    slots = blocks * cap
    me_i, me_j = lax.axis_index("mx"), lax.axis_index("my")
    w = omega[0]

    order = [(a, s) for a in range(n_i) for s in range(n_j)]
    index = [lax.rem(me_i + a, n_i) * n_j + lax.rem(me_j + n_j - s, n_j) for a, s in order]
    for msg, b in zip(msgs, index):
        info[b] = msg[4 * rows :, :].astype(F32)
    chunk = lax.broadcasted_iota(jnp.int32, (blocks, slots), 1) // cap
    source = lax.broadcasted_iota(jnp.int32, (blocks, slots), 0)

    def one_hot(line, depth):
        at = lax.broadcasted_iota(jnp.int32, (depth, slots), 0)
        return (jnp.broadcast_to(line.astype(jnp.int32), at.shape) == at).astype(F32)

    for b in range(blocks):
        line = info[b]
        line = pltpu.roll(line, b * cap, 1) if b else line
        pick[b] = one_hot(line[1:2], cy).astype(BF16)
        rowmask[b] = one_hot(line[0:1], rows)
        row_out = one_hot(line[2:3], rows)
        spread[b] = row_out.astype(BF16)
        lane_out = jnp.transpose(one_hot(line[3:4], cy)).astype(BF16)
        place[b] = lane_out
        group[b] = (chunk == (source + b) % blocks).astype(F32)
        high, low = split(row_out * (line[4:5] + line[5:6] + line[6:7]))
        both = jnp.dot(jnp.concatenate([high, low], axis=0), lane_out, preferred_element_type=F32)
        gain[b] = both[:rows] + both[rows:]

    for msg, b in zip(msgs, index):
        rhs_re, rhs_im, k, m = [msg[n * rows : (n + 1) * rows, :] for n in range(4)]
        most = info[b][7:8] + info[b][8:9] + info[b][9:10]
        rhs_re, rhs_im = decoded(rhs_re, most), decoded(rhs_im, most)
        k, m = lowered(k, STIFF_SCALE, STIFF_POWER), lowered(m, MASS_SCALE, MASS_POWER)
        real_d = 4.4 * k + 0.3 + gain[b] - w * w * m
        imag_d = 0.2 * w * (k + m)
        scale = 1.0 / (real_d * real_d + imag_d * imag_d)
        g, l = real_d * scale, imag_d * scale
        first_re, first_im = rhs_re * g + rhs_im * l, rhs_im * g - rhs_re * l
        gain[b], lag[b], inverse[b] = k * g, k * l, 1.0 / k
        start[b, 0], start[b, 1] = first_re, first_im
        field_a[b, 0], field_a[b, 1] = first_re, first_im

    for b in range(blocks):
        line = info[b]
        line = pltpu.roll(line, b * cap, 1) if b else line
        lane_out = one_hot(line[3:4], cy).astype(BF16)
        found = jnp.dot(jnp.concatenate(split(inverse[b]), axis=0), lane_out, preferred_element_type=F32)
        found = (found[:rows] + found[rows:]) * one_hot(line[2:3], rows)
        found = jnp.sum(found, axis=0, keepdims=True)
        weights[pl.ds(b, 1), :] = (line[4:5] + line[5:6] + line[6:7]) * found

    row8 = lax.broadcasted_iota(jnp.int32, (8, LANES), 0)
    lane_r = lax.broadcasted_iota(jnp.int32, (rows, LANES), 1)
    zero = jnp.zeros((rows, LANES), F32)

    def gather(now, b):
        high, low = split(jnp.concatenate([now[b, 0], now[b, 1]], axis=0))
        got = jnp.dot(jnp.concatenate([high, low], axis=0), pick[b], preferred_element_type=F32)
        for part in range(2):
            mine = got[part * rows : (part + 1) * rows] + got[(part + 2) * rows : (part + 3) * rows]
            values[part, pl.ds(b, 1), :] = jnp.sum(mine * rowmask[b], axis=0, keepdims=True)

    def beside(now, then, b):
        i, j = b // n_j, b % n_j
        for u in range(2):
            lanes = slice(u * LANES, (u + 1) * LANES)
            others = slice((1 - u) * LANES, (2 - u) * LANES)
            for part in range(2):
                own, other = now[b, part, :, lanes], now[b, part, :, others]
                if u == 0:
                    edge = now[b - 1, part, :, others] if j > 0 else zero
                    around = pltpu.roll(jnp.where(lane_r == LANES - 1, edge, other), 1, 1)
                else:
                    edge = now[b + 1, part, :, others] if j < n_j - 1 else zero
                    around = pltpu.roll(jnp.where(lane_r == 0, edge, other), LANES - 1, 1)
                around += other
                above = now[b - n_j, part, rows - 8 :, lanes] if i > 0 else zero[:8]
                below = now[b + n_j, part, :8, lanes] if i < n_i - 1 else zero[:8]
                top = pltpu.roll(jnp.where(row8 == 7, above, own[rows - 8 :]), 1, 0)
                bottom = pltpu.roll(jnp.where(row8 == 0, below, own[:8]), 7, 0)
                around += jnp.concatenate([top, own[:-8]], axis=0)
                around += jnp.concatenate([own[8:], bottom], axis=0)
                then[b, part, :, lanes] = around

    def scatter(then, b):
        left = []
        for part in range(2):
            arrived = jnp.sum(values[part] * group[b], axis=0, keepdims=True)
            left += [spread[b] * x for x in split(arrived * weights[b : b + 1, :])]
        mortar = jnp.dot(jnp.concatenate(left, axis=0), place[b], preferred_element_type=F32)
        sums = [
            then[b, part] + mortar[2 * part * rows : (2 * part + 1) * rows]
            + mortar[(2 * part + 1) * rows : (2 * part + 2) * rows]
            for part in range(2)
        ]
        g, l = gain[b], lag[b]
        then[b, 0] = start[b, 0] + sums[0] * g + sums[1] * l
        then[b, 1] = start[b, 1] + sums[1] * g - sums[0] * l

    def sweep(now, then):
        for b in range(blocks):
            if b < blocks:
                gather(now, b)
            if b >= 0:
                beside(now, then, b - 0)
        for b in range(blocks):
            scatter(then, b)

    def pair(step, carry):
        sweep(field_a, field_b)
        sweep(field_b, field_a)
        return carry

    lax.fori_loop(0, (ITERS - 1) // 2, pair, 0)
    last = field_a
    if (ITERS - 1) % 2:
        sweep(field_a, field_b)
        last = field_b
    tiles = rows // 8
    back = lane_order(cy, True)
    around_mesh = jnp.zeros((rows, LANES), F32)
    for part in range(2):
        for at in (0, LANES + n_j * cy):
            plain[part, :, at : at + LANES] = around_mesh
            ends[part, :, at : at + LANES] = around_mesh[:8]
    end = jnp.where(me_i == 0, 0, rows - 1)
    rim[...] = jnp.zeros_like(rim)
    for j in range(n_j):
        for part in range(2):
            halves = []
            for u in range(2):
                page = pages.at[(j * 4 + part * 2 + u) % 8]
                lanes = slice(u * LANES, (u + 1) * LANES)
                for t in range(tiles):
                    page[pl.ds(t, 8, stride=tiles), :] = last[me_i * n_j + j, part, t * 8 : (t + 1) * 8, lanes]
                halves.append(page[...])
            plain[part, :, LANES + j * cy : LANES + (j + 1) * cy] = permuted(jnp.concatenate(halves, axis=1), back)
            rim[pl.ds(part * 4 + j, 1), :] = last[(1 - me_i) * n_j + j, part, pl.ds(end, 1), :]
    natural = permuted(rim[...], back)
    ends[:, :, LANES : LANES + n_j * cy] = jnp.zeros((2, 8, n_j * cy), F32)
    for j in range(n_j):
        for part in range(2):
            for at in (0, 7):
                ends[part, at : at + 1, LANES + j * cy : LANES + (j + 1) * cy] = natural[
                    part * 4 + j : part * 4 + j + 1
                ]
    for s, out in enumerate(outs):
        base = pl.multiple_of(LANES + lax.rem(me_j + s, n_j) * cy, LANES)
        frame[...] = jnp.zeros_like(frame)
        block = [plain[part, :, pl.ds(base, cy)] for part in range(2)]
        for part in range(2):
            frame[pl.ds(part * 8, 1), :] = ends[part, 0:1, pl.ds(base, cy)]
            for k, (at, lane) in enumerate(((base - LANES, LANES - 1), (base + cy, 0)), 1):
                at = pl.multiple_of(at, LANES)
                beyond = [plain[part, :, pl.ds(at, LANES)], ends[part, :, pl.ds(at, LANES)]]
                beyond = beyond + [jnp.zeros((LANES - rows - 16, LANES), F32), beyond[1]]
                beyond = jnp.concatenate(beyond, axis=0)
                frame[pl.ds(part * 8 + k, 1), :LANES] = jnp.transpose(beyond)[lane : lane + 1]
        block.append(frame[...])
        if s:
            most = largest(*block)
            block = [coded(v, most) for v in block]
            row = lax.broadcasted_iota(jnp.int32, (16, cy), 0)
            for k, piece in enumerate(pieces(most)):
                block[2] = jnp.where(row == 3 + k, piece, block[2].astype(F32)).astype(BF16)
        for v, at in zip(block, (0, rows, 2 * rows)):
            out[at : at + v.shape[0], :] = v


def planes_of(state, density, stiffness, mass):
    return [state[n].astype(F32) for n in range(2 * PARTS)] + [density[...], stiffness[...], mass[...]]


def edge_kernel(state, density, stiffness, mass, first, last, line):
    rows, cy = density.shape
    for out in (first, last, line):
        out[...] = jnp.zeros_like(out)
    top = lax.axis_index("mx") == 0
    lane = lax.broadcasted_iota(jnp.int32, (1, LANES), 1)
    for n, v in enumerate(planes_of(state, density, stiffness, mass)):
        turned = jnp.transpose(jnp.concatenate([v[:, :LANES], v[:, cy - LANES :]], axis=0))
        late = pltpu.roll(turned[LANES - 8 :], rows, 1)
        for k in range(2):
            at = pl.ds(16 * k + n, 1)
            first[at, :] = jnp.where(lane < rows, turned[k : k + 1], 0.0)
            last[at, :] = jnp.where(lane < rows, late[7 - k : 8 - k], 0.0)
            line[at, :] = jnp.where(top, v[rows - 1 - k : rows - k], v[k : k + 1])


def response_kernel(
    omega, state, density, stiffness, mass, first, last, west, east, beyond, inner, ring, rho_ring
):
    rows, cy = density.shape
    w = omega[0]
    top = lax.axis_index("mx") == 0
    zero = jnp.zeros((1, cy), F32)

    def terms(u_re, u_im, nb_re, nb_im, rho, k, m):
        dstiff = 3.0 * rho * rho * k
        da = 4.4 * dstiff - w * w * m
        db = 0.2 * w * (dstiff + m)
        return da * u_re - db * u_im - dstiff * nb_re, da * u_im + db * u_re - dstiff * nb_im

    line = beyond[:, :cy]
    siblings = (beyond[:, cy : cy + LANES], beyond[:, cy + LANES :])
    side = [x[...] + pltpu.roll(y, rows, 1) for x, y in zip((west, east), siblings)]
    lane = lax.broadcasted_iota(jnp.int32, (16, LANES), 1)
    start = jnp.where(top, 0, rows)
    stop = jnp.where(top, LANES - 1, rows - 1)
    corner = (lane == rows) | (lane == LANES - 1)
    around = []
    lane_cy = lax.broadcasted_iota(jnp.int32, (16, cy), 1)
    near = line[:16]
    touch = [jnp.where(top, y[:16, 0:1], y[:16, rows - 1 : rows]) for y in siblings]
    before = jnp.where(lane_cy == 0, touch[0], pltpu.roll(near, 1, 1))
    after = jnp.where(lane_cy == cy - 1, touch[1], pltpu.roll(near, cy - 1, 1))
    adjacent = []
    planes = planes_of(state, density, stiffness, mass)
    for v in planes:
        adjacent.append(jnp.where(top, v[rows - 1 :], v[:1]))
    adjacent = jnp.concatenate(adjacent + [zero] * 7, axis=0)
    around.append(line[16:] + adjacent + before + after)
    for x, own, at in ((side[0], first, 0), (side[1], last, cy - 1)):
        own = jnp.where(corner, near[:, at : at + 1], own[:16, :])
        before = jnp.where(lane == start, 0.0, pltpu.roll(x[:16], 1, 1))
        after = jnp.where(lane == stop, 0.0, pltpu.roll(x[:16], LANES - 1, 1))
        around.append(x[16:] + own + before + after)
    for row, (u, nb) in enumerate(zip([near] + [x[:16] for x in side], around)):
        t = terms(u[:3], u[3:6], nb[:3], nb[3:6], u[6:7], u[7:8], u[8:9])
        for part in range(2):
            for c in range(PARTS):
                ring[part * PARTS + c, row : row + 1, : u.shape[1]] = t[part][c : c + 1]
        rho_ring[row : row + 1, : u.shape[1]] = u[6:7]
    for n in range(2 * PARTS):
        ring[n, 1:, LANES:] = jnp.zeros((7, cy - LANES), F32)
        ring[n, 3:, :LANES] = jnp.zeros((5, LANES), F32)
    rho_ring[1:, LANES:] = jnp.zeros((7, cy - LANES), F32)
    rho_ring[3:, :LANES] = jnp.zeros((5, LANES), F32)

    fill = jnp.zeros((LANES - 16, LANES), F32)
    columns = [jnp.transpose(jnp.concatenate([x[:16], fill], axis=0)) for x in side]
    lane = lax.broadcasted_iota(jnp.int32, (rows, cy), 1)
    row = lax.broadcasted_iota(jnp.int32, (rows, cy), 0)

    def neighbours(n):
        v = planes[n]
        total = jnp.where(lane == 0, columns[0][:rows, n : n + 1], pltpu.roll(v, 1, 1))
        total += jnp.where(lane == cy - 1, columns[1][:rows, n : n + 1], pltpu.roll(v, cy - 1, 1))
        edge = line[n : n + 1]
        total += jnp.where(row == 0, jnp.where(top, zero, edge), pltpu.roll(v, 1, 0))
        return total + jnp.where(row == rows - 1, jnp.where(top, edge, zero), pltpu.roll(v, rows - 1, 0))

    for c in range(PARTS):
        t = terms(planes[c], planes[PARTS + c], neighbours(c), neighbours(PARTS + c), *planes[6:])
        inner[c], inner[PARTS + c] = t


def sens_kernel(n_j, inner, ring, *refs):
    msgs, (field, sens) = refs[:n_j], refs[n_j:]
    rows = inner.shape[1]
    sens[...] = jnp.zeros_like(sens)
    for s, msg in enumerate(msgs):
        c = lax.rem(lax.axis_index("my") + n_j - s, n_j)

        @pl.when(c < PARTS)
        def _(msg=msg, c=c):
            planes = msg[...]
            if msg.dtype == BF16:
                scale = planes[2 * rows :].astype(F32)
                planes = decoded(planes, scale[3:4] + scale[4:5] + scale[5:6])
            re, im = planes[:rows], planes[rows : 2 * rows]
            field[c] = re
            field[PARTS + c] = im
            sens[:rows, :] -= re * inner[c] - im * inner[PARTS + c]
            re, im = planes[2 * rows : 2 * rows + 8], planes[2 * rows + 8 :]
            sens[rows:, :] -= re * ring[c] - im * ring[PARTS + c]


def filter_kernel(density, ring, *refs):
    parts, out = refs[:-1], refs[-1]
    rows, cy = density.shape
    total = parts[0][...]
    for part in parts[1:]:
        total = total + part[...]
    top = lax.axis_index("mx") == 0
    rho = density[...]
    inner, ring = rho * total[:rows], ring[...] * total[rows:]
    columns = jnp.transpose(jnp.concatenate([ring, jnp.zeros((LANES - 8, cy), F32)], axis=0)[:, :LANES])

    def across(v, before, after):
        lane = lax.broadcasted_iota(jnp.int32, v.shape, 1)
        before = jnp.where(lane == 0, before, pltpu.roll(v, 1, 1))
        after = jnp.where(lane == cy - 1, after, pltpu.roll(v, cy - 1, 1))
        return v + 0.5 * (before + after)

    mid = across(inner, columns[:rows, 1:2], columns[:rows, 2:3])
    corner = jnp.where(top, columns[rows : rows + 1], columns[LANES - 1 :])
    end = across(ring, corner[:, 1:2], corner[:, 2:3])[0:1]
    row = lax.broadcasted_iota(jnp.int32, mid.shape, 0)
    empty = jnp.zeros_like(end)
    above = jnp.where(row == 0, jnp.where(top, empty, end), pltpu.roll(mid, 1, 0))
    below = jnp.where(row == rows - 1, jnp.where(top, end, empty), pltpu.roll(mid, rows - 1, 0))
    out[...] = (mid + 0.5 * (above + below)) / (4.0 * rho)


def vmem():
    return pl.BlockSpec(memory_space=pltpu.VMEM)


def smem():
    return pl.BlockSpec(memory_space=pltpu.SMEM)


def shifts(n_j, source_limit, target_limit):
    return [
        [(a, (a + s) % n_j) for a in range(n_j) if a < source_limit and (a + s) % n_j < target_limit]
        for s in range(1, n_j)
    ]


def gathered(
    adjoint_rhs, state, density, stiffness, mass, omega, send_rows, recv_rows, mortar_weight
):
    rhs = adjoint_rhs.reshape(2 * PARTS, *density.shape)
    rows, cy = density.shape
    n_i, n_j = lax.axis_size("mx"), lax.axis_size("my")
    blocks = n_i * n_j
    slots = send_rows.shape[1]
    cap = slots // blocks
    up = [(a, a + 1) for a in range(n_j - 1)]
    edge = jax.ShapeDtypeStruct((32, LANES), F32)
    planes = (state.reshape(2 * PARTS, rows, cy), density, stiffness, mass)
    first, last, line = pl.pallas_call(
        edge_kernel,
        out_shape=[edge, edge, jax.ShapeDtypeStruct((32, cy), F32)],
        in_specs=[vmem()] * 4,
        out_specs=[vmem()] * 3,
        name="edges",
    )(*planes)
    west = lax.ppermute(last, "my", up)
    east = lax.ppermute(first, "my", [(b, a) for a, b in up])
    message = jax.ShapeDtypeStruct((4 * rows + 16, cy), BF16)
    own = pl.pallas_call(
        functools.partial(pack_kernel, n_j),
        out_shape=[message] * n_j,
        in_specs=[vmem()] * 7,
        out_specs=[vmem()] * n_j,
        scratch_shapes=[pltpu.VMEM((8, rows, LANES), F32)],
        name="pack",
    )(rhs, density, stiffness, mass, send_rows, recv_rows, mortar_weight)
    msgs = [own[0]]
    for s, pairs in enumerate(shifts(n_j, n_j, PARTS), 1):
        msgs.append(lax.ppermute(own[s], "my", pairs))
    msgs[1], first, last = lax.optimization_barrier((msgs[1], first, last))
    msgs[-1], west, east = lax.optimization_barrier((msgs[-1], west, east))
    msgs += [lax.ppermute(m, "mx", [(0, 1), (1, 0)]) for m in msgs]
    block = (blocks, rows, cy)
    outs = pl.pallas_call(
        functools.partial(sweep_kernel, n_i, n_j, cap),
        out_shape=[jax.ShapeDtypeStruct((2 * rows + 16, cy), BF16 if s else F32) for s in range(n_j)],
        in_specs=[smem()] + [vmem()] * blocks,
        out_specs=[vmem()] * n_j,
        scratch_shapes=[
            pltpu.VMEM((blocks, 2, rows, cy), F32),
            pltpu.VMEM((blocks, 2, rows, cy), F32),
            pltpu.VMEM((blocks, 2, rows, cy), F32),
            pltpu.VMEM(block, F32),
            pltpu.VMEM(block, F32),
            pltpu.VMEM(block, F32),
            pltpu.VMEM((blocks, 16, cy), F32),
            pltpu.VMEM((blocks, slots), F32),
            pltpu.VMEM((blocks, cy, slots), BF16),
            pltpu.VMEM((blocks, rows, slots), F32),
            pltpu.VMEM((blocks, rows, slots), BF16),
            pltpu.VMEM((blocks, slots, cy), BF16),
            pltpu.VMEM((blocks, blocks, slots), F32),
            pltpu.VMEM((2, blocks, slots), F32),
            pltpu.VMEM((8, rows, LANES), F32),
            pltpu.VMEM((2, rows, n_j * cy + 2 * LANES), F32),
            pltpu.VMEM((2, 8, n_j * cy + 2 * LANES), F32),
            pltpu.VMEM((8, cy), F32),
            pltpu.VMEM((16, cy), F32),
        ],
        compiler_params=pltpu.CompilerParams(vmem_limit_bytes=40 * 1024 * 1024),
        cost_estimate=pl.CostEstimate(flops=30_000_000_000, bytes_accessed=4_000_000, transcendentals=0),
        name="sweeps",
    )(omega, *msgs)
    parts = [outs[0]]
    for s, pairs in enumerate(shifts(n_j, PARTS, n_j), 1):
        parts.append(lax.ppermute(outs[s], "my", pairs))
    beyond = lax.ppermute(jnp.concatenate([line, west, east], axis=1), "mx", [(0, 1), (1, 0)])
    inner, ring, rho_ring = pl.pallas_call(
        response_kernel,
        out_shape=[
            jax.ShapeDtypeStruct((2 * PARTS, rows, cy), F32),
            jax.ShapeDtypeStruct((2 * PARTS, 8, cy), F32),
            jax.ShapeDtypeStruct((8, cy), F32),
        ],
        in_specs=[smem()] + [vmem()] * 9,
        out_specs=[vmem()] * 3,
        name="response",
    )(omega, *planes, first, last, west, east, beyond)
    field, sens = pl.pallas_call(
        functools.partial(sens_kernel, n_j),
        out_shape=[
            jax.ShapeDtypeStruct((2 * PARTS, rows, cy), F32),
            jax.ShapeDtypeStruct((rows + 8, cy), F32),
        ],
        in_specs=[vmem()] * (2 + n_j),
        out_specs=[vmem()] * 2,
        name="sensitivity",
    )(inner, ring, *parts)
    size = lax.axis_size("freq")
    all_freqs = [sens]
    for s in range(1, size):
        all_freqs.append(lax.ppermute(sens, "freq", [(a, (a + s) % size) for a in range(size)]))
    filtered = pl.pallas_call(
        filter_kernel,
        out_shape=jax.ShapeDtypeStruct((rows, cy), F32),
        in_specs=[vmem()] * (2 + size),
        out_specs=vmem(),
        name="filter",
    )(density, rho_ring, *all_freqs)
    return field.reshape(adjoint_rhs.shape), filtered


def solve_split(rhs, density, stiffness, mass, omega, send_rows, recv_rows, mortar_weight):
    rows_x, rows_y = density.shape
    cells = rows_x * rows_y
    w = omega[0]
    stiff = density**3 * stiffness
    rmass = density * mass
    sources = send_rows[0]
    targets = recv_rows[0]
    weights = mortar_weight[0]
    mdiag = jnp.zeros((cells,), jnp.float32).at[targets].add(weights).reshape(rows_x, rows_y)
    real_d = 4.4 * stiff + 0.3 + mdiag - w * w * rmass
    imag_d = 0.2 * w * (stiff + rmass)
    den = real_d * real_d + imag_d * imag_d

    def mortar(field):
        sent = field.reshape(6, cells)[:, sources]
        got = lax.all_to_all(sent, ("mx", "my"), split_axis=1, concat_axis=1, tiled=True)
        added = jnp.zeros((6, cells), jnp.float32).at[:, targets].add(got * weights)
        return added.reshape(6, rows_x, rows_y)

    def sweep(step, field):
        padded = extended(field, (("mx", 1), ("my", 2)), 1)
        beside = (
            padded[:, 2:, 1:-1] + padded[:, :-2, 1:-1] + padded[:, 1:-1, 2:] + padded[:, 1:-1, :-2]
        )
        h = rhs + stiff * beside + mortar(field)
        new_re = (h[:3] * real_d + h[3:] * imag_d) / den
        new_im = (h[3:] * real_d - h[:3] * imag_d) / den
        return jnp.concatenate([new_re, new_im], axis=0)

    return lax.fori_loop(0, ITERS, sweep, jnp.zeros((6, rows_x, rows_y), jnp.float32))


def distributed(
    adjoint_rhs, state, density, stiffness, mass, omega, send_rows, recv_rows, mortar_weight
):
    rows_x, rows_y = density.shape
    w = omega[0]
    dstiff = 3.0 * density**2 * stiffness
    rhs = adjoint_rhs.reshape(6, rows_x, rows_y)
    field = solve_split(rhs, density, stiffness, mass, omega, send_rows, recv_rows, mortar_weight)
    state_six = state.reshape(6, rows_x, rows_y)
    state_pad = extended(state_six, (("mx", 1), ("my", 2)), 1).astype(jnp.float32)
    u = state_six.astype(jnp.float32)
    nb = (
        state_pad[:, 2:, 1:-1]
        + state_pad[:, :-2, 1:-1]
        + state_pad[:, 1:-1, 2:]
        + state_pad[:, 1:-1, :-2]
    )
    da = 4.4 * dstiff - w * w * mass
    db = 0.2 * w * (dstiff + mass)
    t_re = da * u[:3] - db * u[3:] - dstiff * nb[:3]
    t_im = da * u[3:] + db * u[:3] - dstiff * nb[3:]
    sens = -jnp.sum(field[:3] * t_re - field[3:] * t_im, axis=0)
    size = lax.axis_size("freq")
    total = sens
    for s in range(1, size):
        total = total + lax.ppermute(sens, "freq", [(a, (a + s) % size) for a in range(size)])
    weighted = extended(density * total, (("mx", 0), ("my", 1)), 1)
    filt = weighted[1:-1, 1:-1]
    filt = filt + 0.5 * (
        weighted[2:, 1:-1] + weighted[:-2, 1:-1] + weighted[1:-1, 2:] + weighted[1:-1, :-2]
    )
    filt = filt + 0.25 * (
        weighted[2:, 2:] + weighted[:-2, :-2] + weighted[2:, :-2] + weighted[:-2, 2:]
    )
    return (field.reshape(1, 2, 3, rows_x, rows_y), filt / (4.0 * density))


def on_device(*args):
    rows, cy = args[2].shape
    n_i, n_j = lax.axis_size("mx"), lax.axis_size("my")
    fits = n_i == 2 and PARTS <= n_j <= 4 and rows == 64 and cy == 2 * LANES and args[6].shape[1] == cy
    return (gathered if fits else distributed)(*args)


def solution(mesh):
    return jax.shard_map(
        on_device,
        mesh=mesh,
        in_specs=(
            P("freq", None, None, "mx", "my"),
            P("freq", None, None, "mx", "my"),
            P("mx", "my"),
            P("mx", "my"),
            P("mx", "my"),
            P("freq"),
            P(("mx", "my"), None),
            P(("mx", "my"), None),
            P(("mx", "my"), None),
        ),
        out_specs=(P("freq", None, None, "mx", "my"), P("mx", "my")),
        check_vma=False,
    )
```

```python
import functools

import jax
import jax.numpy as jnp
from jax import lax
from jax.experimental import pallas as pl
from jax.experimental.pallas import tpu as pltpu
from jax.sharding import PartitionSpec as P

ITERS = 20
PARTS = 3
FINE = 2
LANES = 128
F32 = jnp.float32
BF16 = jnp.bfloat16


def extended(x, sides, width):
    for axis, dim in sides:
        size, length = (lax.axis_size(axis), x.shape[dim])
        up = [(i, (i + 1) % size) for i in range(size - 1)]
        down = [(j, i) for i, j in up]
        last = lax.slice_in_dim(x, length - width, length, axis=dim)
        first = lax.slice_in_dim(x, 0, width, axis=dim)
        before = lax.ppermute(last, axis, up)
        after = lax.ppermute(first, axis, down)
        x = jnp.concatenate([before, x, after], axis=dim)
    return x


def placed(cell, rows, cy):
    x, y = cell // cy, cell % cy
    tiles = rows // 8
    return (x % tiles) * 8 + x // tiles, (y % 2) * LANES + y // 2


def lane_order(cy, inverse):
    a = lax.broadcasted_iota(jnp.int32, (cy, cy), 0)
    b = lax.broadcasted_iota(jnp.int32, (cy, cy), 1)
    natural, kept = (b, a) if inverse else (a, b)
    return ((natural % 2) * LANES + natural // 2 == kept).astype(F32)


STIFF_SCALE, STIFF_POWER = 1.92, 96.0
MASS_SCALE, MASS_POWER = 1.0, 16.0
POWER, FLOOR, SHIFT = 30.0, 1.0 / 256.0, 4.0


def coded(v, most):
    size = jnp.exp2(POWER * (jnp.log2(jnp.abs(v) / most + FLOOR) + SHIFT))
    return jnp.where(v < 0.0, -size, size).astype(BF16)


def decoded(v, most):
    v = v.astype(F32)
    size = (jnp.exp2(jnp.log2(jnp.abs(v)) * (1.0 / POWER) - SHIFT) - FLOOR) * most
    return jnp.where(v < 0.0, -size, size)


def largest(*arrays):
    tops = [jnp.max(jnp.abs(v), axis=(0, 1), keepdims=True) for v in arrays]
    return jnp.maximum(functools.reduce(jnp.maximum, tops), 1e-30)


def raised(v, scale, power):
    return jnp.exp2(power * jnp.log2(v * (1.0 / scale))).astype(BF16)


def lowered(v, scale, power):
    return scale * jnp.exp2(jnp.log2(v.astype(F32)) * (1.0 / power))


def pieces(v):
    out = []
    for _ in range(3):
        out.append(v.astype(BF16).astype(F32))
        v = v - out[-1]
    return out


def permuted(v, order):
    return jnp.dot(v, order, precision=lax.Precision.HIGHEST, preferred_element_type=F32)


def planes_of(state, density, stiffness, mass):
    return [state[n].astype(F32) for n in range(2 * PARTS)] + [density[...], stiffness[...], mass[...]]


def edge_block(near, far):
    rows = near[: 2 * PARTS] + [x for v in near[2 * PARTS :] for x in pieces(v)]
    rows = rows + [jnp.zeros((1, LANES), F32)] * (16 - len(rows))
    inner = far[: 2 * PARTS] + [jnp.zeros((1, LANES), F32)] * (16 - 2 * PARTS)
    return jnp.concatenate([jnp.concatenate(rows, axis=0), jnp.concatenate(inner, axis=0)], axis=1)


def edge_rows(msg, present):
    block = msg[msg.shape[0] - 16 :, :].astype(F32)
    block = jnp.where(present, block, 0.0)
    near, far = block[:, :LANES], block[:, LANES:]
    n = 2 * PARTS
    exact = [near[n + 3 * p : n + 3 * p + 1] + near[n + 3 * p + 1 : n + 3 * p + 2] + near[n + 3 * p + 2 : n + 3 * p + 3] for p in range(3)]
    return jnp.concatenate([near[:n]] + exact + [jnp.zeros((7, LANES), F32), far], axis=0)


def pack_kernel(n_j, rhs, density, stiffness, mass, send, recv, weight, state, *outs):
    *outs, first, last, line, pages = outs
    rows, cy = density.shape
    tiles = rows // 8
    info = []
    for ref in (send, recv):
        row, column = placed(ref[...], rows, cy)
        info += [row.astype(F32), column.astype(F32)]
    info += pieces(weight[...])
    top = lax.axis_index("mx") == 0
    lane = lax.broadcasted_iota(jnp.int32, (1, LANES), 1)
    sides = [[[], []], [[], []]]
    for out in (first, last, line):
        out[...] = jnp.zeros_like(out)
    for n, v in enumerate(planes_of(state, density, stiffness, mass)):
        turned = jnp.transpose(jnp.concatenate([v[:, :LANES], v[:, cy - LANES :]], axis=0))
        late = pltpu.roll(turned[LANES - 8 :], rows, 1)
        for k in range(2):
            sides[0][k].append(jnp.where(lane < rows, turned[k : k + 1], 0.0))
            sides[1][k].append(jnp.where(lane < rows, late[7 - k : 8 - k], 0.0))
            line[pl.ds(16 * k + n, 1), :] = jnp.where(top, v[rows - 1 - k : rows - k], v[k : k + 1])
        first[pl.ds(n, 1), :] = sides[0][0][-1]
        last[pl.ds(n, 1), :] = sides[1][0][-1]
    edges = [edge_block(*side).astype(BF16) for side in sides]
    order = lane_order(cy, False)
    slot = 0

    def packed(value):
        nonlocal slot
        value = permuted(value, order)
        halves = []
        for u in range(cy // LANES):
            page = pages.at[slot % pages.shape[0]]
            slot += 1
            page[...] = value[:, u * LANES : (u + 1) * LANES]
            halves.append(jnp.concatenate([page[pl.ds(t, 8, stride=tiles), :] for t in range(tiles)], axis=0))
        return jnp.concatenate(halves, axis=1)

    rho = density[...]
    stiff = raised(packed(rho * rho * rho * stiffness[...]), STIFF_SCALE, STIFF_POWER)
    rmass = raised(packed(rho * mass[...]), MASS_SCALE, MASS_POWER)
    for s, out in enumerate(outs):
        c = jnp.minimum(lax.rem(lax.axis_index("my") + s, n_j), PARTS - 1)
        re, im = rhs[c], rhs[PARTS + c]
        most = largest(re, im)
        out[:rows, :] = coded(packed(re), most)
        out[rows : 2 * rows, :] = coded(packed(im), most)
        out[2 * rows : 3 * rows, :] = stiff
        out[3 * rows : 4 * rows, :] = rmass
        scale = [jnp.broadcast_to(x, (1, cy)) for x in pieces(most)]
        out[4 * rows : 4 * rows + 16, :] = jnp.concatenate(info + scale + [jnp.zeros((6, cy), F32)], axis=0).astype(BF16)
        beside = edges[1] if s == 1 else edges[0] if s == n_j - 1 else jnp.zeros((16, cy), BF16)
        out[4 * rows + 16 :, :] = beside


def split(v):
    high = v.astype(BF16)
    return high, (v - high.astype(F32)).astype(BF16)


def sweep_kernel(n_i, n_j, cap, omega, *refs):
    blocks = n_i * n_j
    msgs, refs = refs[: blocks], refs[blocks:]
    outs, refs = refs[:n_j], refs[n_j:]
    field_a, field_b, start, inverse, gain, lag, info, weights, pick, rowmask, spread, place, group, values, pages, plain, ends, rim, frame, mid, values_b = refs
    rows, cy = start.shape[2:]
    slots = blocks * cap
    me_i, me_j = lax.axis_index("mx"), lax.axis_index("my")
    w = omega[0]

    order = [(a, s) for a in range(n_i) for s in range(n_j)]
    index = [lax.rem(me_i + a, n_i) * n_j + lax.rem(me_j + n_j - s, n_j) for a, s in order]
    for msg, b in zip(msgs, index):
        info[b] = msg[4 * rows : 4 * rows + 16, :].astype(F32)
    chunk = lax.broadcasted_iota(jnp.int32, (blocks, slots), 1) // cap
    source = lax.broadcasted_iota(jnp.int32, (blocks, slots), 0)

    def one_hot(line, depth):
        at = lax.broadcasted_iota(jnp.int32, (depth, slots), 0)
        return (jnp.broadcast_to(line.astype(jnp.int32), at.shape) == at).astype(F32)

    for b in range(blocks):
        line = info[b]
        line = pltpu.roll(line, b * cap, 1) if b else line
        pick[b] = one_hot(line[1:2], cy).astype(BF16)
        rowmask[b] = one_hot(line[0:1], rows)
        row_out = one_hot(line[2:3], rows)
        spread[b] = row_out.astype(BF16)
        lane_out = jnp.transpose(one_hot(line[3:4], cy)).astype(BF16)
        place[b] = lane_out
        group[b] = (chunk == (source + b) % blocks).astype(F32)
        high, low = split(row_out * (line[4:5] + line[5:6] + line[6:7]))
        both = jnp.dot(jnp.concatenate([high, low], axis=0), lane_out, preferred_element_type=F32)
        gain[b] = both[:rows] + both[rows:]

    for msg, b in zip(msgs, index):
        rhs_re, rhs_im, k, m = [msg[n * rows : (n + 1) * rows, :] for n in range(4)]
        most = info[b][7:8] + info[b][8:9] + info[b][9:10]
        rhs_re, rhs_im = decoded(rhs_re, most), decoded(rhs_im, most)
        k, m = lowered(k, STIFF_SCALE, STIFF_POWER), lowered(m, MASS_SCALE, MASS_POWER)
        real_d = 4.4 * k + 0.3 + gain[b] - w * w * m
        imag_d = 0.2 * w * (k + m)
        scale = 1.0 / (real_d * real_d + imag_d * imag_d)
        g, l = real_d * scale, imag_d * scale
        first_re, first_im = rhs_re * g + rhs_im * l, rhs_im * g - rhs_re * l
        gain[b], lag[b], inverse[b] = k * g, k * l, 1.0 / k
        start[b, 0], start[b, 1] = first_re, first_im
        field_a[b, 0], field_a[b, 1] = first_re, first_im

    for b in range(blocks):
        line = info[b]
        line = pltpu.roll(line, b * cap, 1) if b else line
        lane_out = one_hot(line[3:4], cy).astype(BF16)
        found = jnp.dot(jnp.concatenate(split(inverse[b]), axis=0), lane_out, preferred_element_type=F32)
        found = (found[:rows] + found[rows:]) * one_hot(line[2:3], rows)
        found = jnp.sum(found, axis=0, keepdims=True)
        weights[pl.ds(b, 1), :] = (line[4:5] + line[5:6] + line[6:7]) * found

    row8 = lax.broadcasted_iota(jnp.int32, (8, LANES), 0)
    lane_r = lax.broadcasted_iota(jnp.int32, (rows, LANES), 1)
    zero = jnp.zeros((rows, LANES), F32)

    def gather(held, b, re, im, fine):
        whole = jnp.concatenate(re + im, axis=0)
        whole = jnp.concatenate(split(whole), axis=0) if fine else whole.astype(BF16)
        got = jnp.dot(whole, pick[b], preferred_element_type=F32)
        mask = rowmask[b]
        for part in range(2):
            mine = got[part * rows : (part + 1) * rows]
            if fine:
                mine += got[(part + 2) * rows : (part + 3) * rows]
            held[part, pl.ds(b, 1), :] = jnp.sum(mine * mask, axis=0, keepdims=True)

    def mortar_at(held, b, fine):
        arrived = [jnp.sum(held[part] * group[b], axis=0, keepdims=True) * weights[b : b + 1, :] for part in range(2)]
        left = []
        for r in range(0, rows, 16):
            for v in arrived:
                left += [spread[b, r : r + 16] * x for x in (split(v) if fine else [v.astype(BF16)])]
        mortar = jnp.dot(jnp.concatenate(left, axis=0), place[b], preferred_element_type=F32)
        each = 2 if fine else 1
        parts = []
        for r in range(rows // 16 * 2):
            part = mortar[r * each * 16 : r * each * 16 + 16]
            parts.append(part + mortar[r * each * 16 + 16 : r * each * 16 + 32] if fine else part)
        return parts

    def around_of(now, b, part, u):
        i, j = b // n_j, b % n_j
        lanes = slice(u * LANES, (u + 1) * LANES)
        others = slice((1 - u) * LANES, (2 - u) * LANES)
        own, other = now[b, part, :, lanes], now[b, part, :, others]
        if u == 0:
            edge = now[b - 1, part, :, others] if j > 0 else zero
            around = pltpu.roll(jnp.where(lane_r == LANES - 1, edge, other), 1, 1)
        else:
            edge = now[b + 1, part, :, others] if j < n_j - 1 else zero
            around = pltpu.roll(jnp.where(lane_r == 0, edge, other), LANES - 1, 1)
        around += other
        above = now[b - n_j, part, rows - 8 :, lanes] if i > 0 else zero[:8]
        below = now[b + n_j, part, :8, lanes] if i < n_i - 1 else zero[:8]
        top = pltpu.roll(jnp.where(row8 == 7, above, own[rows - 8 :]), 1, 0)
        bottom = pltpu.roll(jnp.where(row8 == 0, below, own[:8]), 7, 0)
        around += jnp.concatenate([top, own[:-8]], axis=0)
        return around + jnp.concatenate([own[8:], bottom], axis=0)

    def beside(now, b):
        for u in range(2):
            lanes = slice(u * LANES, (u + 1) * LANES)
            for part in range(2):
                mid[b, part, :, lanes] = around_of(now, b, part, u)

    def sweep(now, then, fine, fine_next):
        held, ahead = (values, values_b) if now is field_a else (values_b, values)

        def finish(b):
            mortar = mortar_at(held, b, fine)
            new = ([], [])
            for n in range(rows // 16):
                at = slice(n * 16, n * 16 + 16)
                re, im = mid[b, 0, at] + mortar[2 * n], mid[b, 1, at] + mortar[2 * n + 1]
                g, l = gain[b, at], lag[b, at]
                new[0].append(start[b, 0, at] + re * g + im * l)
                new[1].append(start[b, 1, at] + im * g - re * l)
                then[b, 0, at], then[b, 1, at] = new[0][-1], new[1][-1]
            if fine_next is not None:
                gather(ahead, b, *new, fine_next)

        for b in range(blocks):
            beside(now, b)
            finish(b)

    def pair(fine, step, carry):
        sweep(field_a, field_b, fine, fine)
        sweep(field_b, field_a, fine, fine)
        return carry

    fine_pairs = min(FINE, ITERS - 1) // 2
    pairs = (ITERS - 1) // 2
    for b in range(blocks):
        gather(values, b, [field_a[b, 0]], [field_a[b, 1]], False)
    lax.fori_loop(0, pairs - fine_pairs, functools.partial(pair, False), 0)
    lax.fori_loop(0, fine_pairs, functools.partial(pair, True), 0)
    last = field_a
    if (ITERS - 1) % 2:
        sweep(field_a, field_b, FINE > 0, None)
        last = field_b
    tiles = rows // 8
    back = lane_order(cy, True)
    around_mesh = jnp.zeros((rows, LANES), F32)
    for part in range(2):
        for at in (0, LANES + n_j * cy):
            plain[part, :, at : at + LANES] = around_mesh
            ends[part, :, at : at + LANES] = around_mesh[:8]
    end = jnp.where(me_i == 0, 0, rows - 1)
    rim[...] = jnp.zeros_like(rim)
    for j in range(n_j):
        for part in range(2):
            halves = []
            for u in range(2):
                page = pages.at[(j * 4 + part * 2 + u) % 8]
                lanes = slice(u * LANES, (u + 1) * LANES)
                for t in range(tiles):
                    page[pl.ds(t, 8, stride=tiles), :] = last[me_i * n_j + j, part, t * 8 : (t + 1) * 8, lanes]
                halves.append(page[...])
            plain[part, :, LANES + j * cy : LANES + (j + 1) * cy] = permuted(jnp.concatenate(halves, axis=1), back)
            rim[pl.ds(part * 4 + j, 1), :] = last[(1 - me_i) * n_j + j, part, pl.ds(end, 1), :]
    natural = permuted(rim[...], back)
    ends[:, :, LANES : LANES + n_j * cy] = jnp.zeros((2, 8, n_j * cy), F32)
    for j in range(n_j):
        for part in range(2):
            for at in (0, 7):
                ends[part, at : at + 1, LANES + j * cy : LANES + (j + 1) * cy] = natural[
                    part * 4 + j : part * 4 + j + 1
                ]
    for s, out in enumerate(outs):
        base = pl.multiple_of(LANES + (me_j ^ s) * cy, LANES)
        frame[...] = jnp.zeros_like(frame)
        block = [plain[part, :, pl.ds(base, cy)] for part in range(2)]
        for part in range(2):
            frame[pl.ds(part * 8, 1), :] = ends[part, 0:1, pl.ds(base, cy)]
            for k, (at, lane) in enumerate(((base - LANES, LANES - 1), (base + cy, 0)), 1):
                at = pl.multiple_of(at, LANES)
                beyond = [plain[part, :, pl.ds(at, LANES)], ends[part, :, pl.ds(at, LANES)]]
                beyond = beyond + [jnp.zeros((LANES - rows - 16, LANES), F32), beyond[1]]
                beyond = jnp.concatenate(beyond, axis=0)
                frame[pl.ds(part * 8 + k, 1), :LANES] = jnp.transpose(beyond)[lane : lane + 1]
        block.append(frame[...])
        if s:
            most = largest(*block)
            block = [coded(v, most) for v in block]
            row = lax.broadcasted_iota(jnp.int32, (16, cy), 0)
            for k, piece in enumerate(pieces(most)):
                block[2] = jnp.where(row == 3 + k, piece, block[2].astype(F32)).astype(BF16)
        for v, at in zip(block, (0, rows, 2 * rows)):
            out[at : at + v.shape[0], :] = v


def response_kernel(
    n_j, omega, state, density, stiffness, mass, first, last, line, west, east, *refs
):
    beyond_west, beyond_east, inner, ring, rho_ring = refs
    rows, cy = density.shape
    w = omega[0]
    top = lax.axis_index("mx") == 0
    present = (lax.axis_index("my") > 0, lax.axis_index("my") < n_j - 1)
    zero = jnp.zeros((1, cy), F32)

    def terms(u_re, u_im, nb_re, nb_im, rho, k, m):
        dstiff = 3.0 * rho * rho * k
        da = 4.4 * dstiff - w * w * m
        db = 0.2 * w * (dstiff + m)
        return da * u_re - db * u_im - dstiff * nb_re, da * u_im + db * u_re - dstiff * nb_im

    line = line[...]
    siblings = [edge_rows(m, p) for m, p in zip((beyond_west, beyond_east), present)]
    side = [edge_rows(m, p) + pltpu.roll(y, rows, 1) for m, p, y in zip((west, east), present, siblings)]
    lane = lax.broadcasted_iota(jnp.int32, (16, LANES), 1)
    start = jnp.where(top, 0, rows)
    stop = jnp.where(top, LANES - 1, rows - 1)
    corner = (lane == rows) | (lane == LANES - 1)
    around = []
    lane_cy = lax.broadcasted_iota(jnp.int32, (16, cy), 1)
    near = line[:16]
    touch = [jnp.where(top, y[:16, 0:1], y[:16, rows - 1 : rows]) for y in siblings]
    before = jnp.where(lane_cy == 0, touch[0], pltpu.roll(near, 1, 1))
    after = jnp.where(lane_cy == cy - 1, touch[1], pltpu.roll(near, cy - 1, 1))
    adjacent = []
    planes = planes_of(state, density, stiffness, mass)
    for v in planes:
        adjacent.append(jnp.where(top, v[rows - 1 :], v[:1]))
    adjacent = jnp.concatenate(adjacent + [zero] * 7, axis=0)
    around.append(line[16:] + adjacent + before + after)
    for x, own, at in ((side[0], first, 0), (side[1], last, cy - 1)):
        own = jnp.where(corner, near[:, at : at + 1], own[:16, :])
        before = jnp.where(lane == start, 0.0, pltpu.roll(x[:16], 1, 1))
        after = jnp.where(lane == stop, 0.0, pltpu.roll(x[:16], LANES - 1, 1))
        around.append(x[16:] + own + before + after)
    for row, (u, nb) in enumerate(zip([near] + [x[:16] for x in side], around)):
        t = terms(u[:3], u[3:6], nb[:3], nb[3:6], u[6:7], u[7:8], u[8:9])
        for part in range(2):
            for c in range(PARTS):
                ring[part * PARTS + c, row : row + 1, : u.shape[1]] = t[part][c : c + 1]
        rho_ring[row : row + 1, : u.shape[1]] = u[6:7]
    for n in range(2 * PARTS):
        ring[n, 1:, LANES:] = jnp.zeros((7, cy - LANES), F32)
        ring[n, 3:, :LANES] = jnp.zeros((5, LANES), F32)
    rho_ring[1:, LANES:] = jnp.zeros((7, cy - LANES), F32)
    rho_ring[3:, :LANES] = jnp.zeros((5, LANES), F32)

    fill = jnp.zeros((LANES - 16, LANES), F32)
    columns = [jnp.transpose(jnp.concatenate([x[:16], fill], axis=0)) for x in side]
    lane = lax.broadcasted_iota(jnp.int32, (rows, cy), 1)
    row = lax.broadcasted_iota(jnp.int32, (rows, cy), 0)

    def neighbours(n):
        v = planes[n]
        total = jnp.where(lane == 0, columns[0][:rows, n : n + 1], pltpu.roll(v, 1, 1))
        total += jnp.where(lane == cy - 1, columns[1][:rows, n : n + 1], pltpu.roll(v, cy - 1, 1))
        edge = line[n : n + 1]
        total += jnp.where(row == 0, jnp.where(top, zero, edge), pltpu.roll(v, 1, 0))
        return total + jnp.where(row == rows - 1, jnp.where(top, edge, zero), pltpu.roll(v, rows - 1, 0))

    for c in range(PARTS):
        t = terms(planes[c], planes[PARTS + c], neighbours(c), neighbours(PARTS + c), *planes[6:])
        inner[c], inner[PARTS + c] = t


def sens_kernel(inner, ring, *refs):
    *msgs, field, sens = refs
    rows = inner.shape[1]
    sens[...] = jnp.zeros_like(sens)
    for s, msg in enumerate(msgs):
        c = lax.axis_index("my") ^ s

        @pl.when(c < PARTS)
        def _(msg=msg, c=c):
            planes = msg[...]
            if msg.dtype == BF16:
                scale = planes[2 * rows :].astype(F32)
                planes = decoded(planes, scale[3:4] + scale[4:5] + scale[5:6])
            re, im = planes[:rows], planes[rows : 2 * rows]
            field[c] = re
            field[PARTS + c] = im
            sens[:rows, :] -= re * inner[c] - im * inner[PARTS + c]
            re, im = planes[2 * rows : 2 * rows + 8], planes[2 * rows + 8 :]
            sens[rows:, :] -= re * ring[c] - im * ring[PARTS + c]


def filter_kernel(density, ring, *refs):
    parts, out = refs[:-1], refs[-1]
    rows, cy = density.shape
    total = parts[0][...]
    for part in parts[1:]:
        total = total + part[...]
    top = lax.axis_index("mx") == 0
    rho = density[...]
    inner, ring = rho * total[:rows], ring[...] * total[rows:]
    columns = jnp.transpose(jnp.concatenate([ring, jnp.zeros((LANES - 8, cy), F32)], axis=0)[:, :LANES])

    def across(v, before, after):
        lane = lax.broadcasted_iota(jnp.int32, v.shape, 1)
        before = jnp.where(lane == 0, before, pltpu.roll(v, 1, 1))
        after = jnp.where(lane == cy - 1, after, pltpu.roll(v, cy - 1, 1))
        return v + 0.5 * (before + after)

    mid = across(inner, columns[:rows, 1:2], columns[:rows, 2:3])
    corner = jnp.where(top, columns[rows : rows + 1], columns[LANES - 1 :])
    end = across(ring, corner[:, 1:2], corner[:, 2:3])[0:1]
    row = lax.broadcasted_iota(jnp.int32, mid.shape, 0)
    empty = jnp.zeros_like(end)
    above = jnp.where(row == 0, jnp.where(top, empty, end), pltpu.roll(mid, 1, 0))
    below = jnp.where(row == rows - 1, jnp.where(top, end, empty), pltpu.roll(mid, rows - 1, 0))
    out[...] = (mid + 0.5 * (above + below)) / (4.0 * rho)


def vmem():
    return pl.BlockSpec(memory_space=pltpu.VMEM)


def smem():
    return pl.BlockSpec(memory_space=pltpu.SMEM)


def gathered(
    adjoint_rhs, state, density, stiffness, mass, omega, send_rows, recv_rows, mortar_weight
):
    rhs = adjoint_rhs.reshape(2 * PARTS, *density.shape)
    rows, cy = density.shape
    n_i, n_j = lax.axis_size("mx"), lax.axis_size("my")
    blocks = n_i * n_j
    slots = send_rows.shape[1]
    cap = slots // blocks
    planes = (state.reshape(2 * PARTS, rows, cy), density, stiffness, mass)
    edge = jax.ShapeDtypeStruct((16, LANES), F32)
    message = jax.ShapeDtypeStruct((4 * rows + 32, cy), BF16)
    *own, first, last, line = pl.pallas_call(
        functools.partial(pack_kernel, n_j),
        out_shape=[message] * n_j + [edge, edge, jax.ShapeDtypeStruct((32, cy), F32)],
        in_specs=[vmem()] * 8,
        out_specs=[vmem()] * (n_j + 3),
        scratch_shapes=[pltpu.VMEM((8, rows, LANES), F32)],
        name="pack",
    )(rhs, density, stiffness, mass, send_rows, recv_rows, mortar_weight, planes[0])
    msgs = [own[0]]
    for s in range(1, n_j):
        pairs = [(a, (a + s) % n_j) for a in range(n_j)]
        pairs = [(a, b) for a, b in pairs if b < PARTS or (s == 1 and b == PARTS)]
        msgs.append(lax.ppermute(own[s], "my", pairs))
    swap = [(0, 1), (1, 0)]
    msgs += [lax.ppermute(m, "mx", swap) for m in msgs]
    line = lax.ppermute(line, "mx", swap)
    block = (blocks, rows, cy)
    outs = pl.pallas_call(
        functools.partial(sweep_kernel, n_i, n_j, cap),
        out_shape=[jax.ShapeDtypeStruct((2 * rows + 16, cy), BF16 if s else F32) for s in range(n_j)],
        in_specs=[smem()] + [vmem()] * blocks,
        out_specs=[vmem()] * n_j,
        scratch_shapes=[
            pltpu.VMEM((blocks, 2, rows, cy), F32),
            pltpu.VMEM((blocks, 2, rows, cy), F32),
            pltpu.VMEM((blocks, 2, rows, cy), F32),
            pltpu.VMEM(block, F32),
            pltpu.VMEM(block, F32),
            pltpu.VMEM(block, F32),
            pltpu.VMEM((blocks, 16, cy), F32),
            pltpu.VMEM((blocks, slots), F32),
            pltpu.VMEM((blocks, cy, slots), BF16),
            pltpu.VMEM((blocks, rows, slots), F32),
            pltpu.VMEM((blocks, rows, slots), BF16),
            pltpu.VMEM((blocks, slots, cy), BF16),
            pltpu.VMEM((blocks, blocks, slots), F32),
            pltpu.VMEM((2, blocks, slots), F32),
            pltpu.VMEM((8, rows, LANES), F32),
            pltpu.VMEM((2, rows, n_j * cy + 2 * LANES), F32),
            pltpu.VMEM((2, 8, n_j * cy + 2 * LANES), F32),
            pltpu.VMEM((8, cy), F32),
            pltpu.VMEM((16, cy), F32),
            pltpu.VMEM((blocks, 2, rows, cy), F32),
            pltpu.VMEM((2, blocks, slots), F32),
        ],
        compiler_params=pltpu.CompilerParams(vmem_limit_bytes=40 * 1024 * 1024),
        cost_estimate=pl.CostEstimate(flops=30_000_000_000, bytes_accessed=4_000_000, transcendentals=0),
        name="sweeps",
    )(omega, *msgs)
    parts = {0: outs[0]}
    for s in (2, 3, 1):
        parts[s] = lax.ppermute(outs[s], "my", [(a, a ^ s) for a in range(PARTS)])
    parts = [parts[s] for s in range(n_j)]
    inner, ring, rho_ring = pl.pallas_call(
        functools.partial(response_kernel, n_j),
        out_shape=[
            jax.ShapeDtypeStruct((2 * PARTS, rows, cy), F32),
            jax.ShapeDtypeStruct((2 * PARTS, 8, cy), F32),
            jax.ShapeDtypeStruct((8, cy), F32),
        ],
        in_specs=[smem()] + [vmem()] * 11,
        out_specs=[vmem()] * 3,
        name="response",
    )(omega, *planes, first, last, line, msgs[1], msgs[n_j - 1], msgs[n_j + 1], msgs[2 * n_j - 1])
    field, sens = pl.pallas_call(
        sens_kernel,
        out_shape=[
            jax.ShapeDtypeStruct((2 * PARTS, rows, cy), F32),
            jax.ShapeDtypeStruct((rows + 8, cy), F32),
        ],
        in_specs=[vmem()] * (2 + n_j),
        out_specs=[vmem()] * 2,
        name="sensitivity",
    )(inner, ring, *parts)
    size = lax.axis_size("freq")
    all_freqs = [sens]
    for s in range(1, size):
        all_freqs.append(lax.ppermute(sens, "freq", [(a, (a + s) % size) for a in range(size)]))
    filtered = pl.pallas_call(
        filter_kernel,
        out_shape=jax.ShapeDtypeStruct((rows, cy), F32),
        in_specs=[vmem()] * (2 + size),
        out_specs=vmem(),
        name="filter",
    )(density, rho_ring, *all_freqs)
    return field.reshape(adjoint_rhs.shape), filtered


def solve_split(rhs, density, stiffness, mass, omega, send_rows, recv_rows, mortar_weight):
    rows_x, rows_y = density.shape
    cells = rows_x * rows_y
    w = omega[0]
    stiff = density**3 * stiffness
    rmass = density * mass
    sources = send_rows[0]
    targets = recv_rows[0]
    weights = mortar_weight[0]
    mdiag = jnp.zeros((cells,), jnp.float32).at[targets].add(weights).reshape(rows_x, rows_y)
    real_d = 4.4 * stiff + 0.3 + mdiag - w * w * rmass
    imag_d = 0.2 * w * (stiff + rmass)
    den = real_d * real_d + imag_d * imag_d

    def mortar(field):
        sent = field.reshape(6, cells)[:, sources]
        got = lax.all_to_all(sent, ("mx", "my"), split_axis=1, concat_axis=1, tiled=True)
        added = jnp.zeros((6, cells), jnp.float32).at[:, targets].add(got * weights)
        return added.reshape(6, rows_x, rows_y)

    def sweep(step, field):
        padded = extended(field, (("mx", 1), ("my", 2)), 1)
        beside = (
            padded[:, 2:, 1:-1] + padded[:, :-2, 1:-1] + padded[:, 1:-1, 2:] + padded[:, 1:-1, :-2]
        )
        h = rhs + stiff * beside + mortar(field)
        new_re = (h[:3] * real_d + h[3:] * imag_d) / den
        new_im = (h[3:] * real_d - h[:3] * imag_d) / den
        return jnp.concatenate([new_re, new_im], axis=0)

    return lax.fori_loop(0, ITERS, sweep, jnp.zeros((6, rows_x, rows_y), jnp.float32))


def distributed(
    adjoint_rhs, state, density, stiffness, mass, omega, send_rows, recv_rows, mortar_weight
):
    rows_x, rows_y = density.shape
    w = omega[0]
    dstiff = 3.0 * density**2 * stiffness
    rhs = adjoint_rhs.reshape(6, rows_x, rows_y)
    field = solve_split(rhs, density, stiffness, mass, omega, send_rows, recv_rows, mortar_weight)
    state_six = state.reshape(6, rows_x, rows_y)
    state_pad = extended(state_six, (("mx", 1), ("my", 2)), 1).astype(jnp.float32)
    u = state_six.astype(jnp.float32)
    nb = (
        state_pad[:, 2:, 1:-1]
        + state_pad[:, :-2, 1:-1]
        + state_pad[:, 1:-1, 2:]
        + state_pad[:, 1:-1, :-2]
    )
    da = 4.4 * dstiff - w * w * mass
    db = 0.2 * w * (dstiff + mass)
    t_re = da * u[:3] - db * u[3:] - dstiff * nb[:3]
    t_im = da * u[3:] + db * u[:3] - dstiff * nb[3:]
    sens = -jnp.sum(field[:3] * t_re - field[3:] * t_im, axis=0)
    size = lax.axis_size("freq")
    total = sens
    for s in range(1, size):
        total = total + lax.ppermute(sens, "freq", [(a, (a + s) % size) for a in range(size)])
    weighted = extended(density * total, (("mx", 0), ("my", 1)), 1)
    filt = weighted[1:-1, 1:-1]
    filt = filt + 0.5 * (
        weighted[2:, 1:-1] + weighted[:-2, 1:-1] + weighted[1:-1, 2:] + weighted[1:-1, :-2]
    )
    filt = filt + 0.25 * (
        weighted[2:, 2:] + weighted[:-2, :-2] + weighted[2:, :-2] + weighted[:-2, 2:]
    )
    return (field.reshape(1, 2, 3, rows_x, rows_y), filt / (4.0 * density))


def on_device(*args):
    rows, cy = args[2].shape
    n_i, n_j = lax.axis_size("mx"), lax.axis_size("my")
    fits = n_i == 2 and n_j == 4 and rows == 64 and cy == 2 * LANES and args[6].shape[1] == cy
    return (gathered if fits else distributed)(*args)


def solution(mesh):
    return jax.shard_map(
        on_device,
        mesh=mesh,
        in_specs=(
            P("freq", None, None, "mx", "my"),
            P("freq", None, None, "mx", "my"),
            P("mx", "my"),
            P("mx", "my"),
            P("mx", "my"),
            P("freq"),
            P(("mx", "my"), None),
            P(("mx", "my"), None),
            P(("mx", "my"), None),
        ),
        out_specs=(P("freq", None, None, "mx", "my"), P("mx", "my")),
        check_vma=False,
    )
```

```python
import functools

import jax
import jax.numpy as jnp
from jax import lax
from jax.experimental import pallas as pl
from jax.experimental.pallas import tpu as pltpu
from jax.sharding import PartitionSpec as P

ITERS = 20
PARTS = 3
FINE = 2
LANES = 128
F32 = jnp.float32
BF16 = jnp.bfloat16


def extended(x, sides, width):
    for axis, dim in sides:
        size, length = (lax.axis_size(axis), x.shape[dim])
        up = [(i, (i + 1) % size) for i in range(size - 1)]
        down = [(j, i) for i, j in up]
        last = lax.slice_in_dim(x, length - width, length, axis=dim)
        first = lax.slice_in_dim(x, 0, width, axis=dim)
        before = lax.ppermute(last, axis, up)
        after = lax.ppermute(first, axis, down)
        x = jnp.concatenate([before, x, after], axis=dim)
    return x


def placed(cell, rows, cy):
    x, y = cell // cy, cell % cy
    tiles = rows // 8
    return (x % tiles) * 8 + x // tiles, (y % 2) * LANES + y // 2


def lane_order(cy, inverse):
    a = lax.broadcasted_iota(jnp.int32, (cy, cy), 0)
    b = lax.broadcasted_iota(jnp.int32, (cy, cy), 1)
    natural, kept = (b, a) if inverse else (a, b)
    return ((natural % 2) * LANES + natural // 2 == kept).astype(F32).astype(BF16)


STIFF_SCALE, STIFF_POWER = 1.92, 96.0
MASS_SCALE, MASS_POWER = 1.0, 16.0
POWER, FLOOR, SHIFT = 30.0, 1.0 / 256.0, 4.0


def coded(v, most):
    size = jnp.exp2(POWER * (jnp.log2(jnp.abs(v) / most + FLOOR) + SHIFT))
    return jnp.where(v < 0.0, -size, size).astype(BF16)


def decoded(v, most):
    v = v.astype(F32)
    size = (jnp.exp2(jnp.log2(jnp.abs(v)) * (1.0 / POWER) - SHIFT) - FLOOR) * most
    return jnp.where(v < 0.0, -size, size)


def largest(*arrays):
    tops = [jnp.max(jnp.abs(v), axis=(0, 1), keepdims=True) for v in arrays]
    return jnp.maximum(functools.reduce(jnp.maximum, tops), 1e-30)


def raised(v, scale, power):
    return jnp.exp2(power * jnp.log2(v * (1.0 / scale))).astype(BF16)


def lowered(v, scale, power):
    return scale * jnp.exp2(jnp.log2(v.astype(F32)) * (1.0 / power))


def pieces(v):
    out = []
    for _ in range(3):
        out.append(v.astype(BF16).astype(F32))
        v = v - out[-1]
    return out


def split(v):
    high = v.astype(BF16)
    return high, (v - high.astype(F32)).astype(BF16)


def permuted(v, order):
    n = v.shape[0]
    moved = jnp.dot(jnp.concatenate(split(v), axis=0), order, preferred_element_type=F32)
    return moved[:n] + moved[n:]


def planes_of(state, density, stiffness, mass):
    return [state[n].astype(F32) for n in range(2 * PARTS)] + [density[...], stiffness[...], mass[...]]


def edge_block(near, far):
    rows = near[: 2 * PARTS] + [x for v in near[2 * PARTS :] for x in pieces(v)]
    rows = rows + [jnp.zeros((1, LANES), F32)] * (16 - len(rows))
    inner = far[: 2 * PARTS] + [jnp.zeros((1, LANES), F32)] * (16 - 2 * PARTS)
    return jnp.concatenate([jnp.concatenate(rows, axis=0), jnp.concatenate(inner, axis=0)], axis=1)


def edge_rows(msg, present):
    block = msg[msg.shape[0] - 16 :, :].astype(F32)
    block = jnp.where(present, block, 0.0)
    near, far = block[:, :LANES], block[:, LANES:]
    n = 2 * PARTS
    exact = [near[n + 3 * p : n + 3 * p + 1] + near[n + 3 * p + 1 : n + 3 * p + 2] + near[n + 3 * p + 2 : n + 3 * p + 3] for p in range(3)]
    return jnp.concatenate([near[:n]] + exact + [jnp.zeros((7, LANES), F32), far], axis=0)


def pack_kernel(n_j, rhs, density, stiffness, mass, send, recv, weight, state, *outs):
    *outs, first, last, line, pages = outs
    rows, cy = density.shape
    tiles = rows // 8
    info = []
    for ref in (send, recv):
        row, column = placed(ref[...], rows, cy)
        info += [row.astype(F32), column.astype(F32)]
    info += pieces(weight[...])
    top = lax.axis_index("mx") == 0
    lane = lax.broadcasted_iota(jnp.int32, (1, LANES), 1)
    sides = [[[], []], [[], []]]
    for out in (first, last, line):
        out[...] = jnp.zeros_like(out)
    for n, v in enumerate(planes_of(state, density, stiffness, mass)):
        turned = jnp.transpose(jnp.concatenate([v[:, :LANES], v[:, cy - LANES :]], axis=0))
        late = pltpu.roll(turned[LANES - 8 :], rows, 1)
        for k in range(2):
            sides[0][k].append(jnp.where(lane < rows, turned[k : k + 1], 0.0))
            sides[1][k].append(jnp.where(lane < rows, late[7 - k : 8 - k], 0.0))
            line[pl.ds(16 * k + n, 1), :] = jnp.where(top, v[rows - 1 - k : rows - k], v[k : k + 1])
        first[pl.ds(n, 1), :] = sides[0][0][-1]
        last[pl.ds(n, 1), :] = sides[1][0][-1]
    edges = [edge_block(*side).astype(BF16) for side in sides]
    order = lane_order(cy, False)
    slot = 0

    def packed(value):
        nonlocal slot
        value = permuted(value, order)
        halves = []
        for u in range(cy // LANES):
            page = pages.at[slot % pages.shape[0]]
            slot += 1
            page[...] = value[:, u * LANES : (u + 1) * LANES]
            halves.append(jnp.concatenate([page[pl.ds(t, 8, stride=tiles), :] for t in range(tiles)], axis=0))
        return jnp.concatenate(halves, axis=1)

    rho = density[...]
    stiff = raised(packed(rho * rho * rho * stiffness[...]), STIFF_SCALE, STIFF_POWER)
    rmass = raised(packed(rho * mass[...]), MASS_SCALE, MASS_POWER)
    for s, out in enumerate(outs):
        c = jnp.minimum(lax.rem(lax.axis_index("my") + s, n_j), PARTS - 1)
        re, im = rhs[c], rhs[PARTS + c]
        most = largest(re, im)
        out[:rows, :] = coded(packed(re), most)
        out[rows : 2 * rows, :] = coded(packed(im), most)
        out[2 * rows : 3 * rows, :] = stiff
        out[3 * rows : 4 * rows, :] = rmass
        scale = [jnp.broadcast_to(x, (1, cy)) for x in pieces(most)]
        out[4 * rows : 4 * rows + 16, :] = jnp.concatenate(info + scale + [jnp.zeros((6, cy), F32)], axis=0).astype(BF16)
        beside = edges[1] if s == 1 else edges[0] if s == n_j - 1 else jnp.zeros((16, cy), BF16)
        out[4 * rows + 16 :, :] = beside


def sweep_kernel(n_i, n_j, cap, omega, *refs):
    blocks = n_i * n_j
    msgs, refs = refs[: blocks], refs[blocks:]
    outs, refs = refs[:n_j], refs[n_j:]
    field_a, field_b, start, inverse, gain, lag, info, weights, pick, rowmask, spread, place, group, values, pages, plain, ends, rim, frame, mid, values_b = refs
    rows, cy = start.shape[2:]
    slots = blocks * cap
    me_i, me_j = lax.axis_index("mx"), lax.axis_index("my")
    w = omega[0]

    order = [(a, s) for a in range(n_i) for s in range(n_j)]
    index = [lax.rem(me_i + a, n_i) * n_j + lax.rem(me_j + n_j - s, n_j) for a, s in order]
    for msg, b in zip(msgs, index):
        info[b] = msg[4 * rows : 4 * rows + 16, :].astype(F32)
    chunk = lax.broadcasted_iota(jnp.int32, (blocks, slots), 1) // cap
    source = lax.broadcasted_iota(jnp.int32, (blocks, slots), 0)

    def one_hot(line, depth):
        at = lax.broadcasted_iota(jnp.int32, (depth, slots), 0)
        return (jnp.broadcast_to(line.astype(jnp.int32), at.shape) == at).astype(F32)

    for b in range(blocks):
        line = info[b]
        line = pltpu.roll(line, b * cap, 1) if b else line
        pick[b] = one_hot(line[1:2], cy).astype(BF16)
        rowmask[b] = one_hot(line[0:1], rows)
        row_out = one_hot(line[2:3], rows)
        spread[b] = row_out.astype(BF16)
        lane_out = jnp.transpose(one_hot(line[3:4], cy)).astype(BF16)
        place[b] = lane_out
        group[b] = (chunk == (source + b) % blocks).astype(F32)
        high, low = split(row_out * (line[4:5] + line[5:6] + line[6:7]))
        both = jnp.dot(jnp.concatenate([high, low], axis=0), lane_out, preferred_element_type=F32)
        gain[b] = both[:rows] + both[rows:]

    for msg, b in zip(msgs, index):
        rhs_re, rhs_im, k, m = [msg[n * rows : (n + 1) * rows, :] for n in range(4)]
        most = info[b][7:8] + info[b][8:9] + info[b][9:10]
        rhs_re, rhs_im = decoded(rhs_re, most), decoded(rhs_im, most)
        k, m = lowered(k, STIFF_SCALE, STIFF_POWER), lowered(m, MASS_SCALE, MASS_POWER)
        real_d = 4.4 * k + 0.3 + gain[b] - w * w * m
        imag_d = 0.2 * w * (k + m)
        scale = 1.0 / (real_d * real_d + imag_d * imag_d)
        g, l = real_d * scale, imag_d * scale
        first_re, first_im = rhs_re * g + rhs_im * l, rhs_im * g - rhs_re * l
        gain[b], lag[b], inverse[b] = k * g, k * l, 1.0 / k
        start[b, 0], start[b, 1] = first_re, first_im
        field_a[b, 0], field_a[b, 1] = first_re, first_im

    for b in range(blocks):
        line = info[b]
        line = pltpu.roll(line, b * cap, 1) if b else line
        lane_out = one_hot(line[3:4], cy).astype(BF16)
        found = jnp.dot(jnp.concatenate(split(inverse[b]), axis=0), lane_out, preferred_element_type=F32)
        found = (found[:rows] + found[rows:]) * one_hot(line[2:3], rows)
        found = jnp.sum(found, axis=0, keepdims=True)
        weights[pl.ds(b, 1), :] = (line[4:5] + line[5:6] + line[6:7]) * found

    row8 = lax.broadcasted_iota(jnp.int32, (8, LANES), 0)
    lane_r = lax.broadcasted_iota(jnp.int32, (rows, LANES), 1)
    zero = jnp.zeros((rows, LANES), F32)

    def gather(held, b, re, im, fine):
        whole = jnp.concatenate(re + im, axis=0)
        whole = jnp.concatenate(split(whole), axis=0) if fine else whole.astype(BF16)
        got = jnp.dot(whole, pick[b], preferred_element_type=F32)
        mask = rowmask[b]
        for part in range(2):
            mine = got[part * rows : (part + 1) * rows]
            if fine:
                mine += got[(part + 2) * rows : (part + 3) * rows]
            held[part, pl.ds(b, 1), :] = jnp.sum(mine * mask, axis=0, keepdims=True)

    def mortar_at(held, b, fine):
        arrived = [jnp.sum(held[part] * group[b], axis=0, keepdims=True) * weights[b : b + 1, :] for part in range(2)]
        left = []
        for r in range(0, rows, 16):
            for v in arrived:
                left += [spread[b, r : r + 16] * x for x in (split(v) if fine else [v.astype(BF16)])]
        mortar = jnp.dot(jnp.concatenate(left, axis=0), place[b], preferred_element_type=F32)
        each = 2 if fine else 1
        parts = []
        for r in range(rows // 16 * 2):
            part = mortar[r * each * 16 : r * each * 16 + 16]
            parts.append(part + mortar[r * each * 16 + 16 : r * each * 16 + 32] if fine else part)
        return parts

    def around_of(now, b, part, u):
        i, j = b // n_j, b % n_j
        lanes = slice(u * LANES, (u + 1) * LANES)
        others = slice((1 - u) * LANES, (2 - u) * LANES)
        own, other = now[b, part, :, lanes], now[b, part, :, others]
        if u == 0:
            edge = now[b - 1, part, :, others] if j > 0 else zero
            around = pltpu.roll(jnp.where(lane_r == LANES - 1, edge, other), 1, 1)
        else:
            edge = now[b + 1, part, :, others] if j < n_j - 1 else zero
            around = pltpu.roll(jnp.where(lane_r == 0, edge, other), LANES - 1, 1)
        around += other
        above = now[b - n_j, part, rows - 8 :, lanes] if i > 0 else zero[:8]
        below = now[b + n_j, part, :8, lanes] if i < n_i - 1 else zero[:8]
        top = pltpu.roll(jnp.where(row8 == 7, above, own[rows - 8 :]), 1, 0)
        bottom = pltpu.roll(jnp.where(row8 == 0, below, own[:8]), 7, 0)
        around += jnp.concatenate([top, own[:-8]], axis=0)
        return around + jnp.concatenate([own[8:], bottom], axis=0)

    def beside(now, b):
        for u in range(2):
            lanes = slice(u * LANES, (u + 1) * LANES)
            for part in range(2):
                mid[b, part, :, lanes] = around_of(now, b, part, u)

    def sweep(now, then, fine, fine_next):
        held, ahead = (values, values_b) if now is field_a else (values_b, values)

        def finish(b):
            mortar = mortar_at(held, b, fine)
            new = ([], [])
            for n in range(rows // 16):
                at = slice(n * 16, n * 16 + 16)
                re, im = mid[b, 0, at] + mortar[2 * n], mid[b, 1, at] + mortar[2 * n + 1]
                g, l = gain[b, at], lag[b, at]
                new[0].append(start[b, 0, at] + re * g + im * l)
                new[1].append(start[b, 1, at] + im * g - re * l)
                then[b, 0, at], then[b, 1, at] = new[0][-1], new[1][-1]
            if fine_next is not None:
                gather(ahead, b, *new, fine_next)

        for b in range(blocks):
            beside(now, b)
            finish(b)

    def pair(fine, step, carry):
        sweep(field_a, field_b, fine, fine)
        sweep(field_b, field_a, fine, fine)
        return carry

    fine_pairs = min(FINE, ITERS - 1) // 2
    pairs = (ITERS - 1) // 2
    for b in range(blocks):
        gather(values, b, [field_a[b, 0]], [field_a[b, 1]], False)
    lax.fori_loop(0, pairs - fine_pairs, functools.partial(pair, False), 0)
    lax.fori_loop(0, fine_pairs, functools.partial(pair, True), 0)
    last = field_a
    if (ITERS - 1) % 2:
        sweep(field_a, field_b, FINE > 0, None)
        last = field_b
    tiles = rows // 8
    back = lane_order(cy, True)
    around_mesh = jnp.zeros((rows, LANES), F32)
    for part in range(2):
        for at in (0, LANES + n_j * cy):
            plain[part, :, at : at + LANES] = around_mesh
            ends[part, :, at : at + LANES] = around_mesh[:8]
    end = jnp.where(me_i == 0, 0, rows - 1)
    rim[...] = jnp.zeros_like(rim)
    for j in range(n_j):
        for part in range(2):
            halves = []
            for u in range(2):
                page = pages.at[(j * 4 + part * 2 + u) % 8]
                lanes = slice(u * LANES, (u + 1) * LANES)
                for t in range(tiles):
                    page[pl.ds(t, 8, stride=tiles), :] = last[me_i * n_j + j, part, t * 8 : (t + 1) * 8, lanes]
                halves.append(page[...])
            plain[part, :, LANES + j * cy : LANES + (j + 1) * cy] = permuted(jnp.concatenate(halves, axis=1), back)
            rim[pl.ds(part * 4 + j, 1), :] = last[(1 - me_i) * n_j + j, part, pl.ds(end, 1), :]
    natural = permuted(rim[...], back)
    ends[:, :, LANES : LANES + n_j * cy] = jnp.zeros((2, 8, n_j * cy), F32)
    for j in range(n_j):
        for part in range(2):
            for at in (0, 7):
                ends[part, at : at + 1, LANES + j * cy : LANES + (j + 1) * cy] = natural[
                    part * 4 + j : part * 4 + j + 1
                ]
    for s, out in enumerate(outs):
        base = pl.multiple_of(LANES + (me_j ^ s) * cy, LANES)
        frame[...] = jnp.zeros_like(frame)
        block = [plain[part, :, pl.ds(base, cy)] for part in range(2)]
        for part in range(2):
            frame[pl.ds(part * 8, 1), :] = ends[part, 0:1, pl.ds(base, cy)]
            for k, (at, lane) in enumerate(((base - LANES, LANES - 1), (base + cy, 0)), 1):
                at = pl.multiple_of(at, LANES)
                beyond = [plain[part, :, pl.ds(at, LANES)], ends[part, :, pl.ds(at, LANES)]]
                beyond = beyond + [jnp.zeros((LANES - rows - 16, LANES), F32), beyond[1]]
                beyond = jnp.concatenate(beyond, axis=0)
                frame[pl.ds(part * 8 + k, 1), :LANES] = jnp.transpose(beyond)[lane : lane + 1]
        block.append(frame[...])
        if s:
            most = largest(*block)
            block = [coded(v, most) for v in block]
            row = lax.broadcasted_iota(jnp.int32, (16, cy), 0)
            for k, piece in enumerate(pieces(most)):
                block[2] = jnp.where(row == 3 + k, piece, block[2].astype(F32)).astype(BF16)
        for v, at in zip(block, (0, rows, 2 * rows)):
            out[at : at + v.shape[0], :] = v


def response_kernel(
    n_j, omega, state, density, stiffness, mass, first, last, line, west, east, *refs
):
    beyond_west, beyond_east, inner, ring, rho_ring = refs
    rows, cy = density.shape
    w = omega[0]
    top = lax.axis_index("mx") == 0
    present = (lax.axis_index("my") > 0, lax.axis_index("my") < n_j - 1)
    zero = jnp.zeros((1, cy), F32)

    def terms(u_re, u_im, nb_re, nb_im, rho, k, m):
        dstiff = 3.0 * rho * rho * k
        da = 4.4 * dstiff - w * w * m
        db = 0.2 * w * (dstiff + m)
        return da * u_re - db * u_im - dstiff * nb_re, da * u_im + db * u_re - dstiff * nb_im

    line = line[...]
    siblings = [edge_rows(m, p) for m, p in zip((beyond_west, beyond_east), present)]
    side = [edge_rows(m, p) + pltpu.roll(y, rows, 1) for m, p, y in zip((west, east), present, siblings)]
    lane = lax.broadcasted_iota(jnp.int32, (16, LANES), 1)
    start = jnp.where(top, 0, rows)
    stop = jnp.where(top, LANES - 1, rows - 1)
    corner = (lane == rows) | (lane == LANES - 1)
    around = []
    lane_cy = lax.broadcasted_iota(jnp.int32, (16, cy), 1)
    near = line[:16]
    touch = [jnp.where(top, y[:16, 0:1], y[:16, rows - 1 : rows]) for y in siblings]
    before = jnp.where(lane_cy == 0, touch[0], pltpu.roll(near, 1, 1))
    after = jnp.where(lane_cy == cy - 1, touch[1], pltpu.roll(near, cy - 1, 1))
    adjacent = []
    planes = planes_of(state, density, stiffness, mass)
    for v in planes:
        adjacent.append(jnp.where(top, v[rows - 1 :], v[:1]))
    adjacent = jnp.concatenate(adjacent + [zero] * 7, axis=0)
    around.append(line[16:] + adjacent + before + after)
    for x, own, at in ((side[0], first, 0), (side[1], last, cy - 1)):
        own = jnp.where(corner, near[:, at : at + 1], own[:16, :])
        before = jnp.where(lane == start, 0.0, pltpu.roll(x[:16], 1, 1))
        after = jnp.where(lane == stop, 0.0, pltpu.roll(x[:16], LANES - 1, 1))
        around.append(x[16:] + own + before + after)
    for row, (u, nb) in enumerate(zip([near] + [x[:16] for x in side], around)):
        t = terms(u[:3], u[3:6], nb[:3], nb[3:6], u[6:7], u[7:8], u[8:9])
        for part in range(2):
            for c in range(PARTS):
                ring[part * PARTS + c, row : row + 1, : u.shape[1]] = t[part][c : c + 1]
        rho_ring[row : row + 1, : u.shape[1]] = u[6:7]
    for n in range(2 * PARTS):
        ring[n, 1:, LANES:] = jnp.zeros((7, cy - LANES), F32)
        ring[n, 3:, :LANES] = jnp.zeros((5, LANES), F32)
    rho_ring[1:, LANES:] = jnp.zeros((7, cy - LANES), F32)
    rho_ring[3:, :LANES] = jnp.zeros((5, LANES), F32)

    fill = jnp.zeros((LANES - 16, LANES), F32)
    columns = [jnp.transpose(jnp.concatenate([x[:16], fill], axis=0)) for x in side]
    lane = lax.broadcasted_iota(jnp.int32, (rows, cy), 1)
    row = lax.broadcasted_iota(jnp.int32, (rows, cy), 0)

    def neighbours(n):
        v = planes[n]
        total = jnp.where(lane == 0, columns[0][:rows, n : n + 1], pltpu.roll(v, 1, 1))
        total += jnp.where(lane == cy - 1, columns[1][:rows, n : n + 1], pltpu.roll(v, cy - 1, 1))
        edge = line[n : n + 1]
        total += jnp.where(row == 0, jnp.where(top, zero, edge), pltpu.roll(v, 1, 0))
        return total + jnp.where(row == rows - 1, jnp.where(top, edge, zero), pltpu.roll(v, rows - 1, 0))

    for c in range(PARTS):
        t = terms(planes[c], planes[PARTS + c], neighbours(c), neighbours(PARTS + c), *planes[6:])
        inner[c], inner[PARTS + c] = t


def sens_kernel(inner, ring, *refs):
    *msgs, field, sens = refs
    rows = inner.shape[1]
    sens[...] = jnp.zeros_like(sens)
    for s, msg in enumerate(msgs):
        c = lax.axis_index("my") ^ s

        @pl.when(c < PARTS)
        def _(msg=msg, c=c):
            planes = msg[...]
            if msg.dtype == BF16:
                scale = planes[2 * rows :].astype(F32)
                planes = decoded(planes, scale[3:4] + scale[4:5] + scale[5:6])
            re, im = planes[:rows], planes[rows : 2 * rows]
            field[c] = re
            field[PARTS + c] = im
            sens[:rows, :] -= re * inner[c] - im * inner[PARTS + c]
            re, im = planes[2 * rows : 2 * rows + 8], planes[2 * rows + 8 :]
            sens[rows:, :] -= re * ring[c] - im * ring[PARTS + c]


def filter_kernel(density, ring, *refs):
    parts, out = refs[:-1], refs[-1]
    rows, cy = density.shape
    total = parts[0][...]
    for part in parts[1:]:
        total = total + part[...]
    top = lax.axis_index("mx") == 0
    rho = density[...]
    inner, ring = rho * total[:rows], ring[...] * total[rows:]
    columns = jnp.transpose(jnp.concatenate([ring, jnp.zeros((LANES - 8, cy), F32)], axis=0)[:, :LANES])

    def across(v, before, after):
        lane = lax.broadcasted_iota(jnp.int32, v.shape, 1)
        before = jnp.where(lane == 0, before, pltpu.roll(v, 1, 1))
        after = jnp.where(lane == cy - 1, after, pltpu.roll(v, cy - 1, 1))
        return v + 0.5 * (before + after)

    mid = across(inner, columns[:rows, 1:2], columns[:rows, 2:3])
    corner = jnp.where(top, columns[rows : rows + 1], columns[LANES - 1 :])
    end = across(ring, corner[:, 1:2], corner[:, 2:3])[0:1]
    row = lax.broadcasted_iota(jnp.int32, mid.shape, 0)
    empty = jnp.zeros_like(end)
    above = jnp.where(row == 0, jnp.where(top, empty, end), pltpu.roll(mid, 1, 0))
    below = jnp.where(row == rows - 1, jnp.where(top, end, empty), pltpu.roll(mid, rows - 1, 0))
    out[...] = (mid + 0.5 * (above + below)) / (4.0 * rho)


def vmem():
    return pl.BlockSpec(memory_space=pltpu.VMEM)


def smem():
    return pl.BlockSpec(memory_space=pltpu.SMEM)


def gathered(
    adjoint_rhs, state, density, stiffness, mass, omega, send_rows, recv_rows, mortar_weight
):
    rhs = adjoint_rhs.reshape(2 * PARTS, *density.shape)
    rows, cy = density.shape
    n_i, n_j = lax.axis_size("mx"), lax.axis_size("my")
    blocks = n_i * n_j
    slots = send_rows.shape[1]
    cap = slots // blocks
    planes = (state.reshape(2 * PARTS, rows, cy), density, stiffness, mass)
    edge = jax.ShapeDtypeStruct((16, LANES), F32)
    message = jax.ShapeDtypeStruct((4 * rows + 32, cy), BF16)
    *own, first, last, line = pl.pallas_call(
        functools.partial(pack_kernel, n_j),
        out_shape=[message] * n_j + [edge, edge, jax.ShapeDtypeStruct((32, cy), F32)],
        in_specs=[vmem()] * 8,
        out_specs=[vmem()] * (n_j + 3),
        scratch_shapes=[pltpu.VMEM((8, rows, LANES), F32)],
        name="pack",
    )(rhs, density, stiffness, mass, send_rows, recv_rows, mortar_weight, planes[0])
    msgs = [own[0]]
    for s in range(1, n_j):
        pairs = [(a, (a + s) % n_j) for a in range(n_j)]
        pairs = [(a, b) for a, b in pairs if b < PARTS or (s == 1 and b == PARTS)]
        msgs.append(lax.ppermute(own[s], "my", pairs))
    swap = [(0, 1), (1, 0)]
    msgs += [lax.ppermute(m, "mx", swap) for m in msgs]
    line = lax.ppermute(line, "mx", swap)
    block = (blocks, rows, cy)
    outs = pl.pallas_call(
        functools.partial(sweep_kernel, n_i, n_j, cap),
        out_shape=[jax.ShapeDtypeStruct((2 * rows + 16, cy), BF16 if s else F32) for s in range(n_j)],
        in_specs=[smem()] + [vmem()] * blocks,
        out_specs=[vmem()] * n_j,
        scratch_shapes=[
            pltpu.VMEM((blocks, 2, rows, cy), F32),
            pltpu.VMEM((blocks, 2, rows, cy), F32),
            pltpu.VMEM((blocks, 2, rows, cy), F32),
            pltpu.VMEM(block, F32),
            pltpu.VMEM(block, F32),
            pltpu.VMEM(block, F32),
            pltpu.VMEM((blocks, 16, cy), F32),
            pltpu.VMEM((blocks, slots), F32),
            pltpu.VMEM((blocks, cy, slots), BF16),
            pltpu.VMEM((blocks, rows, slots), F32),
            pltpu.VMEM((blocks, rows, slots), BF16),
            pltpu.VMEM((blocks, slots, cy), BF16),
            pltpu.VMEM((blocks, blocks, slots), F32),
            pltpu.VMEM((2, blocks, slots), F32),
            pltpu.VMEM((8, rows, LANES), F32),
            pltpu.VMEM((2, rows, n_j * cy + 2 * LANES), F32),
            pltpu.VMEM((2, 8, n_j * cy + 2 * LANES), F32),
            pltpu.VMEM((8, cy), F32),
            pltpu.VMEM((16, cy), F32),
            pltpu.VMEM((blocks, 2, rows, cy), F32),
            pltpu.VMEM((2, blocks, slots), F32),
        ],
        compiler_params=pltpu.CompilerParams(vmem_limit_bytes=40 * 1024 * 1024),
        cost_estimate=pl.CostEstimate(flops=30_000_000_000, bytes_accessed=4_000_000, transcendentals=0),
        name="sweeps",
    )(omega, *msgs)
    parts = {0: outs[0]}
    for s in (2, 3, 1):
        parts[s] = lax.ppermute(outs[s], "my", [(a, a ^ s) for a in range(PARTS)])
    parts = [parts[s] for s in range(n_j)]
    inner, ring, rho_ring = pl.pallas_call(
        functools.partial(response_kernel, n_j),
        out_shape=[
            jax.ShapeDtypeStruct((2 * PARTS, rows, cy), F32),
            jax.ShapeDtypeStruct((2 * PARTS, 8, cy), F32),
            jax.ShapeDtypeStruct((8, cy), F32),
        ],
        in_specs=[smem()] + [vmem()] * 11,
        out_specs=[vmem()] * 3,
        name="response",
    )(omega, *planes, first, last, line, msgs[1], msgs[n_j - 1], msgs[n_j + 1], msgs[2 * n_j - 1])
    field, sens = pl.pallas_call(
        sens_kernel,
        out_shape=[
            jax.ShapeDtypeStruct((2 * PARTS, rows, cy), F32),
            jax.ShapeDtypeStruct((rows + 8, cy), F32),
        ],
        in_specs=[vmem()] * (2 + n_j),
        out_specs=[vmem()] * 2,
        name="sensitivity",
    )(inner, ring, *parts)
    size = lax.axis_size("freq")
    all_freqs = [sens]
    for s in range(1, size):
        all_freqs.append(lax.ppermute(sens, "freq", [(a, (a + s) % size) for a in range(size)]))
    filtered = pl.pallas_call(
        filter_kernel,
        out_shape=jax.ShapeDtypeStruct((rows, cy), F32),
        in_specs=[vmem()] * (2 + size),
        out_specs=vmem(),
        name="filter",
    )(density, rho_ring, *all_freqs)
    return field.reshape(adjoint_rhs.shape), filtered


def solve_split(rhs, density, stiffness, mass, omega, send_rows, recv_rows, mortar_weight):
    rows_x, rows_y = density.shape
    cells = rows_x * rows_y
    w = omega[0]
    stiff = density**3 * stiffness
    rmass = density * mass
    sources = send_rows[0]
    targets = recv_rows[0]
    weights = mortar_weight[0]
    mdiag = jnp.zeros((cells,), jnp.float32).at[targets].add(weights).reshape(rows_x, rows_y)
    real_d = 4.4 * stiff + 0.3 + mdiag - w * w * rmass
    imag_d = 0.2 * w * (stiff + rmass)
    den = real_d * real_d + imag_d * imag_d

    def mortar(field):
        sent = field.reshape(6, cells)[:, sources]
        got = lax.all_to_all(sent, ("mx", "my"), split_axis=1, concat_axis=1, tiled=True)
        added = jnp.zeros((6, cells), jnp.float32).at[:, targets].add(got * weights)
        return added.reshape(6, rows_x, rows_y)

    def sweep(step, field):
        padded = extended(field, (("mx", 1), ("my", 2)), 1)
        beside = (
            padded[:, 2:, 1:-1] + padded[:, :-2, 1:-1] + padded[:, 1:-1, 2:] + padded[:, 1:-1, :-2]
        )
        h = rhs + stiff * beside + mortar(field)
        new_re = (h[:3] * real_d + h[3:] * imag_d) / den
        new_im = (h[3:] * real_d - h[:3] * imag_d) / den
        return jnp.concatenate([new_re, new_im], axis=0)

    return lax.fori_loop(0, ITERS, sweep, jnp.zeros((6, rows_x, rows_y), jnp.float32))


def distributed(
    adjoint_rhs, state, density, stiffness, mass, omega, send_rows, recv_rows, mortar_weight
):
    rows_x, rows_y = density.shape
    w = omega[0]
    dstiff = 3.0 * density**2 * stiffness
    rhs = adjoint_rhs.reshape(6, rows_x, rows_y)
    field = solve_split(rhs, density, stiffness, mass, omega, send_rows, recv_rows, mortar_weight)
    state_six = state.reshape(6, rows_x, rows_y)
    state_pad = extended(state_six, (("mx", 1), ("my", 2)), 1).astype(jnp.float32)
    u = state_six.astype(jnp.float32)
    nb = (
        state_pad[:, 2:, 1:-1]
        + state_pad[:, :-2, 1:-1]
        + state_pad[:, 1:-1, 2:]
        + state_pad[:, 1:-1, :-2]
    )
    da = 4.4 * dstiff - w * w * mass
    db = 0.2 * w * (dstiff + mass)
    t_re = da * u[:3] - db * u[3:] - dstiff * nb[:3]
    t_im = da * u[3:] + db * u[:3] - dstiff * nb[3:]
    sens = -jnp.sum(field[:3] * t_re - field[3:] * t_im, axis=0)
    size = lax.axis_size("freq")
    total = sens
    for s in range(1, size):
        total = total + lax.ppermute(sens, "freq", [(a, (a + s) % size) for a in range(size)])
    weighted = extended(density * total, (("mx", 0), ("my", 1)), 1)
    filt = weighted[1:-1, 1:-1]
    filt = filt + 0.5 * (
        weighted[2:, 1:-1] + weighted[:-2, 1:-1] + weighted[1:-1, 2:] + weighted[1:-1, :-2]
    )
    filt = filt + 0.25 * (
        weighted[2:, 2:] + weighted[:-2, :-2] + weighted[2:, :-2] + weighted[:-2, 2:]
    )
    return (field.reshape(1, 2, 3, rows_x, rows_y), filt / (4.0 * density))


def on_device(*args):
    rows, cy = args[2].shape
    n_i, n_j = lax.axis_size("mx"), lax.axis_size("my")
    fits = n_i == 2 and n_j == 4 and rows == 64 and cy == 2 * LANES and args[6].shape[1] == cy
    return (gathered if fits else distributed)(*args)


def solution(mesh):
    return jax.shard_map(
        on_device,
        mesh=mesh,
        in_specs=(
            P("freq", None, None, "mx", "my"),
            P("freq", None, None, "mx", "my"),
            P("mx", "my"),
            P("mx", "my"),
            P("mx", "my"),
            P("freq"),
            P(("mx", "my"), None),
            P(("mx", "my"), None),
            P(("mx", "my"), None),
        ),
        out_specs=(P("freq", None, None, "mx", "my"), P("mx", "my")),
        check_vma=False,
    )
```

```python
import functools

import jax
import jax.numpy as jnp
from jax import lax
from jax.experimental import pallas as pl
from jax.experimental.pallas import tpu as pltpu
from jax.sharding import PartitionSpec as P

ITERS = 20
PARTS = 3
SMALL_VMEM = 8 * 1024 * 1024
SWEEP_VMEM = 16 * 1024 * 1024
FINE = 2
LANES = 128
F32 = jnp.float32
BF16 = jnp.bfloat16


def extended(x, sides, width):
    for axis, dim in sides:
        size, length = (lax.axis_size(axis), x.shape[dim])
        up = [(i, (i + 1) % size) for i in range(size - 1)]
        down = [(j, i) for i, j in up]
        last = lax.slice_in_dim(x, length - width, length, axis=dim)
        first = lax.slice_in_dim(x, 0, width, axis=dim)
        before = lax.ppermute(last, axis, up)
        after = lax.ppermute(first, axis, down)
        x = jnp.concatenate([before, x, after], axis=dim)
    return x


def placed(cell, rows, cy):
    x, y = cell // cy, cell % cy
    tiles = rows // 8
    return (x % tiles) * 8 + x // tiles, (y % 2) * LANES + y // 2


def lane_order(cy, inverse):
    a = lax.broadcasted_iota(jnp.int32, (cy, cy), 0)
    b = lax.broadcasted_iota(jnp.int32, (cy, cy), 1)
    natural, kept = (b, a) if inverse else (a, b)
    return ((natural % 2) * LANES + natural // 2 == kept).astype(F32).astype(BF16)


STIFF_SCALE, STIFF_POWER = 1.92, 96.0
MASS_SCALE, MASS_POWER = 1.0, 16.0
POWER, FLOOR, SHIFT = 30.0, 1.0 / 256.0, 4.0


def coded(v, most):
    size = jnp.exp2(POWER * (jnp.log2(jnp.abs(v) / most + FLOOR) + SHIFT))
    return jnp.where(v < 0.0, -size, size).astype(BF16)


def decoded(v, most):
    v = v.astype(F32)
    size = (jnp.exp2(jnp.log2(jnp.abs(v)) * (1.0 / POWER) - SHIFT) - FLOOR) * most
    return jnp.where(v < 0.0, -size, size)


def largest(*arrays):
    tops = [jnp.max(jnp.abs(v), axis=(0, 1), keepdims=True) for v in arrays]
    return jnp.maximum(functools.reduce(jnp.maximum, tops), 1e-30)


def raised(v, scale, power):
    return jnp.exp2(power * jnp.log2(v * (1.0 / scale))).astype(BF16)


def lowered(v, scale, power):
    return scale * jnp.exp2(jnp.log2(v.astype(F32)) * (1.0 / power))


def pieces(v):
    out = []
    for _ in range(3):
        out.append(v.astype(BF16).astype(F32))
        v = v - out[-1]
    return out


def split(v):
    high = v.astype(BF16)
    return high, (v - high.astype(F32)).astype(BF16)


def permuted(v, order):
    n = v.shape[0]
    moved = jnp.dot(jnp.concatenate(split(v), axis=0), order, preferred_element_type=F32)
    return moved[:n] + moved[n:]


def planes_of(state, density, stiffness, mass):
    return [state[n].astype(F32) for n in range(2 * PARTS)] + [density[...], stiffness[...], mass[...]]


def edge_block(near, far):
    rows = near[: 2 * PARTS] + [x for v in near[2 * PARTS :] for x in pieces(v)]
    rows = rows + [jnp.zeros((1, LANES), F32)] * (16 - len(rows))
    inner = far[: 2 * PARTS] + [jnp.zeros((1, LANES), F32)] * (16 - 2 * PARTS)
    return jnp.concatenate([jnp.concatenate(rows, axis=0), jnp.concatenate(inner, axis=0)], axis=1)


def edge_rows(msg, present):
    block = msg[msg.shape[0] - 16 :, :].astype(F32)
    block = jnp.where(present, block, 0.0)
    near, far = block[:, :LANES], block[:, LANES:]
    n = 2 * PARTS
    exact = [near[n + 3 * p : n + 3 * p + 1] + near[n + 3 * p + 1 : n + 3 * p + 2] + near[n + 3 * p + 2 : n + 3 * p + 3] for p in range(3)]
    return jnp.concatenate([near[:n]] + exact + [jnp.zeros((7, LANES), F32), far], axis=0)


def pack_kernel(n_j, rhs, density, stiffness, mass, send, recv, weight, state, *outs):
    *outs, first, last, line, pages = outs
    rows, cy = density.shape
    tiles = rows // 8
    info = []
    for ref in (send, recv):
        row, column = placed(ref[...], rows, cy)
        info += [row.astype(F32), column.astype(F32)]
    info += pieces(weight[...])
    top = lax.axis_index("mx") == 0
    lane = lax.broadcasted_iota(jnp.int32, (1, LANES), 1)
    sides = [[[], []], [[], []]]
    for out in (first, last, line):
        out[...] = jnp.zeros_like(out)
    for n, v in enumerate(planes_of(state, density, stiffness, mass)):
        turned = jnp.transpose(jnp.concatenate([v[:, :LANES], v[:, cy - LANES :]], axis=0))
        late = pltpu.roll(turned[LANES - 8 :], rows, 1)
        for k in range(2):
            sides[0][k].append(jnp.where(lane < rows, turned[k : k + 1], 0.0))
            sides[1][k].append(jnp.where(lane < rows, late[7 - k : 8 - k], 0.0))
            line[pl.ds(16 * k + n, 1), :] = jnp.where(top, v[rows - 1 - k : rows - k], v[k : k + 1])
        first[pl.ds(n, 1), :] = sides[0][0][-1]
        last[pl.ds(n, 1), :] = sides[1][0][-1]
    edges = [edge_block(*side).astype(BF16) for side in sides]
    order = lane_order(cy, False)
    slot = 0

    def packed(value):
        nonlocal slot
        value = permuted(value, order)
        halves = []
        for u in range(cy // LANES):
            page = pages.at[slot % pages.shape[0]]
            slot += 1
            page[...] = value[:, u * LANES : (u + 1) * LANES]
            halves.append(jnp.concatenate([page[pl.ds(t, 8, stride=tiles), :] for t in range(tiles)], axis=0))
        return jnp.concatenate(halves, axis=1)

    rho = density[...]
    stiff = raised(packed(rho * rho * rho * stiffness[...]), STIFF_SCALE, STIFF_POWER)
    rmass = raised(packed(rho * mass[...]), MASS_SCALE, MASS_POWER)
    for s, out in enumerate(outs):
        c = jnp.minimum(lax.rem(lax.axis_index("my") + s, n_j), PARTS - 1)
        re, im = rhs[c], rhs[PARTS + c]
        most = largest(re, im)
        out[:rows, :] = coded(packed(re), most)
        out[rows : 2 * rows, :] = coded(packed(im), most)
        out[2 * rows : 3 * rows, :] = stiff
        out[3 * rows : 4 * rows, :] = rmass
        scale = [jnp.broadcast_to(x, (1, cy)) for x in pieces(most)]
        out[4 * rows : 4 * rows + 16, :] = jnp.concatenate(info + scale + [jnp.zeros((6, cy), F32)], axis=0).astype(BF16)
        beside = edges[1] if s == 1 else edges[0] if s == n_j - 1 else jnp.zeros((16, cy), BF16)
        out[4 * rows + 16 :, :] = beside


def sweep_kernel(n_i, n_j, cap, omega, *refs):
    blocks = n_i * n_j
    msgs, refs = refs[: blocks], refs[blocks:]
    outs, refs = refs[:n_j], refs[n_j:]
    field_a, field_b, start, inverse, gain, lag, info, weights, pick, rowmask, spread, place, group, values, pages, plain, ends, rim, frame, mid, values_b = refs
    rows, cy = start.shape[2:]
    slots = blocks * cap
    me_i, me_j = lax.axis_index("mx"), lax.axis_index("my")
    w = omega[0]

    order = [(a, s) for a in range(n_i) for s in range(n_j)]
    index = [lax.rem(me_i + a, n_i) * n_j + lax.rem(me_j + n_j - s, n_j) for a, s in order]
    for msg, b in zip(msgs, index):
        info[b] = msg[4 * rows : 4 * rows + 16, :].astype(F32)
    chunk = lax.broadcasted_iota(jnp.int32, (blocks, slots), 1) // cap
    source = lax.broadcasted_iota(jnp.int32, (blocks, slots), 0)

    def one_hot(line, depth):
        at = lax.broadcasted_iota(jnp.int32, (depth, slots), 0)
        return (jnp.broadcast_to(line.astype(jnp.int32), at.shape) == at).astype(F32)

    for b in range(blocks):
        line = info[b]
        line = pltpu.roll(line, b * cap, 1) if b else line
        pick[b] = one_hot(line[1:2], cy).astype(BF16)
        rowmask[b] = one_hot(line[0:1], rows)
        row_out = one_hot(line[2:3], rows)
        spread[b] = row_out.astype(BF16)
        lane_out = jnp.transpose(one_hot(line[3:4], cy)).astype(BF16)
        place[b] = lane_out
        group[b] = (chunk == (source + b) % blocks).astype(F32)
        high, low = split(row_out * (line[4:5] + line[5:6] + line[6:7]))
        both = jnp.dot(jnp.concatenate([high, low], axis=0), lane_out, preferred_element_type=F32)
        gain[b] = both[:rows] + both[rows:]

    for msg, b in zip(msgs, index):
        rhs_re, rhs_im, k, m = [msg[n * rows : (n + 1) * rows, :] for n in range(4)]
        most = info[b][7:8] + info[b][8:9] + info[b][9:10]
        rhs_re, rhs_im = decoded(rhs_re, most), decoded(rhs_im, most)
        k, m = lowered(k, STIFF_SCALE, STIFF_POWER), lowered(m, MASS_SCALE, MASS_POWER)
        real_d = 4.4 * k + 0.3 + gain[b] - w * w * m
        imag_d = 0.2 * w * (k + m)
        scale = 1.0 / (real_d * real_d + imag_d * imag_d)
        g, l = real_d * scale, imag_d * scale
        first_re, first_im = rhs_re * g + rhs_im * l, rhs_im * g - rhs_re * l
        gain[b], lag[b], inverse[b] = k * g, k * l, 1.0 / k
        start[b, 0], start[b, 1] = first_re, first_im
        field_a[b, 0], field_a[b, 1] = first_re, first_im

    for b in range(blocks):
        line = info[b]
        line = pltpu.roll(line, b * cap, 1) if b else line
        lane_out = one_hot(line[3:4], cy).astype(BF16)
        found = jnp.dot(jnp.concatenate(split(inverse[b]), axis=0), lane_out, preferred_element_type=F32)
        found = (found[:rows] + found[rows:]) * one_hot(line[2:3], rows)
        found = jnp.sum(found, axis=0, keepdims=True)
        weights[pl.ds(b, 1), :] = (line[4:5] + line[5:6] + line[6:7]) * found

    row8 = lax.broadcasted_iota(jnp.int32, (8, LANES), 0)
    lane_r = lax.broadcasted_iota(jnp.int32, (rows, LANES), 1)
    zero = jnp.zeros((rows, LANES), F32)

    def gather(held, b, re, im, fine):
        whole = jnp.concatenate(re + im, axis=0)
        whole = jnp.concatenate(split(whole), axis=0) if fine else whole.astype(BF16)
        got = jnp.dot(whole, pick[b], preferred_element_type=F32)
        mask = rowmask[b]
        for part in range(2):
            mine = got[part * rows : (part + 1) * rows]
            if fine:
                mine += got[(part + 2) * rows : (part + 3) * rows]
            held[part, pl.ds(b, 1), :] = jnp.sum(mine * mask, axis=0, keepdims=True)

    def mortar_at(held, b, fine):
        arrived = [jnp.sum(held[part] * group[b], axis=0, keepdims=True) * weights[b : b + 1, :] for part in range(2)]
        left = []
        for r in range(0, rows, 16):
            for v in arrived:
                left += [spread[b, r : r + 16] * x for x in (split(v) if fine else [v.astype(BF16)])]
        mortar = jnp.dot(jnp.concatenate(left, axis=0), place[b], preferred_element_type=F32)
        each = 2 if fine else 1
        parts = []
        for r in range(rows // 16 * 2):
            part = mortar[r * each * 16 : r * each * 16 + 16]
            parts.append(part + mortar[r * each * 16 + 16 : r * each * 16 + 32] if fine else part)
        return parts

    def around_of(now, b, part, u):
        i, j = b // n_j, b % n_j
        lanes = slice(u * LANES, (u + 1) * LANES)
        others = slice((1 - u) * LANES, (2 - u) * LANES)
        own, other = now[b, part, :, lanes], now[b, part, :, others]
        if u == 0:
            edge = now[b - 1, part, :, others] if j > 0 else zero
            around = pltpu.roll(jnp.where(lane_r == LANES - 1, edge, other), 1, 1)
        else:
            edge = now[b + 1, part, :, others] if j < n_j - 1 else zero
            around = pltpu.roll(jnp.where(lane_r == 0, edge, other), LANES - 1, 1)
        around += other
        above = now[b - n_j, part, rows - 8 :, lanes] if i > 0 else zero[:8]
        below = now[b + n_j, part, :8, lanes] if i < n_i - 1 else zero[:8]
        top = pltpu.roll(jnp.where(row8 == 7, above, own[rows - 8 :]), 1, 0)
        bottom = pltpu.roll(jnp.where(row8 == 0, below, own[:8]), 7, 0)
        around += jnp.concatenate([top, own[:-8]], axis=0)
        return around + jnp.concatenate([own[8:], bottom], axis=0)

    def beside(now, b):
        for u in range(2):
            lanes = slice(u * LANES, (u + 1) * LANES)
            for part in range(2):
                mid[b, part, :, lanes] = around_of(now, b, part, u)

    def sweep(now, then, fine, fine_next):
        held, ahead = (values, values_b) if now is field_a else (values_b, values)

        def finish(b):
            mortar = mortar_at(held, b, fine)
            new = ([], [])
            for n in range(rows // 16):
                at = slice(n * 16, n * 16 + 16)
                re, im = mid[b, 0, at] + mortar[2 * n], mid[b, 1, at] + mortar[2 * n + 1]
                g, l = gain[b, at], lag[b, at]
                new[0].append(start[b, 0, at] + re * g + im * l)
                new[1].append(start[b, 1, at] + im * g - re * l)
                then[b, 0, at], then[b, 1, at] = new[0][-1], new[1][-1]
            if fine_next is not None:
                gather(ahead, b, *new, fine_next)

        for b in range(blocks):
            beside(now, b)
            finish(b)

    def pair(fine, step, carry):
        sweep(field_a, field_b, fine, fine)
        sweep(field_b, field_a, fine, fine)
        return carry

    fine_pairs = min(FINE, ITERS - 1) // 2
    pairs = (ITERS - 1) // 2
    for b in range(blocks):
        gather(values, b, [field_a[b, 0]], [field_a[b, 1]], False)
    lax.fori_loop(0, pairs - fine_pairs, functools.partial(pair, False), 0)
    lax.fori_loop(0, fine_pairs, functools.partial(pair, True), 0)
    last = field_a
    if (ITERS - 1) % 2:
        sweep(field_a, field_b, FINE > 0, None)
        last = field_b
    tiles = rows // 8
    back = lane_order(cy, True)
    around_mesh = jnp.zeros((rows, LANES), F32)
    for part in range(2):
        for at in (0, LANES + n_j * cy):
            plain[part, :, at : at + LANES] = around_mesh
            ends[part, :, at : at + LANES] = around_mesh[:8]
    end = jnp.where(me_i == 0, 0, rows - 1)
    rim[...] = jnp.zeros_like(rim)
    for j in range(n_j):
        for part in range(2):
            halves = []
            for u in range(2):
                page = pages.at[(j * 4 + part * 2 + u) % 8]
                lanes = slice(u * LANES, (u + 1) * LANES)
                for t in range(tiles):
                    page[pl.ds(t, 8, stride=tiles), :] = last[me_i * n_j + j, part, t * 8 : (t + 1) * 8, lanes]
                halves.append(page[...])
            plain[part, :, LANES + j * cy : LANES + (j + 1) * cy] = permuted(jnp.concatenate(halves, axis=1), back)
            rim[pl.ds(part * 4 + j, 1), :] = last[(1 - me_i) * n_j + j, part, pl.ds(end, 1), :]
    natural = permuted(rim[...], back)
    ends[:, :, LANES : LANES + n_j * cy] = jnp.zeros((2, 8, n_j * cy), F32)
    for j in range(n_j):
        for part in range(2):
            for at in (0, 7):
                ends[part, at : at + 1, LANES + j * cy : LANES + (j + 1) * cy] = natural[
                    part * 4 + j : part * 4 + j + 1
                ]
    for s, out in enumerate(outs):
        base = pl.multiple_of(LANES + (me_j ^ s) * cy, LANES)
        frame[...] = jnp.zeros_like(frame)
        block = [plain[part, :, pl.ds(base, cy)] for part in range(2)]
        for part in range(2):
            frame[pl.ds(part * 8, 1), :] = ends[part, 0:1, pl.ds(base, cy)]
            for k, (at, lane) in enumerate(((base - LANES, LANES - 1), (base + cy, 0)), 1):
                at = pl.multiple_of(at, LANES)
                beyond = [plain[part, :, pl.ds(at, LANES)], ends[part, :, pl.ds(at, LANES)]]
                beyond = beyond + [jnp.zeros((LANES - rows - 16, LANES), F32), beyond[1]]
                beyond = jnp.concatenate(beyond, axis=0)
                frame[pl.ds(part * 8 + k, 1), :LANES] = jnp.transpose(beyond)[lane : lane + 1]
        block.append(frame[...])
        if s:
            most = largest(*block)
            block = [coded(v, most) for v in block]
            row = lax.broadcasted_iota(jnp.int32, (16, cy), 0)
            for k, piece in enumerate(pieces(most)):
                block[2] = jnp.where(row == 3 + k, piece, block[2].astype(F32)).astype(BF16)
        for v, at in zip(block, (0, rows, 2 * rows)):
            out[at : at + v.shape[0], :] = v


def response_kernel(
    n_j, omega, state, density, stiffness, mass, first, last, line, west, east, *refs
):
    beyond_west, beyond_east, inner, ring, rho_ring = refs
    rows, cy = density.shape
    w = omega[0]
    top = lax.axis_index("mx") == 0
    present = (lax.axis_index("my") > 0, lax.axis_index("my") < n_j - 1)
    zero = jnp.zeros((1, cy), F32)

    def terms(u_re, u_im, nb_re, nb_im, rho, k, m):
        dstiff = 3.0 * rho * rho * k
        da = 4.4 * dstiff - w * w * m
        db = 0.2 * w * (dstiff + m)
        return da * u_re - db * u_im - dstiff * nb_re, da * u_im + db * u_re - dstiff * nb_im

    line = line[...]
    siblings = [edge_rows(m, p) for m, p in zip((beyond_west, beyond_east), present)]
    side = [edge_rows(m, p) + pltpu.roll(y, rows, 1) for m, p, y in zip((west, east), present, siblings)]
    lane = lax.broadcasted_iota(jnp.int32, (16, LANES), 1)
    start = jnp.where(top, 0, rows)
    stop = jnp.where(top, LANES - 1, rows - 1)
    corner = (lane == rows) | (lane == LANES - 1)
    around = []
    lane_cy = lax.broadcasted_iota(jnp.int32, (16, cy), 1)
    near = line[:16]
    touch = [jnp.where(top, y[:16, 0:1], y[:16, rows - 1 : rows]) for y in siblings]
    before = jnp.where(lane_cy == 0, touch[0], pltpu.roll(near, 1, 1))
    after = jnp.where(lane_cy == cy - 1, touch[1], pltpu.roll(near, cy - 1, 1))
    adjacent = []
    planes = planes_of(state, density, stiffness, mass)
    for v in planes:
        adjacent.append(jnp.where(top, v[rows - 1 :], v[:1]))
    adjacent = jnp.concatenate(adjacent + [zero] * 7, axis=0)
    around.append(line[16:] + adjacent + before + after)
    for x, own, at in ((side[0], first, 0), (side[1], last, cy - 1)):
        own = jnp.where(corner, near[:, at : at + 1], own[:16, :])
        before = jnp.where(lane == start, 0.0, pltpu.roll(x[:16], 1, 1))
        after = jnp.where(lane == stop, 0.0, pltpu.roll(x[:16], LANES - 1, 1))
        around.append(x[16:] + own + before + after)
    for row, (u, nb) in enumerate(zip([near] + [x[:16] for x in side], around)):
        t = terms(u[:3], u[3:6], nb[:3], nb[3:6], u[6:7], u[7:8], u[8:9])
        for part in range(2):
            for c in range(PARTS):
                ring[part * PARTS + c, row : row + 1, : u.shape[1]] = t[part][c : c + 1]
        rho_ring[row : row + 1, : u.shape[1]] = u[6:7]
    for n in range(2 * PARTS):
        ring[n, 1:, LANES:] = jnp.zeros((7, cy - LANES), F32)
        ring[n, 3:, :LANES] = jnp.zeros((5, LANES), F32)
    rho_ring[1:, LANES:] = jnp.zeros((7, cy - LANES), F32)
    rho_ring[3:, :LANES] = jnp.zeros((5, LANES), F32)

    fill = jnp.zeros((LANES - 16, LANES), F32)
    columns = [jnp.transpose(jnp.concatenate([x[:16], fill], axis=0)) for x in side]
    lane = lax.broadcasted_iota(jnp.int32, (rows, cy), 1)
    row = lax.broadcasted_iota(jnp.int32, (rows, cy), 0)

    def neighbours(n):
        v = planes[n]
        total = jnp.where(lane == 0, columns[0][:rows, n : n + 1], pltpu.roll(v, 1, 1))
        total += jnp.where(lane == cy - 1, columns[1][:rows, n : n + 1], pltpu.roll(v, cy - 1, 1))
        edge = line[n : n + 1]
        total += jnp.where(row == 0, jnp.where(top, zero, edge), pltpu.roll(v, 1, 0))
        return total + jnp.where(row == rows - 1, jnp.where(top, edge, zero), pltpu.roll(v, rows - 1, 0))

    for c in range(PARTS):
        t = terms(planes[c], planes[PARTS + c], neighbours(c), neighbours(PARTS + c), *planes[6:])
        inner[c], inner[PARTS + c] = t


def for_each_part(msgs, rows, use):
    for s, msg in enumerate(msgs):
        c = lax.axis_index("my") ^ s

        @pl.when(c < PARTS)
        def _(msg=msg, c=c):
            planes = msg[...]
            if msg.dtype == BF16:
                scale = planes[2 * rows :].astype(F32)
                planes = decoded(planes, scale[3:4] + scale[4:5] + scale[5:6])
            use(c, planes)


def sens_kernel(inner, ring, *refs):
    *msgs, sens = refs
    rows = inner.shape[1]
    sens[...] = jnp.zeros_like(sens)

    def use(c, planes):
        re, im = planes[:rows], planes[rows : 2 * rows]
        sens[:rows, :] -= re * inner[c] - im * inner[PARTS + c]
        re, im = planes[2 * rows : 2 * rows + 8], planes[2 * rows + 8 :]
        sens[rows:, :] -= re * ring[c] - im * ring[PARTS + c]

    for_each_part(msgs, rows, use)


def field_kernel(*refs):
    *msgs, field = refs
    rows = field.shape[1]

    def use(c, planes):
        field[c], field[PARTS + c] = planes[:rows], planes[rows : 2 * rows]

    for_each_part(msgs, rows, use)


def filter_kernel(density, ring, *refs):
    parts, out = refs[:-1], refs[-1]
    rows, cy = density.shape
    total = parts[0][...]
    for part in parts[1:]:
        total = total + part[...]
    top = lax.axis_index("mx") == 0
    rho = density[...]
    inner, ring = rho * total[:rows], ring[...] * total[rows:]
    columns = jnp.transpose(jnp.concatenate([ring, jnp.zeros((LANES - 8, cy), F32)], axis=0)[:, :LANES])

    def across(v, before, after):
        lane = lax.broadcasted_iota(jnp.int32, v.shape, 1)
        before = jnp.where(lane == 0, before, pltpu.roll(v, 1, 1))
        after = jnp.where(lane == cy - 1, after, pltpu.roll(v, cy - 1, 1))
        return v + 0.5 * (before + after)

    mid = across(inner, columns[:rows, 1:2], columns[:rows, 2:3])
    corner = jnp.where(top, columns[rows : rows + 1], columns[LANES - 1 :])
    end = across(ring, corner[:, 1:2], corner[:, 2:3])[0:1]
    row = lax.broadcasted_iota(jnp.int32, mid.shape, 0)
    empty = jnp.zeros_like(end)
    above = jnp.where(row == 0, jnp.where(top, empty, end), pltpu.roll(mid, 1, 0))
    below = jnp.where(row == rows - 1, jnp.where(top, end, empty), pltpu.roll(mid, rows - 1, 0))
    out[...] = (mid + 0.5 * (above + below)) / (4.0 * rho)


def vmem():
    return pl.BlockSpec(memory_space=pltpu.VMEM)


def smem():
    return pl.BlockSpec(memory_space=pltpu.SMEM)


def gathered(
    adjoint_rhs, state, density, stiffness, mass, omega, send_rows, recv_rows, mortar_weight
):
    rhs = adjoint_rhs.reshape(2 * PARTS, *density.shape)
    rows, cy = density.shape
    n_i, n_j = lax.axis_size("mx"), lax.axis_size("my")
    blocks = n_i * n_j
    slots = send_rows.shape[1]
    cap = slots // blocks
    planes = (state.reshape(2 * PARTS, rows, cy), density, stiffness, mass)
    edge = jax.ShapeDtypeStruct((16, LANES), F32)
    message = jax.ShapeDtypeStruct((4 * rows + 32, cy), BF16)
    *own, first, last, line = pl.pallas_call(
        functools.partial(pack_kernel, n_j),
        out_shape=[message] * n_j + [edge, edge, jax.ShapeDtypeStruct((32, cy), F32)],
        in_specs=[vmem()] * 8,
        out_specs=[vmem()] * (n_j + 3),
        scratch_shapes=[pltpu.VMEM((8, rows, LANES), F32)],
        name="pack",
    )(rhs, density, stiffness, mass, send_rows, recv_rows, mortar_weight, planes[0])
    msgs = [own[0]]
    for s in range(1, n_j):
        pairs = [(a, (a + s) % n_j) for a in range(n_j)]
        pairs = [(a, b) for a, b in pairs if b < PARTS or (s == 1 and b == PARTS)]
        msgs.append(lax.ppermute(own[s], "my", pairs))
    swap = [(0, 1), (1, 0)]
    msgs += [lax.ppermute(m, "mx", swap) for m in msgs]
    line = lax.ppermute(line, "mx", swap)
    block = (blocks, rows, cy)
    outs = pl.pallas_call(
        functools.partial(sweep_kernel, n_i, n_j, cap),
        out_shape=[jax.ShapeDtypeStruct((2 * rows + 16, cy), BF16 if s else F32) for s in range(n_j)],
        in_specs=[smem()] + [vmem()] * blocks,
        out_specs=[vmem()] * n_j,
        scratch_shapes=[
            pltpu.VMEM((blocks, 2, rows, cy), F32),
            pltpu.VMEM((blocks, 2, rows, cy), F32),
            pltpu.VMEM((blocks, 2, rows, cy), F32),
            pltpu.VMEM(block, F32),
            pltpu.VMEM(block, F32),
            pltpu.VMEM(block, F32),
            pltpu.VMEM((blocks, 16, cy), F32),
            pltpu.VMEM((blocks, slots), F32),
            pltpu.VMEM((blocks, cy, slots), BF16),
            pltpu.VMEM((blocks, rows, slots), F32),
            pltpu.VMEM((blocks, rows, slots), BF16),
            pltpu.VMEM((blocks, slots, cy), BF16),
            pltpu.VMEM((blocks, blocks, slots), F32),
            pltpu.VMEM((2, blocks, slots), F32),
            pltpu.VMEM((8, rows, LANES), F32),
            pltpu.VMEM((2, rows, n_j * cy + 2 * LANES), F32),
            pltpu.VMEM((2, 8, n_j * cy + 2 * LANES), F32),
            pltpu.VMEM((8, cy), F32),
            pltpu.VMEM((16, cy), F32),
            pltpu.VMEM((blocks, 2, rows, cy), F32),
            pltpu.VMEM((2, blocks, slots), F32),
        ],
        compiler_params=pltpu.CompilerParams(vmem_limit_bytes=SWEEP_VMEM),
        cost_estimate=pl.CostEstimate(flops=30_000_000_000, bytes_accessed=4_000_000, transcendentals=0),
        name="sweeps",
    )(omega, *msgs)
    parts = {0: outs[0]}
    for s in (2, 3, 1):
        parts[s] = lax.ppermute(outs[s], "my", [(a, a ^ s) for a in range(PARTS)])
    parts = [parts[s] for s in range(n_j)]
    inner, ring, rho_ring = pl.pallas_call(
        functools.partial(response_kernel, n_j),
        out_shape=[
            jax.ShapeDtypeStruct((2 * PARTS, rows, cy), F32),
            jax.ShapeDtypeStruct((2 * PARTS, 8, cy), F32),
            jax.ShapeDtypeStruct((8, cy), F32),
        ],
        in_specs=[smem()] + [vmem()] * 11,
        out_specs=[vmem()] * 3,
        compiler_params=pltpu.CompilerParams(vmem_limit_bytes=SMALL_VMEM),
        name="response",
    )(omega, *planes, first, last, line, msgs[1], msgs[n_j - 1], msgs[n_j + 1], msgs[2 * n_j - 1])
    sens = pl.pallas_call(
        sens_kernel,
        out_shape=jax.ShapeDtypeStruct((rows + 8, cy), F32),
        in_specs=[vmem()] * (2 + n_j),
        out_specs=vmem(),
        compiler_params=pltpu.CompilerParams(vmem_limit_bytes=SMALL_VMEM),
        name="sensitivity",
    )(inner, ring, *parts)
    size = lax.axis_size("freq")
    all_freqs = [sens]
    for s in range(1, size):
        all_freqs.append(lax.ppermute(sens, "freq", [(a, (a + s) % size) for a in range(size)]))
    field = pl.pallas_call(
        field_kernel,
        out_shape=jax.ShapeDtypeStruct((2 * PARTS, rows, cy), F32),
        in_specs=[vmem()] * n_j,
        out_specs=vmem(),
        compiler_params=pltpu.CompilerParams(vmem_limit_bytes=SMALL_VMEM),
        name="adjoint",
    )(*parts)
    filtered = pl.pallas_call(
        filter_kernel,
        out_shape=jax.ShapeDtypeStruct((rows, cy), F32),
        in_specs=[vmem()] * (2 + size),
        out_specs=vmem(),
        compiler_params=pltpu.CompilerParams(vmem_limit_bytes=SMALL_VMEM),
        name="filter",
    )(density, rho_ring, *all_freqs)
    return field.reshape(adjoint_rhs.shape), filtered


def solve_split(rhs, density, stiffness, mass, omega, send_rows, recv_rows, mortar_weight):
    rows_x, rows_y = density.shape
    cells = rows_x * rows_y
    w = omega[0]
    stiff = density**3 * stiffness
    rmass = density * mass
    sources = send_rows[0]
    targets = recv_rows[0]
    weights = mortar_weight[0]
    mdiag = jnp.zeros((cells,), jnp.float32).at[targets].add(weights).reshape(rows_x, rows_y)
    real_d = 4.4 * stiff + 0.3 + mdiag - w * w * rmass
    imag_d = 0.2 * w * (stiff + rmass)
    den = real_d * real_d + imag_d * imag_d

    def mortar(field):
        sent = field.reshape(6, cells)[:, sources]
        got = lax.all_to_all(sent, ("mx", "my"), split_axis=1, concat_axis=1, tiled=True)
        added = jnp.zeros((6, cells), jnp.float32).at[:, targets].add(got * weights)
        return added.reshape(6, rows_x, rows_y)

    def sweep(step, field):
        padded = extended(field, (("mx", 1), ("my", 2)), 1)
        beside = (
            padded[:, 2:, 1:-1] + padded[:, :-2, 1:-1] + padded[:, 1:-1, 2:] + padded[:, 1:-1, :-2]
        )
        h = rhs + stiff * beside + mortar(field)
        new_re = (h[:3] * real_d + h[3:] * imag_d) / den
        new_im = (h[3:] * real_d - h[:3] * imag_d) / den
        return jnp.concatenate([new_re, new_im], axis=0)

    return lax.fori_loop(0, ITERS, sweep, jnp.zeros((6, rows_x, rows_y), jnp.float32))


def distributed(
    adjoint_rhs, state, density, stiffness, mass, omega, send_rows, recv_rows, mortar_weight
):
    rows_x, rows_y = density.shape
    w = omega[0]
    dstiff = 3.0 * density**2 * stiffness
    rhs = adjoint_rhs.reshape(6, rows_x, rows_y)
    field = solve_split(rhs, density, stiffness, mass, omega, send_rows, recv_rows, mortar_weight)
    state_six = state.reshape(6, rows_x, rows_y)
    state_pad = extended(state_six, (("mx", 1), ("my", 2)), 1).astype(jnp.float32)
    u = state_six.astype(jnp.float32)
    nb = (
        state_pad[:, 2:, 1:-1]
        + state_pad[:, :-2, 1:-1]
        + state_pad[:, 1:-1, 2:]
        + state_pad[:, 1:-1, :-2]
    )
    da = 4.4 * dstiff - w * w * mass
    db = 0.2 * w * (dstiff + mass)
    t_re = da * u[:3] - db * u[3:] - dstiff * nb[:3]
    t_im = da * u[3:] + db * u[:3] - dstiff * nb[3:]
    sens = -jnp.sum(field[:3] * t_re - field[3:] * t_im, axis=0)
    size = lax.axis_size("freq")
    total = sens
    for s in range(1, size):
        total = total + lax.ppermute(sens, "freq", [(a, (a + s) % size) for a in range(size)])
    weighted = extended(density * total, (("mx", 0), ("my", 1)), 1)
    filt = weighted[1:-1, 1:-1]
    filt = filt + 0.5 * (
        weighted[2:, 1:-1] + weighted[:-2, 1:-1] + weighted[1:-1, 2:] + weighted[1:-1, :-2]
    )
    filt = filt + 0.25 * (
        weighted[2:, 2:] + weighted[:-2, :-2] + weighted[2:, :-2] + weighted[:-2, 2:]
    )
    return (field.reshape(1, 2, 3, rows_x, rows_y), filt / (4.0 * density))


def on_device(*args):
    rows, cy = args[2].shape
    n_i, n_j = lax.axis_size("mx"), lax.axis_size("my")
    fits = n_i == 2 and n_j == 4 and rows == 64 and cy == 2 * LANES and args[6].shape[1] == cy
    return (gathered if fits else distributed)(*args)


def solution(mesh):
    return jax.shard_map(
        on_device,
        mesh=mesh,
        in_specs=(
            P("freq", None, None, "mx", "my"),
            P("freq", None, None, "mx", "my"),
            P("mx", "my"),
            P("mx", "my"),
            P("mx", "my"),
            P("freq"),
            P(("mx", "my"), None),
            P(("mx", "my"), None),
            P(("mx", "my"), None),
        ),
        out_specs=(P("freq", None, None, "mx", "my"), P("mx", "my")),
        check_vma=False,
    )
```

```python
import functools

import jax
import jax.numpy as jnp
from jax import lax
from jax.experimental import pallas as pl
from jax.experimental.pallas import tpu as pltpu
from jax.sharding import PartitionSpec as P

ITERS = 20
PARTS = 3
SMALL_VMEM = 8 * 1024 * 1024
SWEEP_VMEM = 16 * 1024 * 1024
FINE = 2
LANES = 128
F32 = jnp.float32
BF16 = jnp.bfloat16


def extended(x, sides, width):
    for axis, dim in sides:
        size, length = (lax.axis_size(axis), x.shape[dim])
        up = [(i, (i + 1) % size) for i in range(size - 1)]
        down = [(j, i) for i, j in up]
        last = lax.slice_in_dim(x, length - width, length, axis=dim)
        first = lax.slice_in_dim(x, 0, width, axis=dim)
        before = lax.ppermute(last, axis, up)
        after = lax.ppermute(first, axis, down)
        x = jnp.concatenate([before, x, after], axis=dim)
    return x


def placed(cell, rows, cy):
    x, y = cell // cy, cell % cy
    tiles = rows // 8
    return (x % tiles) * 8 + x // tiles, (y % 2) * LANES + y // 2


def lane_order(cy, inverse):
    a = lax.broadcasted_iota(jnp.int32, (cy, cy), 0)
    b = lax.broadcasted_iota(jnp.int32, (cy, cy), 1)
    natural, kept = (b, a) if inverse else (a, b)
    return ((natural % 2) * LANES + natural // 2 == kept).astype(F32).astype(BF16)


STIFF_SCALE, STIFF_POWER = 1.92, 96.0
MASS_SCALE, MASS_POWER = 1.0, 16.0
POWER, FLOOR, SHIFT = 30.0, 1.0 / 256.0, 4.0


def coded(v, most):
    size = jnp.exp2(POWER * (jnp.log2(jnp.abs(v) / most + FLOOR) + SHIFT))
    return jnp.where(v < 0.0, -size, size).astype(BF16)


def decoded(v, most):
    v = v.astype(F32)
    size = (jnp.exp2(jnp.log2(jnp.abs(v)) * (1.0 / POWER) - SHIFT) - FLOOR) * most
    return jnp.where(v < 0.0, -size, size)


def largest(*arrays):
    tops = [jnp.max(jnp.abs(v), axis=(0, 1), keepdims=True) for v in arrays]
    return jnp.maximum(functools.reduce(jnp.maximum, tops), 1e-30)


def raised(v, scale, power):
    return jnp.exp2(power * jnp.log2(v * (1.0 / scale))).astype(BF16)


def lowered(v, scale, power):
    return scale * jnp.exp2(jnp.log2(v.astype(F32)) * (1.0 / power))


def pieces(v):
    out = []
    for _ in range(3):
        out.append(v.astype(BF16).astype(F32))
        v = v - out[-1]
    return out


def split(v):
    high = v.astype(BF16)
    return high, (v - high.astype(F32)).astype(BF16)


def permuted(v, order):
    n = v.shape[0]
    moved = jnp.dot(jnp.concatenate(split(v), axis=0), order, preferred_element_type=F32)
    return moved[:n] + moved[n:]


def planes_of(state, density, stiffness, mass):
    return [state[n].astype(F32) for n in range(2 * PARTS)] + [density[...], stiffness[...], mass[...]]


def edge_block(near, far):
    rows = near[: 2 * PARTS] + [x for v in near[2 * PARTS :] for x in pieces(v)]
    rows = rows + [jnp.zeros((1, LANES), F32)] * (16 - len(rows))
    inner = far[: 2 * PARTS] + [jnp.zeros((1, LANES), F32)] * (16 - 2 * PARTS)
    return jnp.concatenate([jnp.concatenate(rows, axis=0), jnp.concatenate(inner, axis=0)], axis=1)


def edge_rows(msg, present):
    block = msg[msg.shape[0] - 16 :, :].astype(F32)
    block = jnp.where(present, block, 0.0)
    near, far = block[:, :LANES], block[:, LANES:]
    n = 2 * PARTS
    exact = [near[n + 3 * p : n + 3 * p + 1] + near[n + 3 * p + 1 : n + 3 * p + 2] + near[n + 3 * p + 2 : n + 3 * p + 3] for p in range(3)]
    return jnp.concatenate([near[:n]] + exact + [jnp.zeros((7, LANES), F32), far], axis=0)


def pack_kernel(n_j, rhs, density, stiffness, mass, send, recv, weight, state, *outs):
    *outs, first, last, line, pages = outs
    rows, cy = density.shape
    tiles = rows // 8
    info = []
    for ref in (send, recv):
        row, column = placed(ref[...], rows, cy)
        info += [row.astype(F32), column.astype(F32)]
    info += pieces(weight[...])
    top = lax.axis_index("mx") == 0
    lane = lax.broadcasted_iota(jnp.int32, (1, LANES), 1)
    sides = [[[], []], [[], []]]
    for out in (first, last, line):
        out[...] = jnp.zeros_like(out)
    for n, v in enumerate(planes_of(state, density, stiffness, mass)):
        turned = jnp.transpose(jnp.concatenate([v[:, :LANES], v[:, cy - LANES :]], axis=0))
        late = pltpu.roll(turned[LANES - 8 :], rows, 1)
        for k in range(2):
            sides[0][k].append(jnp.where(lane < rows, turned[k : k + 1], 0.0))
            sides[1][k].append(jnp.where(lane < rows, late[7 - k : 8 - k], 0.0))
            line[pl.ds(16 * k + n, 1), :] = jnp.where(top, v[rows - 1 - k : rows - k], v[k : k + 1])
        first[pl.ds(n, 1), :] = sides[0][0][-1]
        last[pl.ds(n, 1), :] = sides[1][0][-1]
    edges = [edge_block(*side).astype(BF16) for side in sides]
    order = lane_order(cy, False)
    slot = 0

    def packed(value):
        nonlocal slot
        value = permuted(value, order)
        halves = []
        for u in range(cy // LANES):
            page = pages.at[slot % pages.shape[0]]
            slot += 1
            page[...] = value[:, u * LANES : (u + 1) * LANES]
            halves.append(jnp.concatenate([page[pl.ds(t, 8, stride=tiles), :] for t in range(tiles)], axis=0))
        return jnp.concatenate(halves, axis=1)

    rho = density[...]
    stiff = raised(packed(rho * rho * rho * stiffness[...]), STIFF_SCALE, STIFF_POWER)
    rmass = raised(packed(rho * mass[...]), MASS_SCALE, MASS_POWER)
    for s, out in enumerate(outs):
        c = jnp.minimum(lax.rem(lax.axis_index("my") + s, n_j), PARTS - 1)
        re, im = rhs[c], rhs[PARTS + c]
        most = largest(re, im)
        out[:rows, :] = coded(packed(re), most)
        out[rows : 2 * rows, :] = coded(packed(im), most)
        out[2 * rows : 3 * rows, :] = stiff
        out[3 * rows : 4 * rows, :] = rmass
        scale = [jnp.broadcast_to(x, (1, cy)) for x in pieces(most)]
        out[4 * rows : 4 * rows + 16, :] = jnp.concatenate(info + scale + [jnp.zeros((6, cy), F32)], axis=0).astype(BF16)
        beside = edges[1] if s == 1 else edges[0] if s == n_j - 1 else jnp.zeros((16, cy), BF16)
        out[4 * rows + 16 :, :] = beside


def sweep_kernel(n_i, n_j, cap, omega, *refs):
    blocks = n_i * n_j
    msgs, refs = refs[: blocks], refs[blocks:]
    outs, refs = refs[:n_j], refs[n_j:]
    field_a, field_b, start, inverse, gain, lag, info, weights, pick, rowmask, spread, place, group, values, pages, plain, ends, rim, frame, mid, values_b = refs
    rows, cy = start.shape[2:]
    slots = blocks * cap
    me_i, me_j = lax.axis_index("mx"), lax.axis_index("my")
    w = omega[0]

    order = [(a, s) for a in range(n_i) for s in range(n_j)]
    index = [lax.rem(me_i + a, n_i) * n_j + lax.rem(me_j + n_j - s, n_j) for a, s in order]
    for msg, b in zip(msgs, index):
        info[b] = msg[4 * rows : 4 * rows + 16, :].astype(F32)
    chunk = lax.broadcasted_iota(jnp.int32, (blocks, slots), 1) // cap
    source = lax.broadcasted_iota(jnp.int32, (blocks, slots), 0)

    def one_hot(line, depth):
        at = lax.broadcasted_iota(jnp.int32, (depth, slots), 0)
        return (jnp.broadcast_to(line.astype(jnp.int32), at.shape) == at).astype(F32)

    turned = [pltpu.roll(info[b], b * cap, 1) if b else info[b] for b in range(blocks)]
    columns = [line[3:4] for line in turned] + [jnp.zeros((LANES - blocks, slots), F32)]
    columns = jnp.transpose(jnp.concatenate(columns, axis=0))
    lane_cy = lax.broadcasted_iota(jnp.int32, (slots, cy), 1).astype(F32)
    for b, line in enumerate(turned):
        pick[b] = one_hot(line[1:2], cy).astype(BF16)
        rowmask[b] = one_hot(line[0:1], rows)
        row_out = one_hot(line[2:3], rows)
        spread[b] = row_out.astype(BF16)
        place[b] = (jnp.broadcast_to(columns[:, b : b + 1], (slots, cy)) == lane_cy).astype(F32).astype(BF16)
        group[b] = (chunk == (source + b) % blocks).astype(F32)
        high, low = split(row_out * (line[4:5] + line[5:6] + line[6:7]))
        both = jnp.dot(jnp.concatenate([high, low], axis=0), place[b], preferred_element_type=F32)
        gain[b] = both[:rows] + both[rows:]

    for msg, b in zip(msgs, index):
        rhs_re, rhs_im, k, m = [msg[n * rows : (n + 1) * rows, :] for n in range(4)]
        most = info[b][7:8] + info[b][8:9] + info[b][9:10]
        rhs_re, rhs_im = decoded(rhs_re, most), decoded(rhs_im, most)
        k, m = lowered(k, STIFF_SCALE, STIFF_POWER), lowered(m, MASS_SCALE, MASS_POWER)
        real_d = 4.4 * k + 0.3 + gain[b] - w * w * m
        imag_d = 0.2 * w * (k + m)
        scale = 1.0 / (real_d * real_d + imag_d * imag_d)
        g, l = real_d * scale, imag_d * scale
        first_re, first_im = rhs_re * g + rhs_im * l, rhs_im * g - rhs_re * l
        gain[b], lag[b], inverse[b] = k * g, k * l, 1.0 / k
        start[b, 0], start[b, 1] = first_re, first_im
        field_a[b, 0], field_a[b, 1] = first_re, first_im

    for b, line in enumerate(turned):
        at_target = lax.dot_general(
            jnp.concatenate(split(inverse[b]), axis=0),
            place[b],
            (((1,), (1,)), ((), ())),
            preferred_element_type=F32,
        )
        found = jnp.sum((at_target[:rows] + at_target[rows:]) * one_hot(line[2:3], rows), axis=0, keepdims=True)
        weights[pl.ds(b, 1), :] = (line[4:5] + line[5:6] + line[6:7]) * found

    row8 = lax.broadcasted_iota(jnp.int32, (8, LANES), 0)
    lane_r = lax.broadcasted_iota(jnp.int32, (rows, LANES), 1)
    zero = jnp.zeros((rows, LANES), F32)

    def gather(held, b, re, im, fine):
        whole = jnp.concatenate(re + im, axis=0)
        whole = jnp.concatenate(split(whole), axis=0) if fine else whole.astype(BF16)
        got = jnp.dot(whole, pick[b], preferred_element_type=F32)
        mask = rowmask[b]
        for part in range(2):
            mine = got[part * rows : (part + 1) * rows]
            if fine:
                mine += got[(part + 2) * rows : (part + 3) * rows]
            held[part, pl.ds(b, 1), :] = jnp.sum(mine * mask, axis=0, keepdims=True)

    def mortar_at(held, b, fine):
        arrived = [jnp.sum(held[part] * group[b], axis=0, keepdims=True) * weights[b : b + 1, :] for part in range(2)]
        left = []
        for r in range(0, rows, 16):
            for v in arrived:
                left += [spread[b, r : r + 16] * x for x in (split(v) if fine else [v.astype(BF16)])]
        mortar = jnp.dot(jnp.concatenate(left, axis=0), place[b], preferred_element_type=F32)
        each = 2 if fine else 1
        parts = []
        for r in range(rows // 16 * 2):
            part = mortar[r * each * 16 : r * each * 16 + 16]
            parts.append(part + mortar[r * each * 16 + 16 : r * each * 16 + 32] if fine else part)
        return parts

    def around_of(now, b, part, u):
        i, j = b // n_j, b % n_j
        lanes = slice(u * LANES, (u + 1) * LANES)
        others = slice((1 - u) * LANES, (2 - u) * LANES)
        own, other = now[b, part, :, lanes], now[b, part, :, others]
        if u == 0:
            edge = now[b - 1, part, :, others] if j > 0 else zero
            around = pltpu.roll(jnp.where(lane_r == LANES - 1, edge, other), 1, 1)
        else:
            edge = now[b + 1, part, :, others] if j < n_j - 1 else zero
            around = pltpu.roll(jnp.where(lane_r == 0, edge, other), LANES - 1, 1)
        around += other
        above = now[b - n_j, part, rows - 8 :, lanes] if i > 0 else zero[:8]
        below = now[b + n_j, part, :8, lanes] if i < n_i - 1 else zero[:8]
        top = pltpu.roll(jnp.where(row8 == 7, above, own[rows - 8 :]), 1, 0)
        bottom = pltpu.roll(jnp.where(row8 == 0, below, own[:8]), 7, 0)
        around += jnp.concatenate([top, own[:-8]], axis=0)
        return around + jnp.concatenate([own[8:], bottom], axis=0)

    def beside(now, b):
        for u in range(2):
            lanes = slice(u * LANES, (u + 1) * LANES)
            for part in range(2):
                mid[b, part, :, lanes] = around_of(now, b, part, u)

    def sweep(now, then, fine, fine_next):
        held, ahead = (values, values_b) if now is field_a else (values_b, values)

        def finish(b):
            mortar = mortar_at(held, b, fine)
            new = ([], [])
            for n in range(rows // 16):
                at = slice(n * 16, n * 16 + 16)
                re, im = mid[b, 0, at] + mortar[2 * n], mid[b, 1, at] + mortar[2 * n + 1]
                g, l = gain[b, at], lag[b, at]
                new[0].append(start[b, 0, at] + re * g + im * l)
                new[1].append(start[b, 1, at] + im * g - re * l)
                then[b, 0, at], then[b, 1, at] = new[0][-1], new[1][-1]
            if fine_next is not None:
                gather(ahead, b, *new, fine_next)

        for b in range(blocks):
            beside(now, b)
            finish(b)

    def pair(fine, step, carry):
        sweep(field_a, field_b, fine, fine)
        sweep(field_b, field_a, fine, fine)
        return carry

    fine_pairs = min(FINE, ITERS - 1) // 2
    pairs = (ITERS - 1) // 2
    for b in range(blocks):
        gather(values, b, [field_a[b, 0]], [field_a[b, 1]], False)
    lax.fori_loop(0, pairs - fine_pairs, functools.partial(pair, False), 0)
    lax.fori_loop(0, fine_pairs, functools.partial(pair, True), 0)
    last = field_a
    if (ITERS - 1) % 2:
        sweep(field_a, field_b, FINE > 0, None)
        last = field_b
    tiles = rows // 8
    back = lane_order(cy, True)
    around_mesh = jnp.zeros((rows, LANES), F32)
    for part in range(2):
        for at in (0, LANES + n_j * cy):
            plain[part, :, at : at + LANES] = around_mesh
            ends[part, :, at : at + LANES] = around_mesh[:8]
    end = jnp.where(me_i == 0, 0, rows - 1)
    rim[...] = jnp.zeros_like(rim)
    for j in range(n_j):
        for part in range(2):
            halves = []
            for u in range(2):
                page = pages.at[(j * 4 + part * 2 + u) % 8]
                lanes = slice(u * LANES, (u + 1) * LANES)
                for t in range(tiles):
                    page[pl.ds(t, 8, stride=tiles), :] = last[me_i * n_j + j, part, t * 8 : (t + 1) * 8, lanes]
                halves.append(page[...])
            plain[part, :, LANES + j * cy : LANES + (j + 1) * cy] = permuted(jnp.concatenate(halves, axis=1), back)
            rim[pl.ds(part * 4 + j, 1), :] = last[(1 - me_i) * n_j + j, part, pl.ds(end, 1), :]
    natural = permuted(rim[...], back)
    ends[:, :, LANES : LANES + n_j * cy] = jnp.zeros((2, 8, n_j * cy), F32)
    for j in range(n_j):
        for part in range(2):
            for at in (0, 7):
                ends[part, at : at + 1, LANES + j * cy : LANES + (j + 1) * cy] = natural[
                    part * 4 + j : part * 4 + j + 1
                ]
    for s, out in enumerate(outs):
        base = pl.multiple_of(LANES + (me_j ^ s) * cy, LANES)
        frame[...] = jnp.zeros_like(frame)
        block = [plain[part, :, pl.ds(base, cy)] for part in range(2)]
        for part in range(2):
            frame[pl.ds(part * 8, 1), :] = ends[part, 0:1, pl.ds(base, cy)]
            for k, (at, lane) in enumerate(((base - LANES, LANES - 1), (base + cy, 0)), 1):
                at = pl.multiple_of(at, LANES)
                beyond = [plain[part, :, pl.ds(at, LANES)], ends[part, :, pl.ds(at, LANES)]]
                beyond = beyond + [jnp.zeros((LANES - rows - 16, LANES), F32), beyond[1]]
                beyond = jnp.concatenate(beyond, axis=0)
                frame[pl.ds(part * 8 + k, 1), :LANES] = jnp.transpose(beyond)[lane : lane + 1]
        block.append(frame[...])
        if s:
            most = largest(*block)
            block = [coded(v, most) for v in block]
            row = lax.broadcasted_iota(jnp.int32, (16, cy), 0)
            for k, piece in enumerate(pieces(most)):
                block[2] = jnp.where(row == 3 + k, piece, block[2].astype(F32)).astype(BF16)
        for v, at in zip(block, (0, rows, 2 * rows)):
            out[at : at + v.shape[0], :] = v


def response_kernel(
    n_j, omega, state, density, stiffness, mass, first, last, line, west, east, *refs
):
    beyond_west, beyond_east, inner, ring, rho_ring = refs
    rows, cy = density.shape
    w = omega[0]
    top = lax.axis_index("mx") == 0
    present = (lax.axis_index("my") > 0, lax.axis_index("my") < n_j - 1)
    zero = jnp.zeros((1, cy), F32)

    def terms(u_re, u_im, nb_re, nb_im, rho, k, m):
        dstiff = 3.0 * rho * rho * k
        da = 4.4 * dstiff - w * w * m
        db = 0.2 * w * (dstiff + m)
        return da * u_re - db * u_im - dstiff * nb_re, da * u_im + db * u_re - dstiff * nb_im

    line = line[...]
    siblings = [edge_rows(m, p) for m, p in zip((beyond_west, beyond_east), present)]
    side = [edge_rows(m, p) + pltpu.roll(y, rows, 1) for m, p, y in zip((west, east), present, siblings)]
    lane = lax.broadcasted_iota(jnp.int32, (16, LANES), 1)
    start = jnp.where(top, 0, rows)
    stop = jnp.where(top, LANES - 1, rows - 1)
    corner = (lane == rows) | (lane == LANES - 1)
    around = []
    lane_cy = lax.broadcasted_iota(jnp.int32, (16, cy), 1)
    near = line[:16]
    touch = [jnp.where(top, y[:16, 0:1], y[:16, rows - 1 : rows]) for y in siblings]
    before = jnp.where(lane_cy == 0, touch[0], pltpu.roll(near, 1, 1))
    after = jnp.where(lane_cy == cy - 1, touch[1], pltpu.roll(near, cy - 1, 1))
    adjacent = []
    planes = planes_of(state, density, stiffness, mass)
    for v in planes:
        adjacent.append(jnp.where(top, v[rows - 1 :], v[:1]))
    adjacent = jnp.concatenate(adjacent + [zero] * 7, axis=0)
    around.append(line[16:] + adjacent + before + after)
    for x, own, at in ((side[0], first, 0), (side[1], last, cy - 1)):
        own = jnp.where(corner, near[:, at : at + 1], own[:16, :])
        before = jnp.where(lane == start, 0.0, pltpu.roll(x[:16], 1, 1))
        after = jnp.where(lane == stop, 0.0, pltpu.roll(x[:16], LANES - 1, 1))
        around.append(x[16:] + own + before + after)
    for row, (u, nb) in enumerate(zip([near] + [x[:16] for x in side], around)):
        t = terms(u[:3], u[3:6], nb[:3], nb[3:6], u[6:7], u[7:8], u[8:9])
        for part in range(2):
            for c in range(PARTS):
                ring[part * PARTS + c, row : row + 1, : u.shape[1]] = t[part][c : c + 1]
        rho_ring[row : row + 1, : u.shape[1]] = u[6:7]
    for n in range(2 * PARTS):
        ring[n, 1:, LANES:] = jnp.zeros((7, cy - LANES), F32)
        ring[n, 3:, :LANES] = jnp.zeros((5, LANES), F32)
    rho_ring[1:, LANES:] = jnp.zeros((7, cy - LANES), F32)
    rho_ring[3:, :LANES] = jnp.zeros((5, LANES), F32)

    fill = jnp.zeros((LANES - 16, LANES), F32)
    columns = [jnp.transpose(jnp.concatenate([x[:16], fill], axis=0)) for x in side]
    lane = lax.broadcasted_iota(jnp.int32, (rows, cy), 1)
    row = lax.broadcasted_iota(jnp.int32, (rows, cy), 0)

    def neighbours(n):
        v = planes[n]
        total = jnp.where(lane == 0, columns[0][:rows, n : n + 1], pltpu.roll(v, 1, 1))
        total += jnp.where(lane == cy - 1, columns[1][:rows, n : n + 1], pltpu.roll(v, cy - 1, 1))
        edge = line[n : n + 1]
        total += jnp.where(row == 0, jnp.where(top, zero, edge), pltpu.roll(v, 1, 0))
        return total + jnp.where(row == rows - 1, jnp.where(top, edge, zero), pltpu.roll(v, rows - 1, 0))

    for c in range(PARTS):
        t = terms(planes[c], planes[PARTS + c], neighbours(c), neighbours(PARTS + c), *planes[6:])
        inner[c], inner[PARTS + c] = t


def for_each_part(msgs, rows, use):
    for s, msg in enumerate(msgs):
        c = lax.axis_index("my") ^ s

        @pl.when(c < PARTS)
        def _(msg=msg, c=c):
            planes = msg[...]
            if msg.dtype == BF16:
                scale = planes[2 * rows :].astype(F32)
                planes = decoded(planes, scale[3:4] + scale[4:5] + scale[5:6])
            use(c, planes)


def sens_kernel(inner, ring, *refs):
    *msgs, sens = refs
    rows = inner.shape[1]
    sens[...] = jnp.zeros_like(sens)

    def use(c, planes):
        re, im = planes[:rows], planes[rows : 2 * rows]
        sens[:rows, :] -= re * inner[c] - im * inner[PARTS + c]
        re, im = planes[2 * rows : 2 * rows + 8], planes[2 * rows + 8 :]
        sens[rows:, :] -= re * ring[c] - im * ring[PARTS + c]

    for_each_part(msgs, rows, use)


def field_kernel(*refs):
    *msgs, field = refs
    rows = field.shape[1]

    def use(c, planes):
        field[c], field[PARTS + c] = planes[:rows], planes[rows : 2 * rows]

    for_each_part(msgs, rows, use)


def filter_kernel(density, ring, *refs):
    parts, out = refs[:-1], refs[-1]
    rows, cy = density.shape
    total = parts[0][...]
    for part in parts[1:]:
        total = total + part[...]
    top = lax.axis_index("mx") == 0
    rho = density[...]
    inner, ring = rho * total[:rows], ring[...] * total[rows:]
    columns = jnp.transpose(jnp.concatenate([ring, jnp.zeros((LANES - 8, cy), F32)], axis=0)[:, :LANES])

    def across(v, before, after):
        lane = lax.broadcasted_iota(jnp.int32, v.shape, 1)
        before = jnp.where(lane == 0, before, pltpu.roll(v, 1, 1))
        after = jnp.where(lane == cy - 1, after, pltpu.roll(v, cy - 1, 1))
        return v + 0.5 * (before + after)

    mid = across(inner, columns[:rows, 1:2], columns[:rows, 2:3])
    corner = jnp.where(top, columns[rows : rows + 1], columns[LANES - 1 :])
    end = across(ring, corner[:, 1:2], corner[:, 2:3])[0:1]
    row = lax.broadcasted_iota(jnp.int32, mid.shape, 0)
    empty = jnp.zeros_like(end)
    above = jnp.where(row == 0, jnp.where(top, empty, end), pltpu.roll(mid, 1, 0))
    below = jnp.where(row == rows - 1, jnp.where(top, end, empty), pltpu.roll(mid, rows - 1, 0))
    out[...] = (mid + 0.5 * (above + below)) / (4.0 * rho)


def vmem():
    return pl.BlockSpec(memory_space=pltpu.VMEM)


def smem():
    return pl.BlockSpec(memory_space=pltpu.SMEM)


def gathered(
    adjoint_rhs, state, density, stiffness, mass, omega, send_rows, recv_rows, mortar_weight
):
    rhs = adjoint_rhs.reshape(2 * PARTS, *density.shape)
    rows, cy = density.shape
    n_i, n_j = lax.axis_size("mx"), lax.axis_size("my")
    blocks = n_i * n_j
    slots = send_rows.shape[1]
    cap = slots // blocks
    planes = (state.reshape(2 * PARTS, rows, cy), density, stiffness, mass)
    edge = jax.ShapeDtypeStruct((16, LANES), F32)
    message = jax.ShapeDtypeStruct((4 * rows + 32, cy), BF16)
    *own, first, last, line = pl.pallas_call(
        functools.partial(pack_kernel, n_j),
        out_shape=[message] * n_j + [edge, edge, jax.ShapeDtypeStruct((32, cy), F32)],
        in_specs=[vmem()] * 8,
        out_specs=[vmem()] * (n_j + 3),
        scratch_shapes=[pltpu.VMEM((8, rows, LANES), F32)],
        name="pack",
    )(rhs, density, stiffness, mass, send_rows, recv_rows, mortar_weight, planes[0])
    msgs = [own[0]]
    for s in range(1, n_j):
        pairs = [(a, (a + s) % n_j) for a in range(n_j)]
        pairs = [(a, b) for a, b in pairs if b < PARTS or (s == 1 and b == PARTS)]
        msgs.append(lax.ppermute(own[s], "my", pairs))
    swap = [(0, 1), (1, 0)]
    msgs += [lax.ppermute(m, "mx", swap) for m in msgs]
    line = lax.ppermute(line, "mx", swap)
    block = (blocks, rows, cy)
    outs = pl.pallas_call(
        functools.partial(sweep_kernel, n_i, n_j, cap),
        out_shape=[jax.ShapeDtypeStruct((2 * rows + 16, cy), BF16 if s else F32) for s in range(n_j)],
        in_specs=[smem()] + [vmem()] * blocks,
        out_specs=[vmem()] * n_j,
        scratch_shapes=[
            pltpu.VMEM((blocks, 2, rows, cy), F32),
            pltpu.VMEM((blocks, 2, rows, cy), F32),
            pltpu.VMEM((blocks, 2, rows, cy), F32),
            pltpu.VMEM(block, F32),
            pltpu.VMEM(block, F32),
            pltpu.VMEM(block, F32),
            pltpu.VMEM((blocks, 16, cy), F32),
            pltpu.VMEM((blocks, slots), F32),
            pltpu.VMEM((blocks, cy, slots), BF16),
            pltpu.VMEM((blocks, rows, slots), F32),
            pltpu.VMEM((blocks, rows, slots), BF16),
            pltpu.VMEM((blocks, slots, cy), BF16),
            pltpu.VMEM((blocks, blocks, slots), F32),
            pltpu.VMEM((2, blocks, slots), F32),
            pltpu.VMEM((8, rows, LANES), F32),
            pltpu.VMEM((2, rows, n_j * cy + 2 * LANES), F32),
            pltpu.VMEM((2, 8, n_j * cy + 2 * LANES), F32),
            pltpu.VMEM((8, cy), F32),
            pltpu.VMEM((16, cy), F32),
            pltpu.VMEM((blocks, 2, rows, cy), F32),
            pltpu.VMEM((2, blocks, slots), F32),
        ],
        compiler_params=pltpu.CompilerParams(vmem_limit_bytes=SWEEP_VMEM),
        cost_estimate=pl.CostEstimate(flops=30_000_000_000, bytes_accessed=4_000_000, transcendentals=0),
        name="sweeps",
    )(omega, *msgs)
    parts = {0: outs[0]}
    for s in (2, 3, 1):
        parts[s] = lax.ppermute(outs[s], "my", [(a, a ^ s) for a in range(PARTS)])
    parts = [parts[s] for s in range(n_j)]
    inner, ring, rho_ring = pl.pallas_call(
        functools.partial(response_kernel, n_j),
        out_shape=[
            jax.ShapeDtypeStruct((2 * PARTS, rows, cy), F32),
            jax.ShapeDtypeStruct((2 * PARTS, 8, cy), F32),
            jax.ShapeDtypeStruct((8, cy), F32),
        ],
        in_specs=[smem()] + [vmem()] * 11,
        out_specs=[vmem()] * 3,
        compiler_params=pltpu.CompilerParams(vmem_limit_bytes=SMALL_VMEM),
        name="response",
    )(omega, *planes, first, last, line, msgs[1], msgs[n_j - 1], msgs[n_j + 1], msgs[2 * n_j - 1])
    sens = pl.pallas_call(
        sens_kernel,
        out_shape=jax.ShapeDtypeStruct((rows + 8, cy), F32),
        in_specs=[vmem()] * (2 + n_j),
        out_specs=vmem(),
        compiler_params=pltpu.CompilerParams(vmem_limit_bytes=SMALL_VMEM),
        name="sensitivity",
    )(inner, ring, *parts)
    size = lax.axis_size("freq")
    all_freqs = [sens]
    for s in range(1, size):
        all_freqs.append(lax.ppermute(sens, "freq", [(a, (a + s) % size) for a in range(size)]))
    field = pl.pallas_call(
        field_kernel,
        out_shape=jax.ShapeDtypeStruct((2 * PARTS, rows, cy), F32),
        in_specs=[vmem()] * n_j,
        out_specs=vmem(),
        compiler_params=pltpu.CompilerParams(vmem_limit_bytes=SMALL_VMEM),
        name="adjoint",
    )(*parts)
    filtered = pl.pallas_call(
        filter_kernel,
        out_shape=jax.ShapeDtypeStruct((rows, cy), F32),
        in_specs=[vmem()] * (2 + size),
        out_specs=vmem(),
        compiler_params=pltpu.CompilerParams(vmem_limit_bytes=SMALL_VMEM),
        name="filter",
    )(density, rho_ring, *all_freqs)
    return field.reshape(adjoint_rhs.shape), filtered


def solve_split(rhs, density, stiffness, mass, omega, send_rows, recv_rows, mortar_weight):
    rows_x, rows_y = density.shape
    cells = rows_x * rows_y
    w = omega[0]
    stiff = density**3 * stiffness
    rmass = density * mass
    sources = send_rows[0]
    targets = recv_rows[0]
    weights = mortar_weight[0]
    mdiag = jnp.zeros((cells,), jnp.float32).at[targets].add(weights).reshape(rows_x, rows_y)
    real_d = 4.4 * stiff + 0.3 + mdiag - w * w * rmass
    imag_d = 0.2 * w * (stiff + rmass)
    den = real_d * real_d + imag_d * imag_d

    def mortar(field):
        sent = field.reshape(6, cells)[:, sources]
        got = lax.all_to_all(sent, ("mx", "my"), split_axis=1, concat_axis=1, tiled=True)
        added = jnp.zeros((6, cells), jnp.float32).at[:, targets].add(got * weights)
        return added.reshape(6, rows_x, rows_y)

    def sweep(step, field):
        padded = extended(field, (("mx", 1), ("my", 2)), 1)
        beside = (
            padded[:, 2:, 1:-1] + padded[:, :-2, 1:-1] + padded[:, 1:-1, 2:] + padded[:, 1:-1, :-2]
        )
        h = rhs + stiff * beside + mortar(field)
        new_re = (h[:3] * real_d + h[3:] * imag_d) / den
        new_im = (h[3:] * real_d - h[:3] * imag_d) / den
        return jnp.concatenate([new_re, new_im], axis=0)

    return lax.fori_loop(0, ITERS, sweep, jnp.zeros((6, rows_x, rows_y), jnp.float32))


def distributed(
    adjoint_rhs, state, density, stiffness, mass, omega, send_rows, recv_rows, mortar_weight
):
    rows_x, rows_y = density.shape
    w = omega[0]
    dstiff = 3.0 * density**2 * stiffness
    rhs = adjoint_rhs.reshape(6, rows_x, rows_y)
    field = solve_split(rhs, density, stiffness, mass, omega, send_rows, recv_rows, mortar_weight)
    state_six = state.reshape(6, rows_x, rows_y)
    state_pad = extended(state_six, (("mx", 1), ("my", 2)), 1).astype(jnp.float32)
    u = state_six.astype(jnp.float32)
    nb = (
        state_pad[:, 2:, 1:-1]
        + state_pad[:, :-2, 1:-1]
        + state_pad[:, 1:-1, 2:]
        + state_pad[:, 1:-1, :-2]
    )
    da = 4.4 * dstiff - w * w * mass
    db = 0.2 * w * (dstiff + mass)
    t_re = da * u[:3] - db * u[3:] - dstiff * nb[:3]
    t_im = da * u[3:] + db * u[:3] - dstiff * nb[3:]
    sens = -jnp.sum(field[:3] * t_re - field[3:] * t_im, axis=0)
    size = lax.axis_size("freq")
    total = sens
    for s in range(1, size):
        total = total + lax.ppermute(sens, "freq", [(a, (a + s) % size) for a in range(size)])
    weighted = extended(density * total, (("mx", 0), ("my", 1)), 1)
    filt = weighted[1:-1, 1:-1]
    filt = filt + 0.5 * (
        weighted[2:, 1:-1] + weighted[:-2, 1:-1] + weighted[1:-1, 2:] + weighted[1:-1, :-2]
    )
    filt = filt + 0.25 * (
        weighted[2:, 2:] + weighted[:-2, :-2] + weighted[2:, :-2] + weighted[:-2, 2:]
    )
    return (field.reshape(1, 2, 3, rows_x, rows_y), filt / (4.0 * density))


def on_device(*args):
    rows, cy = args[2].shape
    n_i, n_j = lax.axis_size("mx"), lax.axis_size("my")
    fits = n_i == 2 and n_j == 4 and rows == 64 and cy == 2 * LANES and args[6].shape[1] == cy
    return (gathered if fits else distributed)(*args)


def solution(mesh):
    return jax.shard_map(
        on_device,
        mesh=mesh,
        in_specs=(
            P("freq", None, None, "mx", "my"),
            P("freq", None, None, "mx", "my"),
            P("mx", "my"),
            P("mx", "my"),
            P("mx", "my"),
            P("freq"),
            P(("mx", "my"), None),
            P(("mx", "my"), None),
            P(("mx", "my"), None),
        ),
        out_specs=(P("freq", None, None, "mx", "my"), P("mx", "my")),
        check_vma=False,
    )
```
